256 devices in a mesh: grp: 32 (over z_hi, y, core), sp: 8 (over x, z_lo).
Axes of the slice: x: 4, y: 4, z: 8 (z_hi: 4, z_lo: 2; z = z_hi * 2 + z_lo), core: 2. Of those that a mesh axis runs over, the one named last changes fastest.
Arguments:
- hidden: bfloat16 [32, 64, 128, 1152], P('grp', 'sp'), may hold values from -60 to 60
- frame_counts: int32 [32], P('grp'), may hold values from 1 to 48, 819 in all
- shifts: float32 [32, 4, 1152], P('grp'), may hold values from -3 to 3
- gates: float32 [32, 2, 1152], P('grp'), may hold values from 0.25 to 1.75
- w_qkv_spatial: bfloat16 [1152, 1728], P('grp'), may hold values from -1 to 1
- w_out_spatial: bfloat16 [576, 1152], P('grp'), may hold values from -0.25 to 0.25
- w_qkv_temporal: bfloat16 [1152, 1728], P('grp'), may hold values from -1 to 1
- w_out_temporal: bfloat16 [576, 1152], P('grp'), may hold values from -0.25 to 0.25
- cotangent: bfloat16 [32, 64, 128, 1152], P('grp', 'sp'), may hold values from -6 to 6
Outputs:
- block_out: bfloat16 [32, 64, 128, 1152], P('grp', 'sp')
- grad_out_temporal: float32 [1152, 576], P('grp', 'sp')
The draws below stay inside these ranges and needn't reach their ends.
Inputs may be any that keep to these rules, and one draw needn't show every extreme that they name: `frame_counts`: each clip has at least one frame; the longest clip has exactly 48 frames and all clips together have 819.
All inputs are finite; a program needn't handle non-finite values. No bound on the sum of `frame_counts` on one device may be relied on, other than what follows from the above.
Results may differ from the reference program's by a relative error of at most 0.034.
Values may be sent and summed in bfloat16 or wider, within the bound.
A program may use at most 128 MiB of HBM per device.

```python
import math
import jax
import jax.numpy as jnp
import numpy as np
from jax import lax

D = 1152
HDIM = 72
HEADS = 8
PIXELS = 128
INNER = 576
CLIPS = 32
FRAMES = 64
LONGEST = 48
ALLFRAMES = 819


def draw_hidden(key, part):
    key = jax.random.fold_in(key, 11)
    first, second, third = jax.random.split(key, 3)
    shape = (CLIPS, FRAMES, PIXELS, D)
    columns = jnp.exp(jax.random.uniform(second, (D,), jnp.float32, 0.0, math.log(10.0))) / 3.0
    rows = jnp.exp(jax.random.uniform(third, (CLIPS, FRAMES, PIXELS, 1), jnp.float32, 0.0, math.log(10.0))) / 3.0
    base = jax.random.normal(first, shape, jnp.float32)
    return jnp.clip(base * columns * rows, -60.0, 60.0).astype(jnp.bfloat16)


def drawn_projection(key):
    values = jax.random.normal(key, (D, 3 * INNER), jnp.float32) / math.sqrt(D)
    return jnp.clip(values, -1.0, 1.0)


def draw_w_qkv_spatial(key, part):
    key = jax.random.fold_in(key, 21)
    return drawn_projection(key).astype(jnp.bfloat16)


def draw_w_qkv_temporal(key, part):
    key = jax.random.fold_in(key, 37)
    return drawn_projection(key).astype(jnp.bfloat16)


def with_spikes(result, key, source, target, parts, factor):
    owner, partner = [(jnp.arange(result.shape[dim]) // (result.shape[dim] // parts)).reshape([-1 if axis == dim else 1 for axis in range(result.ndim)]) for dim in (source, target)]
    chosen = jax.random.permutation(key, parts)[partner]
    strong = (owner == chosen) | (owner == (partner + parts // 2) % parts)
    return jnp.where(strong, factor * result, result)


def level_of(rng, extent, pieces, smallest, top_value):
    def one(position, shards_of):
        heights = jax.random.uniform(jax.random.fold_in(jax.random.fold_in(rng, 6), position), (shards_of,), jnp.float32, smallest / len(pieces), top_value / len(pieces))
        return jnp.repeat(jnp.exp(heights), extent[position] // shards_of).reshape((-1,) + (1,) * (len(extent) - position - 1))

    factor_of = one(*pieces[0])
    for cut in pieces[1:]:
        factor_of = factor_of * one(*cut)
    return factor_of


def split_up(count, total, bound, lean):
    portions = [(1 << 20) // math.isqrt(standing ** lean) + 1 for standing in range(2, count + 1)]
    spare, holding = total - bound - (count - 1), [1] * (count - 1)
    while spare > 0:
        candidates = [i for i in range(count - 1) if holding[i] < bound]
        whole, budget = sum([portions[i] for i in candidates]), spare
        for i in candidates:
            extra = min(bound - holding[i], max(1, budget * portions[i] // whole), spare)
            holding[i] = holding[i] + extra
            spare = spare - extra
    return np.array([bound] + holding)


def ragged(stream_key, amount, total, reach, slope):
    if amount == 2:
        one = jax.random.randint(stream_key, (), max(1, total - reach), min(reach, total - 1) + 1)
        return jnp.stack([one, total - one])
    lengths = jnp.asarray(split_up(amount, total, reach, slope), jnp.int32)
    pairs = (amount - 1) // 2
    source_of, receiver = lengths[1:1 + 2 * pairs:2], lengths[2:2 + 2 * pairs:2]
    margin = jnp.minimum(source_of - 1, reach - receiver)
    moved = jax.random.randint(jax.random.fold_in(stream_key, 1), (pairs,), 0, 1 << 20) % (margin + 1)
    lengths = lengths.at[1:1 + 2 * pairs:2].set(source_of - moved).at[2:2 + 2 * pairs:2].set(receiver + moved)
    return lengths[jax.random.permutation(jax.random.fold_in(stream_key, 2), amount)]


def scatter_about(key, dims, deviation, bound, cuts=(), dtype=jnp.bfloat16):
    values = jax.random.normal(key, dims, jnp.float32) * deviation
    if len(cuts) > 0:
        values = level_of(key, dims, cuts, -0.22, 0.18) * values
    return jnp.clip(values, min=-bound, max=bound).astype(dtype)


def noise_with(rng, extent, width, bound, cuts, heavy, kind=jnp.bfloat16):
    entries = width * jax.random.normal(rng, extent, jnp.float32)
    if cuts:
        entries = entries * level_of(rng, extent, cuts, -0.22, 0.18)
    return jnp.clip(with_spikes(entries, jax.random.fold_in(rng, 3), *heavy), -bound, bound).astype(kind)


def setup_inputs(seed: int = 0) -> dict:
    splits = jax.random.split(jax.random.key(seed), 10)
    return {
        "hidden": draw_hidden(jax.random.fold_in(splits[9], 71), 0),
        "frame_counts": ragged(splits[1], CLIPS, ALLFRAMES, LONGEST, 1).astype(jnp.int32),
        "shifts": scatter_about(splits[2], (CLIPS, 4, D), 0.5, 3.0, ((0, 32),), jnp.float32),
        "gates": jnp.clip(0.25 + 1.5 * jax.random.uniform(splits[3], (CLIPS, 2, D), jnp.float32) ** level_of(splits[3], (CLIPS, 2, D), ((0, 32),), -0.2, 0.2), 0.25, 1.75),
        "w_qkv_spatial": draw_w_qkv_spatial(jax.random.fold_in(splits[9], 71), 0),
        "w_out_spatial": scatter_about(splits[5], (INNER, D), INNER ** -0.5, 0.25, ((0, 32),)),
        "w_qkv_temporal": draw_w_qkv_temporal(jax.random.fold_in(splits[9], 71), 0),
        "w_out_temporal": scatter_about(splits[7], (INNER, D), INNER ** -0.5, 0.25, ((0, 32),)),
        "cotangent": noise_with(splits[8], (CLIPS, FRAMES, PIXELS, D), 1.0, 6.0, ((0, 32), (1, 8)), (0, 3, 32, 2.75)),
    }


def layer_norm(values):
    values = values.astype(jnp.float32)
    centre = lax.optimization_barrier(jnp.mean(values, axis=-1, keepdims=True))
    centred = values - centre
    spread = lax.optimization_barrier(jnp.mean(centred * centred, axis=-1, keepdims=True))
    return centred * lax.rsqrt(spread + 1e-06)

def modulate(values, offsets, shift_row, scale_row):
    return (layer_norm(values) * (1.0 + offsets[scale_row]) + offsets[shift_row]).astype(jnp.bfloat16)

def softmax_rows(scores):
    scores = scores - lax.optimization_barrier(jnp.max(scores, axis=-1, keepdims=True))
    expo = jnp.exp(scores)
    return (expo / lax.optimization_barrier(jnp.sum(expo, axis=-1, keepdims=True))).astype(jnp.bfloat16)

def one_clip(hidden, frame_total, offsets, gating, cotangent, w_qkv_spatial, w_out_spatial, w_qkv_temporal, w_out_temporal):
    alive = jnp.arange(FRAMES) < frame_total
    normed = modulate(hidden, offsets, 0, 1).reshape(FRAMES * PIXELS, D)
    projected = jnp.dot(normed, w_qkv_spatial, preferred_element_type=jnp.float32).astype(jnp.bfloat16)
    projected = projected.reshape(FRAMES, PIXELS, 3, HEADS, HDIM).astype(jnp.float32)
    scores = jnp.einsum('fqhd,fkhd->fhqk', projected[:, :, 0], projected[:, :, 1]) / math.sqrt(HDIM)
    probs = softmax_rows(scores).astype(jnp.float32)
    attended = jnp.einsum('fhqk,fkhd->fqhd', probs, projected[:, :, 2]).astype(jnp.bfloat16)
    branch = jnp.dot(attended.reshape(FRAMES * PIXELS, INNER), w_out_spatial, preferred_element_type=jnp.float32)
    middle = (hidden.astype(jnp.float32) + gating[0] * branch.reshape(FRAMES, PIXELS, D)).astype(jnp.bfloat16)
    normed_t = modulate(middle, offsets, 2, 3).reshape(FRAMES * PIXELS, D)
    projected_t = jnp.dot(normed_t, w_qkv_temporal, preferred_element_type=jnp.float32).astype(jnp.bfloat16)
    projected_t = projected_t.reshape(FRAMES, PIXELS, 3, HEADS, HDIM).astype(jnp.float32)
    scores_t = jnp.einsum('qphd,kphd->phqk', projected_t[:, :, 0], projected_t[:, :, 1]) / math.sqrt(HDIM)
    scores_t = jnp.where(alive[None, None, None, :], scores_t, -1e+30)
    probs_t = softmax_rows(scores_t).astype(jnp.float32)
    attended_t = jnp.einsum('phqk,kphd->qphd', probs_t, projected_t[:, :, 2]).astype(jnp.bfloat16)
    flat_attended = attended_t.reshape(FRAMES * PIXELS, INNER)
    branch_t = jnp.dot(flat_attended, w_out_temporal, preferred_element_type=jnp.float32).reshape(FRAMES, PIXELS, D)
    kept_rows = alive[:, None, None]
    block_out = jnp.where(kept_rows, middle.astype(jnp.float32) + gating[1] * branch_t, 0.0).astype(jnp.bfloat16)
    scaled = jnp.where(kept_rows, gating[1] * cotangent.astype(jnp.float32), 0.0).astype(jnp.bfloat16)
    partial_grad = lax.dot_general(scaled.reshape(FRAMES * PIXELS, D), flat_attended, (((0,), (0,)), ((), ())), preferred_element_type=jnp.float32)
    return (block_out, partial_grad)

def reference(hidden, frame_counts, shifts, gates, w_qkv_spatial, w_out_spatial, w_qkv_temporal, w_out_temporal, cotangent):

    def per_clip(packed):
        return one_clip(packed[0], packed[1], packed[2], packed[3], packed[4], w_qkv_spatial, w_out_spatial, w_qkv_temporal, w_out_temporal)
    outputs, grads = lax.map(per_clip, (hidden, frame_counts, shifts, gates, cotangent))
    return (outputs, lax.optimization_barrier(jnp.sum(grads, axis=0)) / PIXELS)
```

```python
import functools
import math

import jax
import jax.numpy as jnp
from jax import lax
from jax.experimental import pallas as pl
from jax.experimental.pallas import tpu as pltpu
from jax.sharding import PartitionSpec as P

MESH = pl.DeviceIdType.MESH
BF = jnp.bfloat16
F32 = jnp.float32
HDIM = 72
WIDTH = 1152
INNER = 576
PAD = 640
PIX = 128
SLOTS = 8
OWN = 16
SENDERS = 6
PACK = 1792
SCALE = math.log2(math.e) / math.sqrt(HDIM)
ANY = pl.BlockSpec(memory_space=pl.ANY)
VM = pl.BlockSpec(memory_space=pltpu.VMEM)
SM = pl.BlockSpec(memory_space=pltpu.SMEM)
BIG = 56 * 1024 * 1024


def params(cid=None):
    if cid is None:
        return pltpu.CompilerParams(vmem_limit_bytes=BIG)
    return pltpu.CompilerParams(vmem_limit_bytes=BIG, collective_id=cid, has_side_effects=True)


def greet(partners):
    barrier = pltpu.get_barrier_semaphore()
    for who in partners:
        pl.semaphore_signal(barrier, inc=1, device_id=who, device_id_type=MESH)
    pl.semaphore_wait(barrier, len(partners))


def gather_kernel(own_ref, full, ssem, rsem, lsem):
    grp, sp = lax.axis_index("grp"), lax.axis_index("sp")
    h, y, c = grp // 8, (grp // 2) % 4, grp % 2
    low = sp % 2
    up, down, far = lax.rem(y + 1, 4), lax.rem(y + 3, 4), lax.rem(y + 2, 4)
    hx = lax.rem(h + 3 + 2 * low, 4)
    hp = lax.rem(h + 5 - 2 * low, 4)
    hf = lax.rem(h + 2, 4)
    sibling = (grp + 1 - 2 * c, sp)
    y_up = ((h * 4 + up) * 2 + c, sp)
    y_down = ((h * 4 + down) * 2 + c, sp)
    pair = (grp, sp + 1 - 2 * low)
    cross = (hx * 8 + y * 2 + c, sp + 1 - 2 * low)
    half = PACK
    cols_mine = pl.ds(pl.multiple_of(c * half, 128), half)
    cols_other = pl.ds(pl.multiple_of((1 - c) * half, 128), half)
    ca = pl.ds(pl.multiple_of(c * half, 128), half // 2)
    cb = pl.ds(pl.multiple_of(c * half + half // 2, 128), half // 2)

    local = pltpu.make_async_copy(own_ref.at[:, cols_mine], full.at[h, y, c, :, cols_mine], lsem)
    local.start()
    greet([sibling, y_up, y_down, pair, cross])
    count = [0]

    def send(src, dst, who):
        i = count[0]
        count[0] += 1
        copy = pltpu.make_async_remote_copy(
            src_ref=src, dst_ref=dst, send_sem=ssem.at[i], recv_sem=rsem.at[i],
            device_id=who, device_id_type=MESH)
        copy.start()
        return copy

    everything = []

    def go(where, who):
        part = full.at[where]
        copy = send(part, part, who)
        everything.append(copy)
        return copy

    al = slice(None)
    first = send(own_ref.at[:, cols_other], full.at[h, y, c, :, cols_other], sibling)
    local.wait()
    first.wait()
    by1 = [go((h, y, al, al, cb), y_up), go((h, y, al, al, cb), y_down)]
    az1 = go((h, y, al, al, ca), cross)
    for copy in by1:
        copy.wait_recv()
    by2 = [go((h, down, 0, al, cb), y_up), go((h, up, 1, al, cb), y_down)]
    az1.wait_recv()
    az2 = go((hx, y, al, al, ca), pair)
    for copy in by2:
        copy.wait_recv()
    bz1 = go((h, al, al, al, cb), cross)
    last = [go((h, al, al, al, cb), sibling)]
    az2.wait_recv()
    az3 = go((hp, y, 1 - low, al, ca), cross)
    az3.wait_recv()
    az4 = go((hf, y, low, al, ca), pair)
    az4.wait_recv()
    ay1 = [go((al, y, al, al, ca), y_up), go((al, y, al, al, ca), y_down)]
    last.append(go((al, y, al, al, ca), sibling))
    bz1.wait_recv()
    bz2 = go((hx, al, al, al, cb), pair)
    last.append(go((hx, al, al, al, cb), sibling))
    for copy in ay1:
        copy.wait_recv()
    ay2 = [go((al, down, 0, al, ca), y_up), go((al, up, 1, al, ca), y_down)]
    last.append(go((al, down, al, al, ca), sibling))
    last.append(go((al, up, al, al, ca), sibling))
    bz2.wait_recv()
    bz3 = go((hp, al, 1 - low, al, cb), cross)
    last.append(go((hp, al, al, al, cb), sibling))
    bz3.wait_recv()
    bz4 = go((hf, al, low, al, cb), pair)
    for copy in ay2:
        copy.wait_recv()
    last.append(go((al, far, al, al, ca), sibling))
    bz4.wait_recv()
    last.append(go((hf, al, al, al, cb), sibling))
    for copy in last:
        copy.wait_recv()
    for copy in everything:
        copy.wait_send()


GATHER_COPIES = 25


def gather(own):
    rows, columns = own.shape
    return pl.pallas_call(
        gather_kernel,
        out_shape=jax.ShapeDtypeStruct((4, 4, 2, rows, columns), BF),
        in_specs=[ANY],
        out_specs=ANY,
        scratch_shapes=[
            pltpu.SemaphoreType.DMA((GATHER_COPIES,)),
            pltpu.SemaphoreType.DMA((GATHER_COPIES,)),
            pltpu.SemaphoreType.DMA,
        ],
        compiler_params=params(1),
        name="gather",
    )(own)


def pack(qkv, out):
    part = jnp.concatenate([qkv, out.reshape(12, 1728)], axis=0)
    return jnp.pad(part, ((0, 0), (0, PACK - 1728)))


def unpack(part):
    part = part.reshape(32, 48, -1)[:, :, :1728]
    qkv = part[:, :36].reshape(WIDTH, 3, INNER)
    qkv = jnp.pad(qkv, ((0, 0), (0, 0), (0, PAD - INNER))).reshape(WIDTH, 3 * PAD)
    out = jnp.pad(part[:, 36:].reshape(INNER, WIDTH), ((0, PAD - INNER), (0, 0)))
    return qkv, out


def modulated(x, offsets, shift_row, scale_row):
    mean = jnp.sum(x, axis=-1, keepdims=True) * (1.0 / WIDTH)
    x = x - mean
    spread = jnp.sum(x * x, axis=-1, keepdims=True) * (1.0 / WIDTH)
    x = x * lax.rsqrt(spread + 1e-06)
    return (x * (1.0 + offsets[scale_row]) + offsets[shift_row]).astype(BF)


def head_masks(j):
    lane = lax.broadcasted_iota(jnp.int32, (1, 256), 1)
    start = 16 * j
    one = ((lane >= start) & (lane < start + HDIM)).astype(F32).astype(BF)
    two = ((lane >= start + HDIM) & (lane < start + 2 * HDIM)).astype(F32).astype(BF)
    return one, two


def attention(load, keys, valid):
    blocks = [None] * 5
    fill = [] if keys == PIX else [jnp.zeros((PIX - keys, 256), BF)]
    for j in range(4):
        one, two = head_masks(j)
        q, k, v = (load(part * PAD + 128 * j) for part in range(3))
        kk = jnp.concatenate([k * one, *fill, k * two, *fill], axis=0)
        vv = jnp.concatenate([v * one, *fill, v * two, *fill], axis=0)
        s = lax.dot_general(q, kk, (((1,), (1,)), ((), ())), preferred_element_type=F32)
        probs = []
        for part in (s[:, :128], s[:, 128:]):
            if valid is not None:
                part = jnp.where(valid, part, -1e30)
            top = jnp.max(part, axis=-1, keepdims=True)
            e = jnp.exp2((part - top) * SCALE)
            probs.append((e * (1.0 / jnp.sum(e, axis=-1, keepdims=True))).astype(BF))
        o = jnp.dot(jnp.concatenate(probs, axis=1), vv, preferred_element_type=F32)
        for i, piece in ((j, o[:, :128]), (j + 1, o[:, 128:])):
            blocks[i] = piece if blocks[i] is None else blocks[i] + piece
    return jnp.concatenate(blocks, axis=1).astype(BF)


def spatial_kernel(x_ref, shift_ref, gate_ref, wq_ref, wo_ref, mid_ref, nt_ref, normed, qkv, att):
    offsets = [shift_ref[i : i + 1, :] for i in range(4)]
    gate = gate_ref[0:1, :]

    @pl.when(lax.axis_index("sp") < SENDERS)
    def _():
        @pl.loop(0, SLOTS)
        def _(f):
            normed[f] = modulated(x_ref[f].astype(F32), offsets, 0, 1)

        @pl.loop(0, 5)
        def _(n):
            cols = pl.ds(pl.multiple_of(n * 384, 128), 384)
            got = jnp.dot(normed[...].reshape(SLOTS * PIX, WIDTH), wq_ref[:, cols], preferred_element_type=F32)
            qkv[:, :, cols] = got.astype(BF).reshape(SLOTS, PIX, 384)

        @pl.loop(0, SLOTS)
        def _(f):
            att[f] = attention(lambda first: qkv[f, :, first : first + 256], PIX, None)

        @pl.loop(0, SLOTS)
        def _(f):
            branch = jnp.dot(att[f], wo_ref[...], preferred_element_type=F32)
            middle = (x_ref[f].astype(F32) + gate * branch).astype(BF)
            mid_ref[f] = middle
            nt_ref[f] = modulated(middle.astype(F32), offsets, 2, 3)


def spatial(hidden, shifts, gates, wq, wo):
    shape = jax.ShapeDtypeStruct((SLOTS, PIX, WIDTH), BF)
    return pl.pallas_call(
        spatial_kernel,
        out_shape=(shape, shape),
        in_specs=[VM] * 5,
        out_specs=(VM, VM),
        scratch_shapes=[
            pltpu.VMEM((SLOTS, PIX, WIDTH), BF),
            pltpu.VMEM((SLOTS, PIX, 3 * PAD), BF),
            pltpu.VMEM((SLOTS, PIX, PAD), BF),
        ],
        compiler_params=params(),
        name="spatial",
    )(hidden, shifts, gates, wq, wo)


def iota(shape, dim):
    return lax.broadcasted_iota(jnp.int32, shape, dim)


def shuffle(back):
    there, here = iota((128, 128), 1 if back else 0), iota((128, 128), 0 if back else 1)
    return (here == (there % 8) * OWN + there // 8).astype(F32).astype(BF)


def temporal_kernel(total_ref, x_ref, wq_ref, out_ref, xp, qkv, ap):
    rows = SENDERS * 16
    there = shuffle(False)
    back = shuffle(True)
    total = total_ref[0]

    @pl.loop(0, SENDERS)
    def _(s):
        got = jnp.dot(there, x_ref[s].reshape(128, WIDTH), preferred_element_type=F32).astype(BF)
        xp[:, s] = got.reshape(8, 16, WIDTH)

    @pl.loop(0, 5)
    def _(n):
        cols = pl.ds(pl.multiple_of(n * 384, 128), 384)
        got = jnp.dot(xp[...].reshape(8 * rows, WIDTH), wq_ref[:, cols], preferred_element_type=F32)
        qkv[:, :, cols] = got.astype(BF).reshape(8, rows, 384)

    key, row = iota((rows, PIX), 1), iota((rows, PIX), 0)
    frame = (key // 16) * 8 + key % 8
    valid = (key < rows) & (frame < total) & ((key // 8) % 2 == (row // 8) % 2)

    @pl.loop(0, 8)
    def _(g):
        got = attention(lambda first: qkv[g, :, first : first + 256], rows, valid)
        ap[:, g] = got.reshape(SENDERS, 16, PAD)

    @pl.loop(0, SENDERS)
    def _(s):
        got = jnp.dot(back, ap[s].reshape(128, PAD), preferred_element_type=F32).astype(BF)
        out_ref[s] = got.reshape(SLOTS, OWN, PAD)


def temporal(total, tokens, wq):
    return pl.pallas_call(
        temporal_kernel,
        out_shape=jax.ShapeDtypeStruct((SENDERS, SLOTS, OWN, PAD), BF),
        in_specs=[SM, VM, VM],
        out_specs=VM,
        scratch_shapes=[
            pltpu.VMEM((8, SENDERS, 16, WIDTH), BF),
            pltpu.VMEM((8, SENDERS * 16, 3 * PAD), BF),
            pltpu.VMEM((SENDERS, 8, 16, PAD), BF),
        ],
        compiler_params=params(),
        name="temporal",
    )(total, tokens, wq)


def finish_kernel(total_ref, att_ref, mid_ref, cot_ref, gate_ref, wo_ref, out_ref, grad_ref, scaled):
    sp = lax.axis_index("sp")
    gate = gate_ref[1:2, :]
    total = total_ref[0]

    @pl.when(sp < SENDERS)
    def _():
        @pl.loop(0, SLOTS)
        def _(f):
            kept = sp * SLOTS + f < total
            branch = jnp.dot(att_ref[f], wo_ref[...], preferred_element_type=F32)
            out = mid_ref[f].astype(F32) + gate * branch
            out_ref[f] = jnp.where(kept, out, 0.0).astype(BF)
            scaled[f] = jnp.where(kept, gate * cot_ref[f].astype(F32), 0.0).astype(BF)

        @pl.loop(0, 3)
        def _(n):
            cols = pl.ds(pl.multiple_of(n * 384, 128), 384)
            got = lax.dot_general(
                att_ref[...].reshape(SLOTS * PIX, PAD), scaled[:, :, cols].reshape(SLOTS * PIX, 384),
                (((0,), (0,)), ((), ())), preferred_element_type=F32) * (1.0 / PIX)
            for t in range(8):
                rows = jnp.concatenate([got[72 * t : 72 * t + 72], jnp.zeros((8, 384), F32)], axis=0)
                grad_ref[t, :, cols] = rows.astype(BF)

    @pl.when(sp >= SENDERS)
    def _():
        out_ref[...] = jnp.zeros_like(out_ref)
        grad_ref[...] = jnp.zeros_like(grad_ref)


def finish(total, att, middle, cotangent, gates, wo):
    return pl.pallas_call(
        finish_kernel,
        out_shape=(
            jax.ShapeDtypeStruct((SLOTS, PIX, WIDTH), BF),
            jax.ShapeDtypeStruct((8, 80, WIDTH), BF),
        ),
        in_specs=[SM] + [VM] * 5,
        out_specs=(VM, VM),
        scratch_shapes=[pltpu.VMEM((SLOTS, PIX, WIDTH), BF)],
        compiler_params=params(),
        name="finish",
    )(total, att, middle, cotangent, gates, wo)


def tokens_there_kernel(nt_ref, x_ref, ssem, rsem, lsem):
    grp, sp = lax.axis_index("grp"), lax.axis_index("sp")
    peers = [(grp, lax.rem(sp + d, 8)) for d in range(1, 8)]
    greet(peers)

    def copy_to(d):
        to = lax.rem(sp + d, 8)
        src = nt_ref.at[:, pl.ds(pl.multiple_of(to * OWN, OWN), OWN), :]
        return pltpu.make_async_remote_copy(
            src_ref=src, dst_ref=x_ref.at[lax.rem(sp, SENDERS)], send_sem=ssem.at[d], recv_sem=rsem.at[d],
            device_id=(grp, to), device_id_type=MESH)

    @pl.when(sp < SENDERS)
    def _():
        for d in (4, 3, 5, 2, 6, 1, 7):
            copy_to(d).start()
        mine = pltpu.make_async_copy(
            nt_ref.at[:, pl.ds(pl.multiple_of(sp * OWN, OWN), OWN), :], x_ref.at[lax.rem(sp, SENDERS)], lsem)
        mine.start()
        mine.wait()
        for d in range(1, 8):
            copy_to(d).wait_send()

    for d in range(1, 8):
        @pl.when(lax.rem(sp + 8 - d, 8) < SENDERS)
        def _(d=d):
            copy_to(d).wait_recv()


def tokens_back_kernel(a_ref, att_ref, ssem, rsem, lsem):
    grp, sp = lax.axis_index("grp"), lax.axis_index("sp")
    peers = [(grp, lax.rem(sp + d, 8)) for d in range(1, 8)]
    greet(peers)
    mine = att_ref.at[:, pl.ds(pl.multiple_of(sp * OWN, OWN), OWN), :]

    def copy_to(d):
        to = lax.rem(sp + d, 8)
        return pltpu.make_async_remote_copy(
            src_ref=a_ref.at[lax.rem(to, SENDERS)], dst_ref=mine, send_sem=ssem.at[d], recv_sem=rsem.at[d],
            device_id=(grp, to), device_id_type=MESH)

    for d in (4, 3, 5, 2, 6, 1, 7):
        @pl.when(lax.rem(sp + d, 8) < SENDERS)
        def _(d=d):
            copy_to(d).start()

    @pl.when(sp < SENDERS)
    def _():
        own = pltpu.make_async_copy(a_ref.at[lax.rem(sp, SENDERS)], mine, lsem)
        own.start()
        own.wait()
        for d in range(1, 8):
            copy_to(d).wait_recv()

    for d in range(1, 8):
        @pl.when(lax.rem(sp + d, 8) < SENDERS)
        def _(d=d):
            copy_to(d).wait_send()


def exchange(kernel, cid, name, shape, array):
    return pl.pallas_call(
        kernel,
        out_shape=jax.ShapeDtypeStruct(shape, BF),
        in_specs=[ANY],
        out_specs=ANY,
        scratch_shapes=[
            pltpu.SemaphoreType.DMA((8,)),
            pltpu.SemaphoreType.DMA((8,)),
            pltpu.SemaphoreType.DMA,
        ],
        compiler_params=params(cid),
        name=name,
    )(array)


def reduce_kernel(g_ref, out_ref, r0, red, r1, flipped, buf, r2, s0, t0, s1, t1, s2, t2):
    grp, sp = lax.axis_index("grp"), lax.axis_index("sp")
    c, low, x = grp % 2, sp % 2, sp // 2
    chip = grp // 2
    sibling = (grp + 1 - 2 * c, sp)
    greet([(lax.rem(grp + d, 32), sp) for d in range(1, 32)] + [(grp, lax.rem(sp + d, 8)) for d in range(1, 8)])

    swap = pltpu.make_async_remote_copy(
        src_ref=g_ref.at[:, 1 - c], dst_ref=r0, send_sem=s0, recv_sem=t0, device_id=sibling, device_id_type=MESH)
    swap.start()
    swap.wait()

    slot = lax.rem(sp, SENDERS)

    def step1(to_x):
        return pltpu.make_async_remote_copy(
            src_ref=red.at[to_x], dst_ref=r1.at[slot], send_sem=s1.at[to_x], recv_sem=t1.at[slot],
            device_id=(grp, 2 * to_x + c), device_id_type=MESH)

    @pl.when(sp < SENDERS)
    def _():
        for i in range(4):
            red[i] = (g_ref[i, c].astype(F32) + r0[i].astype(F32)).astype(BF)
        for i in range(4):
            @pl.when(2 * i + c != sp)
            def _(i=i):
                step1(i).start()

            @pl.when(2 * i + c == sp)
            def _(i=i):
                r1[slot] = red[i]

        for i in range(4):
            @pl.when(2 * i + c != sp)
            def _(i=i):
                step1(i).wait_send()

    def step2(d):
        to = lax.rem(grp + d, 32)
        return pltpu.make_async_remote_copy(
            src_ref=buf.at[to], dst_ref=r2.at[chip], send_sem=s2.at[d], recv_sem=t2.at[d],
            device_id=(to, sp), device_id_type=MESH)

    @pl.when(low == c)
    def _():
        for s in range(SENDERS):
            @pl.when(sp != s)
            def _(s=s):
                pltpu.make_async_remote_copy(
                    src_ref=red.at[0], dst_ref=r1.at[s], send_sem=s1.at[0], recv_sem=t1.at[s],
                    device_id=sibling, device_id_type=MESH).wait_recv()

        total = r1[0].astype(F32)
        for s in range(1, SENDERS):
            total = total + r1[s].astype(F32)
        total = jnp.concatenate([total, jnp.zeros((48, WIDTH), F32)], axis=0)
        for n in range(9):
            flipped[128 * n : 128 * n + 128] = total[:, 128 * n : 128 * n + 128].T
        for g in range(32):
            rows = jnp.concatenate([flipped[36 * g : 36 * g + 36], jnp.zeros((12, 128), F32)], axis=0)
            buf[g] = rows.astype(BF)

        @pl.loop(1, 32)
        def _(d):
            step2(d).start()

        r2[chip] = buf[grp]

        @pl.loop(1, 32)
        def _(d):
            step2(d).wait_send()

    @pl.loop(1, 32)
    def _(d):
        @pl.when(lax.rem(grp + 32 - d, 2) == low)
        def _():
            step2(d).wait_recv()

    total = r2[0].astype(F32)
    for i in range(1, 16):
        total = total + r2[i].astype(F32)
    out_ref[...] = total


def reduce_gradient(parts):
    return pl.pallas_call(
        reduce_kernel,
        out_shape=jax.ShapeDtypeStruct((48, 128), F32),
        in_specs=[VM],
        out_specs=VM,
        scratch_shapes=[
            pltpu.VMEM((4, 80, WIDTH), BF),
            pltpu.VMEM((4, 80, WIDTH), BF),
            pltpu.VMEM((SENDERS, 80, WIDTH), BF),
            pltpu.VMEM((WIDTH, 128), F32),
            pltpu.VMEM((32, 48, 128), BF),
            pltpu.VMEM((16, 48, 128), BF),
            pltpu.SemaphoreType.DMA,
            pltpu.SemaphoreType.DMA,
            pltpu.SemaphoreType.DMA((4,)),
            pltpu.SemaphoreType.DMA((SENDERS,)),
            pltpu.SemaphoreType.DMA((32,)),
            pltpu.SemaphoreType.DMA((32,)),
        ],
        compiler_params=params(4),
        name="reduce_gradient",
    )(parts)


def on_device(
    hidden,
    frame_counts,
    shifts,
    gates,
    w_qkv_spatial,
    w_out_spatial,
    w_qkv_temporal,
    w_out_temporal,
    cotangent,
):
    own = jnp.concatenate(
        [pack(w_qkv_spatial, w_out_spatial), pack(w_qkv_temporal, w_out_temporal)], axis=1
    )
    full = gather(own)
    wq_s, wo_s = unpack(full[..., :PACK])
    wq_t, wo_t = unpack(full[..., PACK:])
    middle, normed_t = spatial(hidden[0], shifts[0], gates[0], wq_s, wo_s)
    tokens = exchange(tokens_there_kernel, 2, "tokens_there", (SENDERS, SLOTS, OWN, WIDTH), normed_t)
    mixed = temporal(frame_counts, tokens, wq_t)
    att = exchange(tokens_back_kernel, 3, "tokens_back", (SLOTS, PIX, PAD), mixed)
    block_out, parts = finish(frame_counts, att, middle, cotangent[0], gates[0], wo_t)
    grad = reduce_gradient(parts.reshape(4, 2, 80, WIDTH))
    return block_out[None], grad[:36, :HDIM]


def solution(mesh):
    return jax.shard_map(
        on_device,
        mesh=mesh,
        in_specs=(
            P("grp", "sp", None, None),
            P("grp"),
            P("grp", None, None),
            P("grp", None, None),
            P("grp", None),
            P("grp", None),
            P("grp", None),
            P("grp", None),
            P("grp", "sp", None, None),
        ),
        out_specs=(P("grp", "sp", None, None), P("grp", "sp")),
        check_vma=False,
    )
```

```python
import math

import jax
import jax.numpy as jnp
from jax import lax
from jax.experimental import pallas as pl
from jax.experimental.pallas import tpu as pltpu
from jax.sharding import PartitionSpec as P

MESH = pl.DeviceIdType.MESH
BF = jnp.bfloat16
F32 = jnp.float32
HDIM = 72
WIDTH = 1152
INNER = 576
PAD = 640
PIX = 128
SLOTS = 8
OWN = 16
SENDERS = 6
PACK = 1792
SCALE = math.log2(math.e) / math.sqrt(HDIM)
BATCH = 2
GROUPS = 8
ANY = pl.BlockSpec(memory_space=pl.ANY)
VM = pl.BlockSpec(memory_space=pltpu.VMEM)
SM = pl.BlockSpec(memory_space=pltpu.SMEM)
BIG = 56 * 1024 * 1024


def greet(partners):
    barrier = pltpu.get_barrier_semaphore()
    for who in partners:
        pl.semaphore_signal(barrier, inc=1, device_id=who, device_id_type=MESH)
    pl.semaphore_wait(barrier, len(partners))


def pack(qkv_ref, out_ref):
    qkv, out = qkv_ref[...].astype(F32), out_ref[...].astype(F32)
    k, v = qkv[:, INNER : 2 * INNER], qkv[:, 2 * INNER :]
    top = jnp.concatenate([qkv[:, :INNER], k[:, 512:], k[:, :512], v, jnp.zeros((36, 64), F32)], axis=1)
    blank = jnp.zeros((6, 64), F32)
    side = jnp.concatenate([
        jnp.concatenate([out[12:, :INNER], blank], axis=1),
        jnp.concatenate([blank, out[12:, INNER:]], axis=1),
    ], axis=0)
    low = jnp.concatenate([out[:12], side], axis=1)
    return jnp.concatenate([top, low], axis=0).astype(BF)


BOTH_WAYS = (
    ((), ("az1", "by1u", "by1d", "by2", "bz10", "ay1u0", "ay1d0")),
    (("az1",), ("az2", "ay1u1", "ay1d1")),
    (("by1u", "by1d"), ("bz11", "bz12")),
    (("bz10",), ("bz20",)),
    (("by2",), ("bz13",)),
    (("ay1u0", "ay1d0"), ("ay2u0", "ay2d0")),
    (("az2",), ("az3", "ay1u2", "ay1d2")),
    (("bz20",), ("bz30",)),
    (("bz11",), ("bz21",)),
    (("ay1u1", "ay1d1"), ("ay2u1", "ay2d1")),
    (("az3",), ("ay1u3", "ay1d3")),
    (("bz12",), ("bz22",)),
    (("bz30",), ("bz40",)),
    (("bz21",), ("bz31",)),
    (("ay2u0", "ay2d0"), ("as0",)),
    (("bz13",), ("bz23",)),
    (("ay1u2", "ay1d2"), ("ay2u2", "ay2d2")),
    (("bz22",), ("bz32",)),
    (("bz40",), ("bs0",)),
    (("bz31",), ("bz41",)),
    (("ay2u1", "ay2d1"), ("as1",)),
    (("ay1u3", "ay1d3"), ("ay2u3", "ay2d3")),
    (("bz23",), ("bz33",)),
    (("bz32",), ("bz42",)),
    (("bz41",), ("bs1",)),
    (("ay2u2", "ay2d2"), ("as2",)),
    (("bz33",), ("bz43",)),
    (("bz42",), ("bs2",)),
    (("ay2u3", "ay2d3"), ("as3",)),
    (("bz43",), ("bs3",)),
)
ONE_WAY = (
    ((), ("az1", "ay1u0", "ay1d0")),
    (("az1",), ("az2", "ay1u1", "ay1d1")),
    (("az2",), ("az3", "ay1u2", "ay1d2")),
    (("ay1u0", "ay1d0"), ("ay2u0", "ay2d0")),
    (("az3",), ("ay1u3", "ay1d3")),
    (("ay1u1", "ay1d1"), ("ay2u1", "ay2d1")),
    (("ay2u0", "ay2d0"), ("as0",)),
    (("ay1u2", "ay1d2"), ("ay2u2", "ay2d2")),
    (("ay2u1", "ay2d1"), ("as1",)),
    (("ay1u3", "ay1d3"), ("ay2u3", "ay2d3")),
    (("ay2u2", "ay2d2"), ("as2",)),
    (("ay2u3", "ay2d3"), ("as3",)),
)


def gather_plan(full, ssem, rsem, split, order):
    grp, sp = lax.axis_index("grp"), lax.axis_index("sp")
    h, y, c = grp // 8, (grp // 2) % 4, grp % 2
    low = sp % 2
    up, down, far = lax.rem(y + 1, 4), lax.rem(y + 3, 4), lax.rem(y + 2, 4)
    hx = lax.rem(h + 3 + 2 * low, 4)
    hp = lax.rem(h + 5 - 2 * low, 4)
    hf = lax.rem(h + 2, 4)
    sibling = (grp + 1 - 2 * c, sp)
    y_up = ((h * 4 + up) * 2 + c, sp)
    y_down = ((h * 4 + down) * 2 + c, sp)
    y_far = ((h * 4 + far) * 2 + c, sp)
    pair = (grp, sp + 1 - 2 * low)
    cross = (hx * 8 + y * 2 + c, sp + 1 - 2 * low)
    al = slice(None)
    ca, a1, a2 = pl.ds(0, split), pl.ds(0, split // 2), pl.ds(split // 2, split // 2)
    table = {}

    def add(name, where, who):
        table[name] = (len(table), where, who)

    hs, ys = (h, hx, hp, hf), (y, up, down, far)
    add("az1", (h, y, c, al, ca), cross)
    add("az2", (hx, y, c, al, ca), pair)
    add("az3", (hp, y, c, al, ca), cross)
    for k in range(4):
        add(f"ay1u{k}", (hs[k], y, c, al, ca), y_up)
        add(f"ay1d{k}", (hs[k], y, c, al, ca), y_down)
        add(f"ay2u{k}", (hs[k], down, c, al, a1), y_up)
        add(f"ay2d{k}", (hs[k], up, c, al, a2), y_down)
        add(f"as{k}", (hs[k], al, c, al, ca), sibling)
    if split < PACK:
        rest = PACK - split
        cb = pl.ds(split, rest)

        def part(which):
            return pl.ds(pl.multiple_of(split + which * (rest // 2), 128), rest // 2)

        add("by1u", (h, y, c, al, cb), y_up)
        add("by1d", (h, y, c, al, cb), y_down)
        add("by2", (h, y, c, al, cb), y_far)
        for k in range(4):
            add(f"bz1{k}", (h, ys[k], c, al, cb), cross)
            add(f"bz2{k}", (hx, ys[k], c, al, cb), pair)
            add(f"bz3{k}", (hp, ys[k], c, al, part(1 - low)), cross)
            add(f"bz4{k}", (hf, ys[k], c, al, part(low)), pair)
            add(f"bs{k}", (al, ys[k], c, al, cb), sibling)

    def copy(name):
        i, where, who = table[name]
        return pltpu.make_async_remote_copy(
            src_ref=full.at[where], dst_ref=full.at[where], send_sem=ssem.at[i], recv_sem=rsem.at[i],
            device_id=who, device_id_type=MESH)

    def step(waits, starts):
        def run():
            for name in waits:
                copy(name).wait_recv()
            for name in starts:
                copy(name).start()
        return run

    def settle():
        for name in table:
            if name[1] == "s":
                copy(name).wait_recv()

    def drain():
        for name in table:
            copy(name).wait_send()

    partners = [sibling, y_up, y_down, y_far, pair, cross]
    return [step(*pair_of) for pair_of in order], settle, drain, (h, y, c), partners


COPIES = 46
SPLIT = 768


def iota(shape, dim):
    return lax.broadcasted_iota(jnp.int32, shape, dim)


def picks(condition):
    return condition.astype(F32).astype(BF)


def unpack(full, wq, wo):
    col, row = iota((144, 192), 1), iota((144, 192), 0)
    of, at = col // 48, col % 48
    top = picks((at < 36) & (36 * of + at == row))
    col, row = iota((72, 192), 1), iota((72, 192), 0)
    of, at = col // 48, col % 48 - 36
    main = picks((at >= 0) & (18 * of + at == row))
    left = picks((at >= 0) & (at < 6) & (18 * of + 12 + at == row))
    right = picks((at >= 6) & (18 * of + 6 + at == row))
    keep = iota((144, 128), 1) < 64

    @pl.loop(0, 4)
    def _(h):
        outs = []
        for i in range(2):
            block = full[h, 2 * i : 2 * i + 2].reshape(192, PACK)
            got = jnp.dot(top, block, preferred_element_type=F32)
            rows = pl.ds(pl.multiple_of((2 * h + i) * 144, 16), 144)
            mixed = got[:, 512:640]
            turned = jnp.concatenate([mixed[:, 64:], mixed[:, :64]], axis=1)
            wq[rows, 0:512] = got[:, 0:512].astype(BF)
            wq[rows, 512:640] = jnp.where(keep, mixed, 0.0).astype(BF)
            wq[rows, 640:1152] = got[:, 640:1152].astype(BF)
            wq[rows, 1152:1280] = jnp.where(keep, turned, 0.0).astype(BF)
            wq[rows, 1280:1920] = got[:, 1152:1792].astype(BF)
            whole = jnp.dot(main, block[:, :WIDTH], preferred_element_type=F32)
            side = block[:, WIDTH:]
            one = jnp.dot(left, side, preferred_element_type=F32)
            two = jnp.dot(right, side, preferred_element_type=F32)
            blank = jnp.zeros((72, 512), F32)
            outs.append(whole + jnp.concatenate([one, blank], axis=1) + jnp.concatenate([blank, two], axis=1))
        wo[pl.ds(pl.multiple_of(144 * h, 16), 144), :] = jnp.concatenate(outs, axis=0).astype(BF)

    wo[INNER:, :] = jnp.zeros((PAD - INNER, WIDTH), BF)


def modulated(x, offsets, shift_row, scale_row):
    mean = jnp.sum(x, axis=-1, keepdims=True) * (1.0 / WIDTH)
    x = x - mean
    spread = jnp.sum(x * x, axis=-1, keepdims=True) * (1.0 / WIDTH)
    x = x * lax.rsqrt(spread + 1e-06)
    return (x * (1.0 + offsets[scale_row]) + offsets[shift_row]).astype(BF)


def head_masks(j):
    lane = iota((1, 256), 1)
    start = 16 * j
    one = picks((lane >= start) & (lane < start + HDIM))
    two = picks((lane >= start + HDIM) & (lane < start + 2 * HDIM))
    return one, two


def attention(load, keys, valid):
    blocks = [None] * 5
    fill = [] if keys == PIX else [jnp.zeros((PIX - keys, 256), BF)]
    for j in range(4):
        one, two = head_masks(j)
        q, k, v = (load(part * PAD + 128 * j) for part in range(3))
        kk = jnp.concatenate([k * one, *fill, k * two, *fill], axis=0)
        vv = jnp.concatenate([v * one, *fill, v * two, *fill], axis=0)
        heads = jnp.concatenate(
            [jnp.broadcast_to(one, (PIX, 256)), jnp.broadcast_to(two, (PIX, 256))], axis=0)
        s = lax.dot_general(q, kk, (((1,), (1,)), ((), ())), preferred_element_type=F32)
        expo = []
        for part in (s[:, :128], s[:, 128:]):
            if valid is not None:
                part = jnp.where(valid, part, -1e30)
            top = jnp.max(part, axis=-1, keepdims=True)
            expo.append(jnp.exp2((part - top) * SCALE).astype(BF))
        expo = jnp.concatenate(expo, axis=1)
        o = jnp.dot(expo, vv, preferred_element_type=F32)
        total = jnp.dot(expo, heads, preferred_element_type=F32)
        o = o * (1.0 / jnp.where(total == 0.0, 1.0, total))
        for i, piece in ((j, o[:, :128]), (j + 1, o[:, 128:])):
            blocks[i] = piece if blocks[i] is None else blocks[i] + piece
    return jnp.concatenate(blocks, axis=1).astype(BF)


def shuffle(back):
    there, here = iota((128, 128), 1 if back else 0), iota((128, 128), 0 if back else 1)
    return picks(here == (there % 8) * OWN + there // 8)


def block_kernel(
    total_ref, shift_ref, gate_ref, hidden_ref, cot_in_ref, w1_ref, w2_ref, w3_ref, w4_ref,
    out_ref, grad_ref,
    full_s, full_t, wq, wo, hid, nrm, mid, nt, cot, qkv, att2, x_in, qkv_n, qkv_t, ap, attp, att,
    g_part, r0, red, r1, flipped, buf, r2,
    gs_s, gr_s, gs_t, gr_t, load_sem, there_s, there_r, there_l, back_s, back_r,
    s0, t0, s1, t1, s2, t2, out_sem,
):
    grp, sp = lax.axis_index("grp"), lax.axis_index("sp")
    c, low, chip = grp % 2, sp % 2, grp // 2
    sibling = (grp + 1 - 2 * c, sp)
    slot = lax.rem(sp, SENDERS)
    busy = sp < SENDERS
    offsets = [shift_ref[i : i + 1, :] for i in range(4)]
    total = total_ref[0]

    steps_s, settle_s, drain_s, here, partners = gather_plan(full_s, gs_s, gr_s, SPLIT, BOTH_WAYS)
    steps_t, settle_t, drain_t, _, _ = gather_plan(full_t, gs_t, gr_t, PACK, ONE_WAY)
    loads = [
        pltpu.make_async_copy(hidden_ref, hid, load_sem.at[0]),
        pltpu.make_async_copy(cot_in_ref, cot, load_sem.at[1]),
    ]
    for load in loads:
        load.start()
    full_s[here] = pack(w1_ref, w2_ref)
    full_t[here] = pack(w3_ref, w4_ref)
    greet_all = [(lax.rem(grp + d, 32), sp) for d in range(1, 32)]
    greet_all += [(grp, lax.rem(sp + d, 8)) for d in range(1, 8)] + [partners[-1]]
    greet(greet_all)
    steps_s[0]()
    loads[0].wait()

    @pl.loop(0, SLOTS)
    def _(f):
        @pl.when(busy)
        def _():
            nrm[f] = modulated(hid[f].astype(F32), offsets, 0, 1)

        for i in range(SLOTS):
            @pl.when(f == i)
            def _(i=i):
                for run in steps_s[1 + i : 2 + i]:
                    run()

    for run in steps_s[9:22]:
        run()
    steps_t[0]()
    for run in steps_s[22:]:
        run()
    steps_t[1]()
    settle_s()

    @pl.when(busy)
    def _():
        unpack(full_s, wq, wo)

    def there(i, d):
        to = lax.rem(sp + d, 8)
        frames = pl.ds(BATCH * i, BATCH)
        return pltpu.make_async_remote_copy(
            src_ref=nt.at[frames, pl.ds(pl.multiple_of(to * OWN, OWN), OWN), :],
            dst_ref=x_in.at[slot, frames], send_sem=there_s.at[i, d], recv_sem=there_r.at[i, d],
            device_id=(grp, to), device_id_type=MESH)

    def there_own(i):
        frames = pl.ds(BATCH * i, BATCH)
        return pltpu.make_async_copy(
            nt.at[frames, pl.ds(pl.multiple_of(sp * OWN, OWN), OWN), :], x_in.at[slot, frames], there_l.at[i])

    rest = steps_t[2:]

    @pl.loop(0, SLOTS // BATCH)
    def _(i):
        def beside(part):
            for n in range(SLOTS // BATCH):
                chosen = rest[3 * n + part : 3 * n + part + 1]
                if chosen:
                    @pl.when(i == n)
                    def _(chosen=chosen):
                        for run in chosen:
                            run()

        @pl.when(busy)
        def _():
            rows = nrm[pl.ds(BATCH * i, BATCH)].reshape(BATCH * PIX, WIDTH)
            got = jnp.dot(rows, wq[...], preferred_element_type=F32)
            qkv[...] = got.astype(BF).reshape(BATCH, PIX, 3 * PAD)

        beside(0)

        @pl.when(busy)
        def _():
            for u in range(BATCH):
                att2[u] = attention(lambda first: qkv[u, :, first : first + 256], PIX, None)

        beside(1)

        @pl.when(busy)
        def _():
            for u in range(BATCH):
                f = BATCH * i + u
                branch = jnp.dot(att2[u], wo[...], preferred_element_type=F32)
                middle = (hid[f].astype(F32) + gate_ref[0:1, :] * branch).astype(BF)
                mid[f] = middle
                nt[f] = modulated(middle.astype(F32), offsets, 2, 3)
            for d in (4, 3, 5, 2, 6, 1, 7):
                there(i, d).start()
            there_own(i).start()

        beside(2)

    settle_t()
    unpack(full_t, wq, wo)

    rows = SENDERS * 16

    @pl.loop(0, SLOTS // BATCH)
    def _(i):
        @pl.when((i == SLOTS // BATCH - 1) & busy)
        def _():
            loads[1].wait()

            @pl.loop(0, SLOTS)
            def _(f):
                kept = sp * SLOTS + f < total
                nrm[f] = jnp.where(kept, gate_ref[1:2, :] * cot[f].astype(F32), 0.0).astype(BF)

        for d in range(1, 8):
            @pl.when(lax.rem(sp + 8 - d, 8) < SENDERS)
            def _(d=d):
                there(i, d).wait_recv()

        @pl.when(busy)
        def _():
            there_own(i).wait()

        got = jnp.dot(
            x_in[:, pl.ds(BATCH * i, BATCH)].reshape(SENDERS * BATCH * OWN, WIDTH), wq[...],
            preferred_element_type=F32)
        lines = pl.ds(pl.multiple_of(i * BATCH * OWN, 16), BATCH * OWN)
        qkv_n[:, lines, :] = got.astype(BF).reshape(SENDERS, BATCH * OWN, 3 * PAD)

    @pl.when(sp >= SENDERS)
    def _():
        loads[1].wait()

    order = shuffle(False)

    @pl.loop(0, SENDERS)
    def _(s):
        got = jnp.dot(order, qkv_n[s], preferred_element_type=F32).astype(BF)
        qkv_t[:, s] = got.reshape(GROUPS, 16, 3 * PAD)

    key, row = iota((rows, PIX), 1), iota((rows, PIX), 0)
    frame = (key // 16) * 8 + key % 8
    valid = (key < rows) & (frame < total) & ((key // 8) % 2 == (row // 8) % 2)

    def back(i, d):
        to = lax.rem(sp + d, 8)
        pairs = pl.ds(2 * i, 2)
        return pltpu.make_async_remote_copy(
            src_ref=ap.at[lax.rem(to, SENDERS), pairs], dst_ref=attp.at[sp, pairs],
            send_sem=back_s.at[i, d], recv_sem=back_r.at[i, d],
            device_id=(grp, to), device_id_type=MESH)

    @pl.loop(0, GROUPS // 2)
    def _(i):
        for u in range(2):
            mixed = attention(
                lambda first: qkv_t[2 * i + u, :, :, first : first + 256].reshape(rows, 256), rows, valid)
            ap[:, 2 * i + u] = mixed.reshape(SENDERS, 16, PAD)
        for d in (4, 3, 5, 2, 6, 1, 7):
            @pl.when(lax.rem(sp + d, 8) < SENDERS)
            def _(d=d):
                back(i, d).start()

        @pl.when(busy)
        def _():
            attp[sp, pl.ds(2 * i, 2)] = ap[slot, pl.ds(2 * i, 2)]

    swap = pltpu.make_async_remote_copy(
        src_ref=g_part.at[:, 1 - c], dst_ref=r0, send_sem=s0, recv_sem=t0, device_id=sibling, device_id_type=MESH)

    def step1(to_x):
        return pltpu.make_async_remote_copy(
            src_ref=red.at[to_x], dst_ref=r1.at[slot], send_sem=s1.at[to_x], recv_sem=t1.at[slot],
            device_id=(grp, 2 * to_x + c), device_id_type=MESH)

    def step2(d):
        to = lax.rem(grp + d, 32)
        return pltpu.make_async_remote_copy(
            src_ref=buf.at[to], dst_ref=r2.at[chip], send_sem=s2.at[d], recv_sem=t2.at[d],
            device_id=(to, sp), device_id_type=MESH)

    def output(f):
        kept = sp * SLOTS + f < total
        branch = jnp.dot(att[f], wo[...], preferred_element_type=F32)
        out = mid[f].astype(F32) + gate_ref[1:2, :] * branch
        hid[f] = jnp.where(kept, out, 0.0).astype(BF)

    @pl.when(busy)
    def _():
        for i in range(GROUPS // 2):
            for d in range(1, 8):
                back(i, d).wait_recv()
        unorder = shuffle(True)

        @pl.loop(0, 8)
        def _(t):
            got = jnp.dot(unorder, attp[t].reshape(128, PAD), preferred_element_type=F32).astype(BF)
            att[:, pl.ds(pl.multiple_of(t * OWN, OWN), OWN), :] = got.reshape(SLOTS, OWN, PAD)

        @pl.loop(0, 3)
        def _(n):
            cols = pl.ds(pl.multiple_of(n * 384, 128), 384)
            got = lax.dot_general(
                att[...].reshape(SLOTS * PIX, PAD), nrm[:, :, cols].reshape(SLOTS * PIX, 384),
                (((0,), (0,)), ((), ())), preferred_element_type=F32) * (1.0 / PIX)
            for t in range(8):
                part = jnp.concatenate([got[72 * t : 72 * t + 72], jnp.zeros((8, 384), F32)], axis=0)
                g_part[t // 2, t % 2, :, cols] = part.astype(BF)

        swap.start()

        @pl.loop(0, SLOTS // 2)
        def _(f):
            output(f)

        swap.wait()
        for i in range(4):
            red[i] = (g_part[i, c].astype(F32) + r0[i].astype(F32)).astype(BF)
        for i in range(4):
            @pl.when(2 * i + c != sp)
            def _(i=i):
                step1(i).start()

            @pl.when(2 * i + c == sp)
            def _(i=i):
                r1[slot] = red[i]

        @pl.loop(SLOTS // 2, SLOTS)
        def _(f):
            output(f)

    @pl.when(sp >= SENDERS)
    def _():
        hid[...] = jnp.zeros_like(hid)

    result = pltpu.make_async_copy(hid, out_ref, out_sem)
    result.start()

    @pl.when(low == c)
    def _():
        for s in range(SENDERS):
            @pl.when(sp != s)
            def _(s=s):
                pltpu.make_async_remote_copy(
                    src_ref=red.at[0], dst_ref=r1.at[s], send_sem=s1.at[0], recv_sem=t1.at[s],
                    device_id=sibling, device_id_type=MESH).wait_recv()

        whole = r1[0].astype(F32)
        for s in range(1, SENDERS):
            whole = whole + r1[s].astype(F32)
        whole = jnp.concatenate([whole, jnp.zeros((48, WIDTH), F32)], axis=0)
        for n in range(9):
            flipped[128 * n : 128 * n + 128] = whole[:, 128 * n : 128 * n + 128].T
        for g in range(32):
            part = jnp.concatenate([flipped[36 * g : 36 * g + 36], jnp.zeros((12, 128), F32)], axis=0)
            buf[g] = part.astype(BF)

        @pl.loop(1, 32)
        def _(d):
            step2(d).start()

        r2[chip] = buf[grp]

        @pl.loop(1, 32)
        def _(d):
            step2(d).wait_send()

    @pl.loop(1, 32)
    def _(d):
        @pl.when(lax.rem(grp + 32 - d, 2) == low)
        def _():
            step2(d).wait_recv()

    whole = r2[0].astype(F32)
    for i in range(1, 16):
        whole = whole + r2[i].astype(F32)
    grad_ref[...] = whole[:36, :HDIM]

    drain_s()
    drain_t()

    @pl.when(busy)
    def _():
        for i in range(4):
            @pl.when(2 * i + c != sp)
            def _(i=i):
                step1(i).wait_send()

        for i in range(SLOTS // BATCH):
            for d in range(1, 8):
                there(i, d).wait_send()

    for i in range(GROUPS // 2):
        for d in range(1, 8):
            @pl.when(lax.rem(sp + d, 8) < SENDERS)
            def _(d=d, i=i):
                back(i, d).wait_send()

    result.wait()


def on_device(
    hidden,
    frame_counts,
    shifts,
    gates,
    w_qkv_spatial,
    w_out_spatial,
    w_qkv_temporal,
    w_out_temporal,
    cotangent,
):
    frames = (SLOTS, PIX, WIDTH)
    dma = pltpu.SemaphoreType.DMA
    block_out, grad = pl.pallas_call(
        block_kernel,
        out_shape=(jax.ShapeDtypeStruct(frames, BF), jax.ShapeDtypeStruct((36, HDIM), F32)),
        in_specs=[SM, VM, VM, ANY, ANY, VM, VM, VM, VM],
        out_specs=(ANY, VM),
        scratch_shapes=[
            pltpu.VMEM((4, 4, 2, 48, PACK), BF),
            pltpu.VMEM((4, 4, 2, 48, PACK), BF),
            pltpu.VMEM((WIDTH, 3 * PAD), BF),
            pltpu.VMEM((PAD, WIDTH), BF),
            *[pltpu.VMEM(frames, BF)] * 5,
            pltpu.VMEM((BATCH, PIX, 3 * PAD), BF),
            pltpu.VMEM((BATCH, PIX, PAD), BF),
            pltpu.VMEM((SENDERS, SLOTS, OWN, WIDTH), BF),
            pltpu.VMEM((SENDERS, 128, 3 * PAD), BF),
            pltpu.VMEM((GROUPS, SENDERS, 16, 3 * PAD), BF),
            pltpu.VMEM((SENDERS, GROUPS, 16, PAD), BF),
            pltpu.VMEM((8, GROUPS, 16, PAD), BF),
            pltpu.VMEM((SLOTS, PIX, PAD), BF),
            pltpu.VMEM((4, 2, 80, WIDTH), BF),
            pltpu.VMEM((4, 80, WIDTH), BF),
            pltpu.VMEM((4, 80, WIDTH), BF),
            pltpu.VMEM((SENDERS, 80, WIDTH), BF),
            pltpu.VMEM((WIDTH, 128), F32),
            pltpu.VMEM((32, 48, 128), BF),
            pltpu.VMEM((16, 48, 128), BF),
            dma((COPIES,)), dma((COPIES,)), dma((COPIES,)), dma((COPIES,)),
            dma((2,)),
            dma((4, 8)), dma((4, 8)), dma((4,)),
            dma((4, 8)), dma((4, 8)),
            dma, dma, dma((4,)), dma((SENDERS,)), dma((32,)), dma((32,)), dma,
        ],
        compiler_params=pltpu.CompilerParams(
            vmem_limit_bytes=BIG, collective_id=1, has_side_effects=True),
        name="block",
    )(
        frame_counts, shifts[0], gates[0], hidden[0], cotangent[0],
        w_qkv_spatial, w_out_spatial, w_qkv_temporal, w_out_temporal,
    )
    return block_out[None], grad


def solution(mesh):
    return jax.shard_map(
        on_device,
        mesh=mesh,
        in_specs=(
            P("grp", "sp", None, None),
            P("grp"),
            P("grp", None, None),
            P("grp", None, None),
            P("grp", None),
            P("grp", None),
            P("grp", None),
            P("grp", None),
            P("grp", "sp", None, None),
        ),
        out_specs=(P("grp", "sp", None, None), P("grp", "sp")),
        check_vma=False,
    )
```

```python
import math

import jax
import jax.numpy as jnp
from jax import lax
from jax.experimental import pallas as pl
from jax.experimental.pallas import tpu as pltpu
from jax.sharding import PartitionSpec as P

MESH = pl.DeviceIdType.MESH
BF = jnp.bfloat16
F32 = jnp.float32
HDIM = 72
WIDTH = 1152
INNER = 576
PAD = 640
PIX = 128
SLOTS = 8
OWN = 16
SENDERS = 6
PACK = 1792
SCALE = math.log2(math.e) / math.sqrt(HDIM)
BATCH = 2
GROUPS = 8
ANY = pl.BlockSpec(memory_space=pl.ANY)
VM = pl.BlockSpec(memory_space=pltpu.VMEM)
SM = pl.BlockSpec(memory_space=pltpu.SMEM)
BIG = 56 * 1024 * 1024


def greet(partners):
    barrier = pltpu.get_barrier_semaphore()
    for who in partners:
        pl.semaphore_signal(barrier, inc=1, device_id=who, device_id_type=MESH)
    pl.semaphore_wait(barrier, len(partners))


def pack(qkv_ref, out_ref):
    qkv, out = qkv_ref[...].astype(F32), out_ref[...].astype(F32)
    k, v = qkv[:, INNER : 2 * INNER], qkv[:, 2 * INNER :]
    top = jnp.concatenate([qkv[:, :INNER], k[:, 512:], k[:, :512], v, jnp.zeros((36, 64), F32)], axis=1)
    blank = jnp.zeros((6, 64), F32)
    side = jnp.concatenate([
        jnp.concatenate([out[12:, :INNER], blank], axis=1),
        jnp.concatenate([blank, out[12:, INNER:]], axis=1),
    ], axis=0)
    low = jnp.concatenate([out[:12], side], axis=1)
    return jnp.concatenate([top, low], axis=0).astype(BF)


STEPS = (
    ((), ("z1p", "z1q", "upp0", "dnp0", "upq0", "dnq0")),
    (("z1p",), ("z2p", "upp1", "dnp1")),
    (("z1q",), ("z2q", "upq1", "dnq1")),
    (("upp0", "dnp0"), ("farp0",)),
    (("upq0", "dnq0"), ("farq0",)),
    (("z2p",), ("z3p", "upp2", "dnp2")),
    (("z2q",), ("z3q", "upq2", "dnq2")),
    (("upp1", "dnp1"), ("farp1",)),
    (("upq1", "dnq1"), ("farq1",)),
    (("z3p",), ("upp3", "dnp3")),
    (("z3q",), ("upq3", "dnq3")),
    (("farp0", "farq0"), ("s0",)),
    (("upp2", "dnp2"), ("farp2",)),
    (("upq2", "dnq2"), ("farq2",)),
    (("farp1", "farq1"), ("s1",)),
    (("upp3", "dnp3"), ("farp3",)),
    (("upq3", "dnq3"), ("farq3",)),
    (("farp2", "farq2"), ("s2",)),
    (("farp3", "farq3"), ("s3",)),
)


def gather_plan(full, ssem, rsem):
    grp, sp = lax.axis_index("grp"), lax.axis_index("sp")
    h, y, c = grp // 8, (grp // 2) % 4, grp % 2
    low = sp % 2
    up, down = lax.rem(y + 1, 4), lax.rem(y + 3, 4)
    hx = lax.rem(h + 3 + 2 * low, 4)
    hp = lax.rem(h + 5 - 2 * low, 4)
    hf = lax.rem(h + 2, 4)
    sibling = (grp + 1 - 2 * c, sp)
    y_up = ((h * 4 + up) * 2 + c, sp)
    y_down = ((h * 4 + down) * 2 + c, sp)
    pair = (grp, sp + 1 - 2 * low)
    cross = (hx * 8 + y * 2 + c, sp + 1 - 2 * low)
    al = slice(None)
    hs = (h, hx, hp, hf)
    table = {}

    def add(name, where, who):
        table[name] = (len(table), where, who)

    for stream, cols in (("p", pl.ds(0, PACK // 2)), ("q", pl.ds(PACK // 2, PACK // 2))):
        add("z1" + stream, (h, y, c, al, cols), cross)
        add("z2" + stream, (hx, y, c, al, cols), pair)
        add("z3" + stream, (hp, y, c, al, cols), cross)
        for k in range(4):
            add(f"up{stream}{k}", (hs[k], y, c, al, cols), y_up)
            add(f"dn{stream}{k}", (hs[k], y, c, al, cols), y_down)
            if stream == "p":
                add(f"farp{k}", (hs[k], down, c, al, cols), y_up)
            else:
                add(f"farq{k}", (hs[k], up, c, al, cols), y_down)
    for k in range(4):
        add(f"s{k}", (hs[k], al, c), sibling)

    def copy(name):
        i, where, who = table[name]
        return pltpu.make_async_remote_copy(
            src_ref=full.at[where], dst_ref=full.at[where], send_sem=ssem.at[i], recv_sem=rsem.at[i],
            device_id=who, device_id_type=MESH)

    def step(waits, starts):
        def run():
            for name in waits:
                copy(name).wait_recv()
            for name in starts:
                copy(name).start()
        return run

    def settle(k):
        copy(f"s{k}").wait_recv()
        return hs[k]

    def drain():
        for name in table:
            copy(name).wait_send()

    return [step(*both) for both in STEPS], settle, drain, (h, y, c), cross


COPIES = 34


def iota(shape, dim):
    return lax.broadcasted_iota(jnp.int32, shape, dim)


def picks(condition):
    return condition.astype(F32).astype(BF)


def unpack(full, settle, wq, wo):
    col, row = iota((144, 192), 1), iota((144, 192), 0)
    of, at = col // 48, col % 48
    top = picks((at < 36) & (36 * of + at == row))
    col, row = iota((72, 192), 1), iota((72, 192), 0)
    of, at = col // 48, col % 48 - 36
    main = picks((at >= 0) & (18 * of + at == row) & (at < 12))
    left = picks((at >= 0) & (at < 6) & (18 * of + 12 + at == row))
    right = picks((at >= 6) & (18 * of + 6 + at == row))
    keep = iota((144, 128), 1) < 64

    wo[INNER:, :] = jnp.zeros((PAD - INNER, WIDTH), BF)
    for k in range(4):
        h = settle(k)
        outs = []
        for i in range(2):
            block = full[h, 2 * i : 2 * i + 2].reshape(192, PACK)
            got = jnp.dot(top, block, preferred_element_type=F32)
            rows = pl.ds(pl.multiple_of((2 * h + i) * 144, 16), 144)
            mixed = got[:, 512:640]
            turned = jnp.concatenate([mixed[:, 64:], mixed[:, :64]], axis=1)
            wq[rows, 0:512] = got[:, 0:512].astype(BF)
            wq[rows, 512:640] = jnp.where(keep, mixed, 0.0).astype(BF)
            wq[rows, 640:1152] = got[:, 640:1152].astype(BF)
            wq[rows, 1152:1280] = jnp.where(keep, turned, 0.0).astype(BF)
            wq[rows, 1280:1920] = got[:, 1152:1792].astype(BF)
            whole = jnp.dot(main, block[:, :WIDTH], preferred_element_type=F32)
            side = block[:, WIDTH:]
            one = jnp.dot(left, side, preferred_element_type=F32)
            two = jnp.dot(right, side, preferred_element_type=F32)
            blank = jnp.zeros((72, 512), F32)
            outs.append(whole + jnp.concatenate([one, blank], axis=1) + jnp.concatenate([blank, two], axis=1))
        wo[pl.ds(pl.multiple_of(144 * h, 16), 144), :] = jnp.concatenate(outs, axis=0).astype(BF)


def modulated(x, offsets, shift_row, scale_row):
    mean = jnp.sum(x, axis=-1, keepdims=True) * (1.0 / WIDTH)
    x = x - mean
    spread = jnp.sum(x * x, axis=-1, keepdims=True) * (1.0 / WIDTH)
    x = x * lax.rsqrt(spread + 1e-06)
    return (x * (1.0 + offsets[scale_row]) + offsets[shift_row]).astype(BF)


def head_masks(j):
    lane = iota((1, 256), 1)
    start = 16 * j
    one = picks((lane >= start) & (lane < start + HDIM))
    two = picks((lane >= start + HDIM) & (lane < start + 2 * HDIM))
    return one, two


def attention(load, keys, valid):
    blocks = [None] * 5
    fill = [] if keys == PIX else [jnp.zeros((PIX - keys, 256), BF)]
    for j in range(4):
        one, two = head_masks(j)
        q, k, v = (load(part * PAD + 128 * j) for part in range(3))
        kk = jnp.concatenate([k * one, *fill, k * two, *fill], axis=0)
        vv = jnp.concatenate([v * one, *fill, v * two, *fill], axis=0)
        heads = jnp.concatenate(
            [jnp.broadcast_to(one, (PIX, 256)), jnp.broadcast_to(two, (PIX, 256))], axis=0)
        s = lax.dot_general(q, kk, (((1,), (1,)), ((), ())), preferred_element_type=F32)
        expo = []
        for part in (s[:, :128], s[:, 128:]):
            if valid is not None:
                part = jnp.where(valid, part, -1e30)
            top = jnp.max(part, axis=-1, keepdims=True)
            expo.append(jnp.exp2((part - top) * SCALE).astype(BF))
        expo = jnp.concatenate(expo, axis=1)
        o = jnp.dot(expo, vv, preferred_element_type=F32)
        total = jnp.dot(expo, heads, preferred_element_type=F32)
        o = o * (1.0 / jnp.where(total == 0.0, 1.0, total))
        for i, piece in ((j, o[:, :128]), (j + 1, o[:, 128:])):
            blocks[i] = piece if blocks[i] is None else blocks[i] + piece
    return jnp.concatenate(blocks, axis=1).astype(BF)


def shuffle(back):
    there, here = iota((128, 128), 1 if back else 0), iota((128, 128), 0 if back else 1)
    return picks(here == (there % 8) * OWN + there // 8)


def block_kernel(
    total_ref, shift_ref, gate_ref, hidden_ref, cot_in_ref, w1_ref, w2_ref, w3_ref, w4_ref,
    out_ref, grad_ref,
    full_s, full_t, wq, wo_s, wo_t, hid, nrm, mid, cot, qkv, att_s, x_in, a_in, xp, qkv_t, ap, attp, att,
    g_part, r0, red, r1, flipped, buf, r2,
    gs_s, gr_s, gs_t, gr_t, load_sem, early_s, early_r, there_s, there_r, there_l, back_s, back_r,
    s0, t0, s1, t1, s2, t2, out_sem,
):
    grp, sp = lax.axis_index("grp"), lax.axis_index("sp")
    c, low, chip = grp % 2, sp % 2, grp // 2
    sibling = (grp + 1 - 2 * c, sp)
    slot = lax.rem(sp, SENDERS)
    busy = sp < SENDERS
    offsets = [shift_ref[i : i + 1, :] for i in range(4)]
    total = total_ref[0]
    rows = SENDERS * 16
    batches = SLOTS // BATCH

    def from_me(d):
        return lax.rem(sp + d, 8)

    def pixels(rank):
        return pl.ds(pl.multiple_of(rank * OWN, OWN), OWN)

    def if_sends(d):
        return pl.when(lax.rem(sp + 8 - d, 8) < SENDERS)

    def if_gets(d):
        return pl.when(from_me(d) < SENDERS)

    def remote(src, dst, send_sem, recv_sem, who):
        return pltpu.make_async_remote_copy(
            src_ref=src, dst_ref=dst, send_sem=send_sem, recv_sem=recv_sem,
            device_id=who, device_id_type=MESH)

    def early(d):
        to = from_me(d)
        return remote(hidden_ref.at[:, pixels(to), :], x_in.at[slot], early_s.at[d], early_r.at[d], (grp, to))

    def there(i, d):
        to, frames = from_me(d), pl.ds(BATCH * i, BATCH)
        return remote(
            att_s.at[frames, pixels(to), :], a_in.at[slot, frames], there_s.at[i, d], there_r.at[i, d], (grp, to))

    def there_own(i):
        frames = pl.ds(BATCH * i, BATCH)
        return pltpu.make_async_copy(att_s.at[frames, pixels(sp), :], a_in.at[slot, frames], there_l.at[i])

    def back(i, d):
        to, pairs = from_me(d), pl.ds(2 * i, 2)
        return remote(
            ap.at[lax.rem(to, SENDERS), pairs], attp.at[sp, pairs], back_s.at[i, d], back_r.at[i, d], (grp, to))

    steps_s, settle_s, drain_s, here, cross = gather_plan(full_s, gs_s, gr_s)
    steps_t, settle_t, drain_t, _, _ = gather_plan(full_t, gs_t, gr_t)
    loads = [
        pltpu.make_async_copy(hidden_ref, hid, load_sem.at[0]),
        pltpu.make_async_copy(cot_in_ref, cot, load_sem.at[1]),
        pltpu.make_async_copy(hidden_ref.at[:, pixels(sp), :], x_in.at[slot], load_sem.at[2]),
    ]
    loads[0].start()
    loads[1].start()

    @pl.when(busy)
    def _():
        loads[2].start()

    full_s[here] = pack(w1_ref, w2_ref)
    full_t[here] = pack(w3_ref, w4_ref)
    greet_all = [(lax.rem(grp + d, 32), sp) for d in range(1, 32)]
    greet_all += [(grp, from_me(d)) for d in range(1, 8)] + [cross]
    greet(greet_all)
    steps_s[0]()

    @pl.when(busy)
    def _():
        for d in (4, 2, 6):
            early(d).start()

    loads[0].wait()
    loads[1].wait()

    @pl.loop(0, SLOTS)
    def _(f):
        @pl.when(busy)
        def _():
            nrm[f] = modulated(hid[f].astype(F32), offsets, 0, 1)

        for i in range(SLOTS):
            @pl.when(f == i)
            def _(i=i):
                steps_s[1 + i]()

        @pl.when((f == 1) & busy)
        def _():
            for d in (3, 5, 1, 7):
                early(d).start()

    for run in steps_s[9:17]:
        run()
    steps_t[0]()
    for run in steps_s[17:]:
        run()
    unpack(full_s, settle_s, wq, wo_s)

    rest = steps_t[1:]

    @pl.loop(0, batches)
    def _(i):
        @pl.when(busy)
        def _():
            tokens = nrm[pl.ds(BATCH * i, BATCH)].reshape(BATCH * PIX, WIDTH)
            got = jnp.dot(tokens, wq[...], preferred_element_type=F32)
            qkv[...] = got.astype(BF).reshape(BATCH, PIX, 3 * PAD)
            for u in range(BATCH):
                att_s[BATCH * i + u] = attention(lambda first: qkv[u, :, first : first + 256], PIX, None)
            for d in (4, 3, 5, 2, 6, 1, 7):
                there(i, d).start()
            there_own(i).start()

        for n in range(batches):
            @pl.when(i == n)
            def _(n=n):
                for run in rest[2 * n : 2 * n + 2]:
                    run()

    rest = rest[2 * batches :]

    for d in range(1, 8):
        @if_sends(d)
        def _(d=d):
            early(d).wait_recv()

    @pl.when(busy)
    def _():
        loads[2].wait()

    @pl.loop(0, batches)
    def _(i):
        for d in range(1, 8):
            @if_sends(d)
            def _(d=d):
                there(i, d).wait_recv()

        @pl.when(busy)
        def _():
            there_own(i).wait()

        frames = pl.ds(BATCH * i, BATCH)
        lines = SENDERS * BATCH * OWN
        branch = jnp.dot(a_in[:, frames].reshape(lines, PAD), wo_s[...], preferred_element_type=F32)
        middle = x_in[:, frames].reshape(lines, WIDTH).astype(F32) + gate_ref[0:1, :] * branch
        normed = modulated(middle.astype(BF).astype(F32), offsets, 2, 3)
        x_in[:, frames] = normed.reshape(SENDERS, BATCH, OWN, WIDTH)

        for n in range(batches):
            @pl.when(i == n)
            def _(n=n):
                for run in rest[n : n + 1]:
                    run()

    order = shuffle(False)

    @pl.loop(0, SENDERS)
    def _(s):
        got = jnp.dot(order, x_in[s].reshape(128, WIDTH), preferred_element_type=F32).astype(BF)
        xp[:, s] = got.reshape(GROUPS, 16, WIDTH)

    for run in rest[batches:]:
        run()
    unpack(full_t, settle_t, wq, wo_t)

    key, row = iota((rows, PIX), 1), iota((rows, PIX), 0)
    frame = (key // 16) * 8 + key % 8
    valid = (key < rows) & (frame < total) & ((key // 8) % 2 == (row // 8) % 2)

    @pl.loop(0, GROUPS // 2)
    def _(i):
        got = jnp.dot(xp[pl.ds(2 * i, 2)].reshape(2 * rows, WIDTH), wq[...], preferred_element_type=F32)
        qkv_t[...] = got.astype(BF).reshape(2, rows, 3 * PAD)
        for u in range(2):
            mixed = attention(lambda first: qkv_t[u, :, first : first + 256], rows, valid)
            ap[:, 2 * i + u] = mixed.reshape(SENDERS, 16, PAD)
        for d in (4, 3, 5, 2, 6, 1, 7):
            @if_gets(d)
            def _(d=d):
                back(i, d).start()

        @pl.when(busy)
        def _():
            attp[sp, pl.ds(2 * i, 2)] = ap[slot, pl.ds(2 * i, 2)]

    def swap(n):
        cols = pl.ds(384 * n, 384)
        return remote(g_part.at[:, 1 - c, :, cols], r0.at[:, :, cols], s0.at[n], t0.at[n], sibling)

    def step1(n, to_x):
        cols = pl.ds(384 * n, 384)
        return remote(
            red.at[to_x, :, cols], r1.at[slot, :, cols], s1.at[n, to_x], t1.at[n, slot], (grp, 2 * to_x + c))

    def step2(d):
        to = lax.rem(grp + d, 32)
        return remote(buf.at[to], r2.at[chip], s2.at[d], t2.at[d], (to, sp))

    @pl.when(busy)
    def _():
        @pl.loop(0, SLOTS)
        def _(f):
            kept = sp * SLOTS + f < total
            branch = jnp.dot(att_s[f], wo_s[...], preferred_element_type=F32)
            mid[f] = (hid[f].astype(F32) + gate_ref[0:1, :] * branch).astype(BF)
            nrm[f] = jnp.where(kept, gate_ref[1:2, :] * cot[f].astype(F32), 0.0).astype(BF)

        unorder = shuffle(True)
        for i in range(GROUPS // 2):
            for d in range(1, 8):
                back(i, d).wait_recv()

        @pl.loop(0, 8)
        def _(t):
            got = jnp.dot(unorder, attp[t].reshape(128, PAD), preferred_element_type=F32).astype(BF)
            att[:, pixels(t), :] = got.reshape(SLOTS, OWN, PAD)

        def gradient(n):
            cols = slice(384 * n, 384 * n + 384)
            got = lax.dot_general(
                att[...].reshape(SLOTS * PIX, PAD), nrm[:, :, cols].reshape(SLOTS * PIX, 384),
                (((0,), (0,)), ((), ())), preferred_element_type=F32) * (1.0 / PIX)
            for t in range(8):
                part = jnp.concatenate([got[72 * t : 72 * t + 72], jnp.zeros((8, 384), F32)], axis=0)
                g_part[t // 2, t % 2, :, cols] = part.astype(BF)
            swap(n).start()

        def pass_on(n):
            cols = slice(384 * n, 384 * n + 384)
            swap(n).wait()
            for i in range(4):
                red[i, :, cols] = (g_part[i, c, :, cols].astype(F32) + r0[i, :, cols].astype(F32)).astype(BF)
            for i in range(4):
                @pl.when(2 * i + c != sp)
                def _(i=i):
                    step1(n, i).start()

                @pl.when(2 * i + c == sp)
                def _(i=i):
                    r1[slot, :, cols] = red[i, :, cols]

        gradient(0)
        gradient(1)
        pass_on(0)
        gradient(2)
        pass_on(1)
        pass_on(2)

        @pl.loop(0, SLOTS)
        def _(f):
            kept = sp * SLOTS + f < total
            branch = jnp.dot(att[f], wo_t[...], preferred_element_type=F32)
            out = mid[f].astype(F32) + gate_ref[1:2, :] * branch
            hid[f] = jnp.where(kept, out, 0.0).astype(BF)

    @pl.when(sp >= SENDERS)
    def _():
        hid[...] = jnp.zeros_like(hid)

    result = pltpu.make_async_copy(hid, out_ref, out_sem)
    result.start()

    @pl.when(low == c)
    def _():
        for n in range(3):
            for s in range(SENDERS):
                @pl.when(sp != s)
                def _(n=n, s=s):
                    cols = pl.ds(384 * n, 384)
                    remote(
                        red.at[0, :, cols], r1.at[s, :, cols], s1.at[n, 0], t1.at[n, s], sibling).wait_recv()

        whole = r1[0].astype(F32)
        for s in range(1, SENDERS):
            whole = whole + r1[s].astype(F32)
        whole = jnp.concatenate([whole, jnp.zeros((48, WIDTH), F32)], axis=0)
        for n in range(9):
            flipped[128 * n : 128 * n + 128] = whole[:, 128 * n : 128 * n + 128].T
        for g in range(32):
            part = jnp.concatenate([flipped[36 * g : 36 * g + 36], jnp.zeros((12, 128), F32)], axis=0)
            buf[g] = part.astype(BF)

        @pl.loop(1, 32)
        def _(d):
            step2(d).start()

        r2[chip] = buf[grp]

        @pl.loop(1, 32)
        def _(d):
            step2(d).wait_send()

    @pl.loop(1, 32)
    def _(d):
        @pl.when(lax.rem(grp + 32 - d, 2) == low)
        def _():
            step2(d).wait_recv()

    whole = r2[0].astype(F32)
    for i in range(1, 16):
        whole = whole + r2[i].astype(F32)
    grad_ref[...] = whole[:36, :HDIM]

    drain_s()
    drain_t()

    @pl.when(busy)
    def _():
        for n in range(3):
            for i in range(4):
                @pl.when(2 * i + c != sp)
                def _(n=n, i=i):
                    step1(n, i).wait_send()

        for d in range(1, 8):
            early(d).wait_send()
            for i in range(batches):
                there(i, d).wait_send()

    for i in range(GROUPS // 2):
        for d in range(1, 8):
            @if_gets(d)
            def _(d=d, i=i):
                back(i, d).wait_send()

    result.wait()


def on_device(
    hidden,
    frame_counts,
    shifts,
    gates,
    w_qkv_spatial,
    w_out_spatial,
    w_qkv_temporal,
    w_out_temporal,
    cotangent,
):
    frames = (SLOTS, PIX, WIDTH)
    dma = pltpu.SemaphoreType.DMA
    block_out, grad = pl.pallas_call(
        block_kernel,
        out_shape=(jax.ShapeDtypeStruct(frames, BF), jax.ShapeDtypeStruct((36, HDIM), F32)),
        in_specs=[SM, VM, VM, ANY, ANY, VM, VM, VM, VM],
        out_specs=(ANY, VM),
        scratch_shapes=[
            pltpu.VMEM((4, 4, 2, 48, PACK), BF),
            pltpu.VMEM((4, 4, 2, 48, PACK), BF),
            pltpu.VMEM((WIDTH, 3 * PAD), BF),
            pltpu.VMEM((PAD, WIDTH), BF),
            pltpu.VMEM((PAD, WIDTH), BF),
            *[pltpu.VMEM(frames, BF)] * 4,
            pltpu.VMEM((BATCH, PIX, 3 * PAD), BF),
            pltpu.VMEM((SLOTS, PIX, PAD), BF),
            pltpu.VMEM((SENDERS, SLOTS, OWN, WIDTH), BF),
            pltpu.VMEM((SENDERS, SLOTS, OWN, PAD), BF),
            pltpu.VMEM((GROUPS, SENDERS, 16, WIDTH), BF),
            pltpu.VMEM((2, SENDERS * 16, 3 * PAD), BF),
            pltpu.VMEM((SENDERS, GROUPS, 16, PAD), BF),
            pltpu.VMEM((8, GROUPS, 16, PAD), BF),
            pltpu.VMEM((SLOTS, PIX, PAD), BF),
            pltpu.VMEM((4, 2, 80, WIDTH), BF),
            pltpu.VMEM((4, 80, WIDTH), BF),
            pltpu.VMEM((4, 80, WIDTH), BF),
            pltpu.VMEM((SENDERS, 80, WIDTH), BF),
            pltpu.VMEM((WIDTH, 128), F32),
            pltpu.VMEM((32, 48, 128), BF),
            pltpu.VMEM((16, 48, 128), BF),
            dma((COPIES,)), dma((COPIES,)), dma((COPIES,)), dma((COPIES,)),
            dma((3,)), dma((8,)), dma((8,)),
            dma((4, 8)), dma((4, 8)), dma((4,)),
            dma((4, 8)), dma((4, 8)),
            dma((3,)), dma((3,)), dma((3, 4)), dma((3, SENDERS)), dma((32,)), dma((32,)), dma,
        ],
        compiler_params=pltpu.CompilerParams(
            vmem_limit_bytes=BIG, collective_id=1, has_side_effects=True),
        name="block",
    )(
        frame_counts, shifts[0], gates[0], hidden[0], cotangent[0],
        w_qkv_spatial, w_out_spatial, w_qkv_temporal, w_out_temporal,
    )
    return block_out[None], grad


def solution(mesh):
    return jax.shard_map(
        on_device,
        mesh=mesh,
        in_specs=(
            P("grp", "sp", None, None),
            P("grp"),
            P("grp", None, None),
            P("grp", None, None),
            P("grp", None),
            P("grp", None),
            P("grp", None),
            P("grp", None),
            P("grp", "sp", None, None),
        ),
        out_specs=(P("grp", "sp", None, None), P("grp", "sp")),
        check_vma=False,
    )
```

```python
import math

import jax
import jax.numpy as jnp
from jax import lax
from jax.experimental import pallas as pl
from jax.experimental.pallas import tpu as pltpu
from jax.sharding import PartitionSpec as P

MESH = pl.DeviceIdType.MESH
BF = jnp.bfloat16
F32 = jnp.float32
HDIM = 72
WIDTH = 1152
INNER = 576
PAD = 640
PIX = 128
SLOTS = 8
OWN = 16
SENDERS = 6
PACK = 1792
SCALE = math.log2(math.e) / math.sqrt(HDIM)
BATCH = 2
GROUPS = 8
ANY = pl.BlockSpec(memory_space=pl.ANY)
VM = pl.BlockSpec(memory_space=pltpu.VMEM)
SM = pl.BlockSpec(memory_space=pltpu.SMEM)
BIG = 56 * 1024 * 1024


def greet(partners):
    barrier = pltpu.get_barrier_semaphore()
    for who in partners:
        pl.semaphore_signal(barrier, inc=1, device_id=who, device_id_type=MESH)
    pl.semaphore_wait(barrier, len(partners))


def pack(qkv_ref, out_ref):
    qkv, out = qkv_ref[...].astype(F32), out_ref[...].astype(F32)
    k, v = qkv[:, INNER : 2 * INNER], qkv[:, 2 * INNER :]
    top = jnp.concatenate([qkv[:, :INNER], k[:, 512:], k[:, :512], v, jnp.zeros((36, 64), F32)], axis=1)
    blank = jnp.zeros((6, 64), F32)
    side = jnp.concatenate([
        jnp.concatenate([out[12:, :INNER], blank], axis=1),
        jnp.concatenate([blank, out[12:, INNER:]], axis=1),
    ], axis=0)
    low = jnp.concatenate([out[:12], side], axis=1)
    return jnp.concatenate([top, low], axis=0).astype(BF)


PLAIN = (
    ((), ("z1p", "z1q", "upp0", "dnp0", "upq0", "dnq0")),
    (("z1p",), ("z2p", "upp1", "dnp1")),
    (("z1q",), ("z2q", "upq1", "dnq1")),
    (("upp0", "dnp0"), ("farp0",)),
    (("upq0", "dnq0"), ("farq0",)),
    (("z2p",), ("z3p", "upp2", "dnp2")),
    (("z2q",), ("z3q", "upq2", "dnq2")),
    (("upp1", "dnp1"), ("farp1",)),
    (("upq1", "dnq1"), ("farq1",)),
    (("z3p",), ("upp3", "dnp3")),
    (("z3q",), ("upq3", "dnq3")),
    (("farp0", "farq0"), ("s0",)),
    (("upp2", "dnp2"), ("farp2",)),
    (("upq2", "dnq2"), ("farq2",)),
    (("farp1", "farq1"), ("s1",)),
    (("upp3", "dnp3"), ("farp3",)),
    (("upq3", "dnq3"), ("farq3",)),
    (("farp2", "farq2"), ("s2",)),
    (("farp3", "farq3"), ("s3",)),
)
MIXED = (
    ((), ("z1p", "z1q", "upp0", "dnp0", "by1u", "by1d", "by2", "upq0", "dnq0", "bz10")),
    (("z1p",), ("z2p", "upp1", "dnp1")),
    (("upp0", "dnp0"), ("farp0",)),
    (("z1q",), ("z2q", "upq1", "dnq1")),
    (("by1u", "by1d"), ("bz11", "bz12")),
    (("bz10",), ("bz20",)),
    (("z2p",), ("z3p", "upp2", "dnp2")),
    (("z2q",), ("z3q", "upq2", "dnq2")),
    (("by2",), ("bz13",)),
    (("upq0", "dnq0"), ("farq0",)),
    (("bz11",), ("bz21",)),
    (("upp1", "dnp1"), ("farp1",)),
    (("bz20",), ("bz30",)),
    (("bz12",), ("bz22",)),
    (("upq1", "dnq1"), ("farq1",)),
    (("z3p",), ("upp3", "dnp3")),
    (("z3q",), ("upq3", "dnq3")),
    (("farp0", "farq0"), ("s0",)),
    (("bz21",), ("bz31",)),
    (("bz13",), ("bz23",)),
    (("upp2", "dnp2"), ("farp2",)),
    (("bz22",), ("bz32",)),
    (("upq2", "dnq2"), ("farq2",)),
    (("bz30",), ("bz40",)),
    (("farp1", "farq1"), ("s1",)),
    (("bz31",), ("bz41",)),
    (("upp3", "dnp3"), ("farp3",)),
    (("bz23",), ("bz33",)),
    (("upq3", "dnq3"), ("farq3",)),
    (("bz32",), ("bz42",)),
    (("farp2", "farq2"), ("s2",)),
    (("bz40",), ("r0",)),
    (("bz41",), ("r1",)),
    (("bz33",), ("bz43",)),
    (("bz42",), ("r2",)),
    (("farp3", "farq3"), ("s3",)),
    (("bz43",), ("r3",)),
)


def gather_plan(full, ssem, rsem, split, order):
    grp, sp = lax.axis_index("grp"), lax.axis_index("sp")
    h, y, c = grp // 8, (grp // 2) % 4, grp % 2
    low = sp % 2
    up, down, far = lax.rem(y + 1, 4), lax.rem(y + 3, 4), lax.rem(y + 2, 4)
    hx = lax.rem(h + 3 + 2 * low, 4)
    hp = lax.rem(h + 5 - 2 * low, 4)
    hf = lax.rem(h + 2, 4)
    sibling = (grp + 1 - 2 * c, sp)
    y_up = ((h * 4 + up) * 2 + c, sp)
    y_down = ((h * 4 + down) * 2 + c, sp)
    pair = (grp, sp + 1 - 2 * low)
    cross = (hx * 8 + y * 2 + c, sp + 1 - 2 * low)
    al = slice(None)
    hs = (h, hx, hp, hf)
    table = {}

    def add(name, where, who):
        table[name] = (len(table), where, who)

    for stream, cols in (("p", pl.ds(0, split // 2)), ("q", pl.ds(split // 2, split // 2))):
        add("z1" + stream, (h, y, c, al, cols), cross)
        add("z2" + stream, (hx, y, c, al, cols), pair)
        add("z3" + stream, (hp, y, c, al, cols), cross)
        for k in range(4):
            add(f"up{stream}{k}", (hs[k], y, c, al, cols), y_up)
            add(f"dn{stream}{k}", (hs[k], y, c, al, cols), y_down)
            if stream == "p":
                add(f"farp{k}", (hs[k], down, c, al, cols), y_up)
            else:
                add(f"farq{k}", (hs[k], up, c, al, cols), y_down)
    for k in range(4):
        add(f"s{k}", (hs[k], al, c, al, pl.ds(0, split)), sibling)
    if split < PACK:
        rest = PACK - split
        cols = pl.ds(split, rest)
        ys = (y, up, down, far)

        def part(which):
            return pl.ds(pl.multiple_of(split + which * (rest // 2), 128), rest // 2)

        add("by1u", (h, y, c, al, cols), y_up)
        add("by1d", (h, y, c, al, cols), y_down)
        add("by2", (h, y, c, al, cols), ((h * 4 + far) * 2 + c, sp))
        for k in range(4):
            add(f"bz1{k}", (h, ys[k], c, al, cols), cross)
            add(f"bz2{k}", (hx, ys[k], c, al, cols), pair)
            add(f"bz3{k}", (hp, ys[k], c, al, part(1 - low)), cross)
            add(f"bz4{k}", (hf, ys[k], c, al, part(low)), pair)
            add(f"r{k}", (al, ys[k], c, al, cols), sibling)

    def copy(name):
        i, where, who = table[name]
        return pltpu.make_async_remote_copy(
            src_ref=full.at[where], dst_ref=full.at[where], send_sem=ssem.at[i], recv_sem=rsem.at[i],
            device_id=who, device_id_type=MESH)

    def step(waits, starts):
        def run():
            for name in waits:
                copy(name).wait_recv()
            for name in starts:
                copy(name).start()
        return run

    def settle(k):
        copy(f"s{k}").wait_recv()
        return hs[k]

    def settle_rest():
        for k in range(4):
            copy(f"r{k}").wait_recv()

    def drain():
        for name in table:
            copy(name).wait_send()

    settled = (settle, settle_rest if split < PACK else None, hs)
    return [step(*both) for both in order], settled, drain, (h, y, c), cross


COPIES = 57
SPLIT = 1024


def iota(shape, dim):
    return lax.broadcasted_iota(jnp.int32, shape, dim)


def picks(condition):
    return condition.astype(F32).astype(BF)


def unpack(full, settled, wq, wo):
    col, row = iota((144, 192), 1), iota((144, 192), 0)
    of, at = col // 48, col % 48
    top = picks((at < 36) & (36 * of + at == row))
    col, row = iota((72, 192), 1), iota((72, 192), 0)
    of, at = col // 48, col % 48 - 36
    main = picks((at >= 0) & (18 * of + at == row) & (at < 12))
    left = picks((at >= 0) & (at < 6) & (18 * of + 12 + at == row))
    right = picks((at >= 6) & (18 * of + 6 + at == row))
    keep = iota((144, 128), 1) < 64
    settle, settle_rest, hs = settled

    def block(h, i, first, last):
        return full[h, 2 * i : 2 * i + 2, :, :, first:last].reshape(192, last - first)

    def rows_of(h, i):
        return pl.ds(pl.multiple_of((2 * h + i) * 144, 16), 144)

    def low_columns(h):
        for i in range(2):
            rows = rows_of(h, i)
            got = jnp.dot(top, block(h, i, 0, SPLIT), preferred_element_type=F32)
            mixed = got[:, 512:640]
            turned = jnp.concatenate([mixed[:, 64:], mixed[:, :64]], axis=1)
            wq[rows, 0:512] = got[:, 0:512].astype(BF)
            wq[rows, 512:640] = jnp.where(keep, mixed, 0.0).astype(BF)
            wq[rows, 640:SPLIT] = got[:, 640:SPLIT].astype(BF)
            wq[rows, 1152:1280] = jnp.where(keep, turned, 0.0).astype(BF)

    def high_columns(h):
        outs = []
        for i in range(2):
            rows, packed = rows_of(h, i), block(h, i, 0, PACK)
            got = jnp.dot(top, packed[:, SPLIT:], preferred_element_type=F32)
            wq[rows, SPLIT:1152] = got[:, : 1152 - SPLIT].astype(BF)
            wq[rows, 1280:1920] = got[:, 1152 - SPLIT :].astype(BF)
            whole = jnp.dot(main, packed[:, :WIDTH], preferred_element_type=F32)
            side = packed[:, WIDTH:]
            one = jnp.dot(left, side, preferred_element_type=F32)
            two = jnp.dot(right, side, preferred_element_type=F32)
            blank = jnp.zeros((72, 512), F32)
            outs.append(whole + jnp.concatenate([one, blank], axis=1) + jnp.concatenate([blank, two], axis=1))
        wo[pl.ds(pl.multiple_of(144 * h, 16), 144), :] = jnp.concatenate(outs, axis=0).astype(BF)

    wo[INNER:, :] = jnp.zeros((PAD - INNER, WIDTH), BF)
    for k in range(4):
        settle(k)
        low_columns(hs[k])
        if settle_rest is None:
            high_columns(hs[k])
    if settle_rest is not None:
        settle_rest()
        for k in range(4):
            high_columns(hs[k])


def modulated(x, offsets, shift_row, scale_row):
    mean = jnp.sum(x, axis=-1, keepdims=True) * (1.0 / WIDTH)
    x = x - mean
    spread = jnp.sum(x * x, axis=-1, keepdims=True) * (1.0 / WIDTH)
    x = x * lax.rsqrt(spread + 1e-06)
    return (x * (1.0 + offsets[scale_row]) + offsets[shift_row]).astype(BF)


def head_masks(j):
    lane = iota((1, 256), 1)
    start = 16 * j
    one = picks((lane >= start) & (lane < start + HDIM))
    two = picks((lane >= start + HDIM) & (lane < start + 2 * HDIM))
    return one, two


def attention(load, keys, valid):
    blocks = [None] * 5
    fill = [] if keys == PIX else [jnp.zeros((PIX - keys, 256), BF)]
    for j in range(4):
        one, two = head_masks(j)
        q, k, v = (load(part * PAD + 128 * j) for part in range(3))
        kk = jnp.concatenate([k * one, *fill, k * two, *fill], axis=0)
        vv = jnp.concatenate([v * one, *fill, v * two, *fill], axis=0)
        heads = jnp.concatenate(
            [jnp.broadcast_to(one, (PIX, 256)), jnp.broadcast_to(two, (PIX, 256))], axis=0)
        s = lax.dot_general(q, kk, (((1,), (1,)), ((), ())), preferred_element_type=F32)
        expo = []
        for part in (s[:, :128], s[:, 128:]):
            if valid is not None:
                part = jnp.where(valid, part, -1e30)
            top = jnp.max(part, axis=-1, keepdims=True)
            expo.append(jnp.exp2((part - top) * SCALE).astype(BF))
        expo = jnp.concatenate(expo, axis=1)
        o = jnp.dot(expo, vv, preferred_element_type=F32)
        total = jnp.dot(expo, heads, preferred_element_type=F32)
        o = o * (1.0 / jnp.where(total == 0.0, 1.0, total))
        for i, piece in ((j, o[:, :128]), (j + 1, o[:, 128:])):
            blocks[i] = piece if blocks[i] is None else blocks[i] + piece
    return jnp.concatenate(blocks, axis=1).astype(BF)


def shuffle(back):
    there, here = iota((128, 128), 1 if back else 0), iota((128, 128), 0 if back else 1)
    return picks(here == (there % 8) * OWN + there // 8)


def block_kernel(
    total_ref, shift_ref, gate_ref, hidden_ref, cot_in_ref, w1_ref, w2_ref, w3_ref, w4_ref,
    out_ref, grad_ref,
    full_s, full_t, wq, wo_s, wo_t, hid, nrm, mid, cot, qkv, att_s, x_in, a_in, xp, qkv_t, ap, attp, att,
    g_part, r0, red, r1, flipped, buf, r2,
    gs_s, gr_s, gs_t, gr_t, load_sem, early_s, early_r, there_s, there_r, there_l, back_s, back_r,
    s0, t0, s1, t1, s2, t2, out_sem,
):
    grp, sp = lax.axis_index("grp"), lax.axis_index("sp")
    c, low, chip = grp % 2, sp % 2, grp // 2
    sibling = (grp + 1 - 2 * c, sp)
    slot = lax.rem(sp, SENDERS)
    busy = sp < SENDERS
    offsets = [shift_ref[i : i + 1, :] for i in range(4)]
    total = total_ref[0]
    rows = SENDERS * 16
    batches = SLOTS // BATCH

    def from_me(d):
        return lax.rem(sp + d, 8)

    def pixels(rank):
        return pl.ds(pl.multiple_of(rank * OWN, OWN), OWN)

    def if_sends(d):
        return pl.when(lax.rem(sp + 8 - d, 8) < SENDERS)

    def if_gets(d):
        return pl.when(from_me(d) < SENDERS)

    def remote(src, dst, send_sem, recv_sem, who):
        return pltpu.make_async_remote_copy(
            src_ref=src, dst_ref=dst, send_sem=send_sem, recv_sem=recv_sem,
            device_id=who, device_id_type=MESH)

    def early(d):
        to = from_me(d)
        return remote(hidden_ref.at[:, pixels(to), :], x_in.at[slot], early_s.at[d], early_r.at[d], (grp, to))

    def there(i, d):
        to, frames = from_me(d), pl.ds(BATCH * i, BATCH)
        return remote(
            att_s.at[frames, pixels(to), :], a_in.at[slot, frames], there_s.at[i, d], there_r.at[i, d], (grp, to))

    def there_own(i):
        frames = pl.ds(BATCH * i, BATCH)
        return pltpu.make_async_copy(att_s.at[frames, pixels(sp), :], a_in.at[slot, frames], there_l.at[i])

    def back(i, d):
        to, pairs = from_me(d), pl.ds(2 * i, 2)
        return remote(
            ap.at[lax.rem(to, SENDERS), pairs], attp.at[sp, pairs], back_s.at[i, d], back_r.at[i, d], (grp, to))

    steps_s, settled_s, drain_s, here, cross = gather_plan(full_s, gs_s, gr_s, SPLIT, MIXED)
    steps_t, settled_t, drain_t, _, _ = gather_plan(full_t, gs_t, gr_t, PACK, PLAIN)
    loads = [
        pltpu.make_async_copy(hidden_ref, hid, load_sem.at[0]),
        pltpu.make_async_copy(cot_in_ref, cot, load_sem.at[1]),
        pltpu.make_async_copy(hidden_ref.at[:, pixels(sp), :], x_in.at[slot], load_sem.at[2]),
    ]
    loads[0].start()
    loads[1].start()

    @pl.when(busy)
    def _():
        loads[2].start()

    full_s[here] = pack(w1_ref, w2_ref)
    full_t[here] = pack(w3_ref, w4_ref)
    greet_all = [(lax.rem(grp + d, 32), sp) for d in range(1, 32)]
    greet_all += [(grp, from_me(d)) for d in range(1, 8)] + [cross]
    greet(greet_all)
    steps_s[0]()

    @pl.when(busy)
    def _():
        for d in (4, 2, 6):
            early(d).start()

    loads[0].wait()
    loads[1].wait()

    @pl.loop(0, SLOTS)
    def _(f):
        @pl.when(busy)
        def _():
            nrm[f] = modulated(hid[f].astype(F32), offsets, 0, 1)

        for i in range(SLOTS):
            @pl.when(f == i)
            def _(i=i):
                steps_s[1 + i]()

    for run in steps_s[9:22]:
        run()

    @pl.when(busy)
    def _():
        for d in (3, 5, 1, 7):
            early(d).start()

    for run in steps_s[22:29]:
        run()
    steps_t[0]()
    for run in steps_s[29:]:
        run()
    unpack(full_s, settled_s, wq, wo_s)

    rest = steps_t[1:]

    @pl.loop(0, batches)
    def _(i):
        @pl.when(busy)
        def _():
            tokens = nrm[pl.ds(BATCH * i, BATCH)].reshape(BATCH * PIX, WIDTH)
            got = jnp.dot(tokens, wq[...], preferred_element_type=F32)
            qkv[...] = got.astype(BF).reshape(BATCH, PIX, 3 * PAD)
            for u in range(BATCH):
                att_s[BATCH * i + u] = attention(lambda first: qkv[u, :, first : first + 256], PIX, None)
            for d in (4, 3, 5, 2, 6, 1, 7):
                there(i, d).start()
            there_own(i).start()

        for n in range(batches):
            @pl.when(i == n)
            def _(n=n):
                for run in rest[(0, 5, 8, 10)[n] : (5, 8, 10, 12)[n]]:
                    run()

    rest = rest[12:]

    for d in range(1, 8):
        @if_sends(d)
        def _(d=d):
            early(d).wait_recv()

    @pl.when(busy)
    def _():
        loads[2].wait()

    @pl.loop(0, batches)
    def _(i):
        for n in range(batches):
            @pl.when(i == n)
            def _(n=n):
                for run in rest[2 * n : 2 * n + 2]:
                    run()

        for d in range(1, 8):
            @if_sends(d)
            def _(d=d):
                there(i, d).wait_recv()

        @pl.when(busy)
        def _():
            there_own(i).wait()

        frames = pl.ds(BATCH * i, BATCH)
        lines = SENDERS * BATCH * OWN
        branch = jnp.dot(a_in[:, frames].reshape(lines, PAD), wo_s[...], preferred_element_type=F32)
        middle = x_in[:, frames].reshape(lines, WIDTH).astype(F32) + gate_ref[0:1, :] * branch
        normed = modulated(middle.astype(BF).astype(F32), offsets, 2, 3)
        x_in[:, frames] = normed.reshape(SENDERS, BATCH, OWN, WIDTH)

    order = shuffle(False)

    @pl.loop(0, SENDERS)
    def _(s):
        got = jnp.dot(order, x_in[s].reshape(128, WIDTH), preferred_element_type=F32).astype(BF)
        xp[:, s] = got.reshape(GROUPS, 16, WIDTH)

    unpack(full_t, settled_t, wq, wo_t)

    key, row = iota((rows, PIX), 1), iota((rows, PIX), 0)
    frame = (key // 16) * 8 + key % 8
    valid = (key < rows) & (frame < total) & ((key // 8) % 2 == (row // 8) % 2)

    @pl.loop(0, GROUPS // 2)
    def _(i):
        got = jnp.dot(xp[pl.ds(2 * i, 2)].reshape(2 * rows, WIDTH), wq[...], preferred_element_type=F32)
        qkv_t[...] = got.astype(BF).reshape(2, rows, 3 * PAD)
        for u in range(2):
            mixed = attention(lambda first: qkv_t[u, :, first : first + 256], rows, valid)
            ap[:, 2 * i + u] = mixed.reshape(SENDERS, 16, PAD)
        for d in (4, 3, 5, 2, 6, 1, 7):
            @if_gets(d)
            def _(d=d):
                back(i, d).start()

        @pl.when(busy)
        def _():
            attp[sp, pl.ds(2 * i, 2)] = ap[slot, pl.ds(2 * i, 2)]

    def swap(n):
        cols = pl.ds(384 * n, 384)
        return remote(g_part.at[:, 1 - c, :, cols], r0.at[:, :, cols], s0.at[n], t0.at[n], sibling)

    def step1(n, to_x):
        cols = pl.ds(384 * n, 384)
        return remote(
            red.at[to_x, :, cols], r1.at[slot, :, cols], s1.at[n, to_x], t1.at[n, slot], (grp, 2 * to_x + c))

    def step2(d):
        to = lax.rem(grp + d, 32)
        return remote(buf.at[to], r2.at[chip], s2.at[d], t2.at[d], (to, sp))

    @pl.when(busy)
    def _():
        @pl.loop(0, SLOTS)
        def _(f):
            kept = sp * SLOTS + f < total
            branch = jnp.dot(att_s[f], wo_s[...], preferred_element_type=F32)
            mid[f] = (hid[f].astype(F32) + gate_ref[0:1, :] * branch).astype(BF)
            nrm[f] = jnp.where(kept, gate_ref[1:2, :] * cot[f].astype(F32), 0.0).astype(BF)

        unorder = shuffle(True)
        for i in range(GROUPS // 2):
            for d in range(1, 8):
                back(i, d).wait_recv()

        @pl.loop(0, 8)
        def _(t):
            got = jnp.dot(unorder, attp[t].reshape(128, PAD), preferred_element_type=F32).astype(BF)
            att[:, pixels(t), :] = got.reshape(SLOTS, OWN, PAD)

        def gradient(n):
            cols = slice(384 * n, 384 * n + 384)
            got = lax.dot_general(
                att[...].reshape(SLOTS * PIX, PAD), nrm[:, :, cols].reshape(SLOTS * PIX, 384),
                (((0,), (0,)), ((), ())), preferred_element_type=F32) * (1.0 / PIX)
            for t in range(8):
                part = jnp.concatenate([got[72 * t : 72 * t + 72], jnp.zeros((8, 384), F32)], axis=0)
                g_part[t // 2, t % 2, :, cols] = part.astype(BF)
            swap(n).start()

        def pass_on(n):
            cols = slice(384 * n, 384 * n + 384)
            swap(n).wait()
            for i in range(4):
                red[i, :, cols] = (g_part[i, c, :, cols].astype(F32) + r0[i, :, cols].astype(F32)).astype(BF)
            for i in range(4):
                @pl.when(2 * i + c != sp)
                def _(i=i):
                    step1(n, i).start()

                @pl.when(2 * i + c == sp)
                def _(i=i):
                    r1[slot, :, cols] = red[i, :, cols]

        gradient(0)
        gradient(1)
        pass_on(0)
        gradient(2)
        pass_on(1)
        pass_on(2)

        @pl.loop(0, SLOTS)
        def _(f):
            kept = sp * SLOTS + f < total
            branch = jnp.dot(att[f], wo_t[...], preferred_element_type=F32)
            out = mid[f].astype(F32) + gate_ref[1:2, :] * branch
            hid[f] = jnp.where(kept, out, 0.0).astype(BF)

    @pl.when(sp >= SENDERS)
    def _():
        hid[...] = jnp.zeros_like(hid)

    result = pltpu.make_async_copy(hid, out_ref, out_sem)
    result.start()

    @pl.when(low == c)
    def _():
        for n in range(3):
            for s in range(SENDERS):
                @pl.when(sp != s)
                def _(n=n, s=s):
                    cols = pl.ds(384 * n, 384)
                    remote(
                        red.at[0, :, cols], r1.at[s, :, cols], s1.at[n, 0], t1.at[n, s], sibling).wait_recv()

        whole = r1[0].astype(F32)
        for s in range(1, SENDERS):
            whole = whole + r1[s].astype(F32)
        whole = jnp.concatenate([whole, jnp.zeros((48, WIDTH), F32)], axis=0)
        for n in range(9):
            flipped[128 * n : 128 * n + 128] = whole[:, 128 * n : 128 * n + 128].T
        for g in range(32):
            part = jnp.concatenate([flipped[36 * g : 36 * g + 36], jnp.zeros((12, 128), F32)], axis=0)
            buf[g] = part.astype(BF)

        @pl.loop(1, 32)
        def _(d):
            step2(d).start()

        r2[chip] = buf[grp]

        @pl.loop(1, 32)
        def _(d):
            step2(d).wait_send()

    @pl.loop(1, 32)
    def _(d):
        @pl.when(lax.rem(grp + 32 - d, 2) == low)
        def _():
            step2(d).wait_recv()

    whole = r2[0].astype(F32)
    for i in range(1, 16):
        whole = whole + r2[i].astype(F32)
    grad_ref[...] = whole[:36, :HDIM]

    drain_s()
    drain_t()

    @pl.when(busy)
    def _():
        for n in range(3):
            for i in range(4):
                @pl.when(2 * i + c != sp)
                def _(n=n, i=i):
                    step1(n, i).wait_send()

        for d in range(1, 8):
            early(d).wait_send()
            for i in range(batches):
                there(i, d).wait_send()

    for i in range(GROUPS // 2):
        for d in range(1, 8):
            @if_gets(d)
            def _(d=d, i=i):
                back(i, d).wait_send()

    result.wait()


def on_device(
    hidden,
    frame_counts,
    shifts,
    gates,
    w_qkv_spatial,
    w_out_spatial,
    w_qkv_temporal,
    w_out_temporal,
    cotangent,
):
    frames = (SLOTS, PIX, WIDTH)
    dma = pltpu.SemaphoreType.DMA
    block_out, grad = pl.pallas_call(
        block_kernel,
        out_shape=(jax.ShapeDtypeStruct(frames, BF), jax.ShapeDtypeStruct((36, HDIM), F32)),
        in_specs=[SM, VM, VM, ANY, ANY, VM, VM, VM, VM],
        out_specs=(ANY, VM),
        scratch_shapes=[
            pltpu.VMEM((4, 4, 2, 48, PACK), BF),
            pltpu.VMEM((4, 4, 2, 48, PACK), BF),
            pltpu.VMEM((WIDTH, 3 * PAD), BF),
            pltpu.VMEM((PAD, WIDTH), BF),
            pltpu.VMEM((PAD, WIDTH), BF),
            *[pltpu.VMEM(frames, BF)] * 4,
            pltpu.VMEM((BATCH, PIX, 3 * PAD), BF),
            pltpu.VMEM((SLOTS, PIX, PAD), BF),
            pltpu.VMEM((SENDERS, SLOTS, OWN, WIDTH), BF),
            pltpu.VMEM((SENDERS, SLOTS, OWN, PAD), BF),
            pltpu.VMEM((GROUPS, SENDERS, 16, WIDTH), BF),
            pltpu.VMEM((2, SENDERS * 16, 3 * PAD), BF),
            pltpu.VMEM((SENDERS, GROUPS, 16, PAD), BF),
            pltpu.VMEM((8, GROUPS, 16, PAD), BF),
            pltpu.VMEM((SLOTS, PIX, PAD), BF),
            pltpu.VMEM((4, 2, 80, WIDTH), BF),
            pltpu.VMEM((4, 80, WIDTH), BF),
            pltpu.VMEM((4, 80, WIDTH), BF),
            pltpu.VMEM((SENDERS, 80, WIDTH), BF),
            pltpu.VMEM((WIDTH, 128), F32),
            pltpu.VMEM((32, 48, 128), BF),
            pltpu.VMEM((16, 48, 128), BF),
            dma((COPIES,)), dma((COPIES,)), dma((COPIES,)), dma((COPIES,)),
            dma((3,)), dma((8,)), dma((8,)),
            dma((4, 8)), dma((4, 8)), dma((4,)),
            dma((4, 8)), dma((4, 8)),
            dma((3,)), dma((3,)), dma((3, 4)), dma((3, SENDERS)), dma((32,)), dma((32,)), dma,
        ],
        compiler_params=pltpu.CompilerParams(
            vmem_limit_bytes=BIG, collective_id=1, has_side_effects=True),
        name="block",
    )(
        frame_counts, shifts[0], gates[0], hidden[0], cotangent[0],
        w_qkv_spatial, w_out_spatial, w_qkv_temporal, w_out_temporal,
    )
    return block_out[None], grad


def solution(mesh):
    return jax.shard_map(
        on_device,
        mesh=mesh,
        in_specs=(
            P("grp", "sp", None, None),
            P("grp"),
            P("grp", None, None),
            P("grp", None, None),
            P("grp", None),
            P("grp", None),
            P("grp", None),
            P("grp", None),
            P("grp", "sp", None, None),
        ),
        out_specs=(P("grp", "sp", None, None), P("grp", "sp")),
        check_vma=False,
    )
```

```python
import math

import jax
import jax.numpy as jnp
from jax import lax
from jax.experimental import pallas as pl
from jax.experimental.pallas import tpu as pltpu
from jax.sharding import PartitionSpec as P

MESH = pl.DeviceIdType.MESH
BF = jnp.bfloat16
F32 = jnp.float32
HDIM = 72
WIDTH = 1152
INNER = 576
PAD = 640
PIX = 128
SLOTS = 8
OWN = 16
SENDERS = 6
PACK = 1792
SCALE = math.log2(math.e) / math.sqrt(HDIM)
BATCH = 2
GROUPS = 8
ANY = pl.BlockSpec(memory_space=pl.ANY)
VM = pl.BlockSpec(memory_space=pltpu.VMEM)
SM = pl.BlockSpec(memory_space=pltpu.SMEM)
BIG = 56 * 1024 * 1024


def pack(qkv_ref, out_ref):
    qkv, out = qkv_ref[...].astype(F32), out_ref[...].astype(F32)
    k, v = qkv[:, INNER : 2 * INNER], qkv[:, 2 * INNER :]
    top = jnp.concatenate([qkv[:, :INNER], k[:, 512:], k[:, :512], v, jnp.zeros((36, 64), F32)], axis=1)
    blank = jnp.zeros((6, 64), F32)
    side = jnp.concatenate([
        jnp.concatenate([out[12:, :INNER], blank], axis=1),
        jnp.concatenate([blank, out[12:, INNER:]], axis=1),
    ], axis=0)
    low = jnp.concatenate([out[:12], side], axis=1)
    return jnp.concatenate([top, low], axis=0).astype(BF)


STEPS = (
    ((), ("z1p", "z1q")),
    ((), ("upp0", "dnp0", "upq0", "dnq0")),
    (("z1p",), ("z2p", "upp1", "dnp1")),
    (("z1q",), ("z2q", "upq1", "dnq1")),
    (("upp0", "dnp0"), ("farp0",)),
    (("upq0", "dnq0"), ("farq0",)),
    (("z2p",), ("z3p", "upp2", "dnp2")),
    (("z2q",), ("z3q", "upq2", "dnq2")),
    (("upp1", "dnp1"), ("farp1",)),
    (("upq1", "dnq1"), ("farq1",)),
    (("z3p",), ("upp3", "dnp3")),
    (("z3q",), ("upq3", "dnq3")),
    (("farp0", "farq0"), ("s0",)),
    (("upp2", "dnp2"), ("farp2",)),
    (("upq2", "dnq2"), ("farq2",)),
    (("farp1", "farq1"), ("s1",)),
    (("upp3", "dnp3"), ("farp3",)),
    (("upq3", "dnq3"), ("farq3",)),
    (("farp2", "farq2"), ("s2",)),
    (("farp3", "farq3"), ("s3",)),
)


def gather_plan(full, ssem, rsem):
    grp, sp = lax.axis_index("grp"), lax.axis_index("sp")
    h, y, c = grp // 8, (grp // 2) % 4, grp % 2
    low = sp % 2
    up, down = lax.rem(y + 1, 4), lax.rem(y + 3, 4)
    hx = lax.rem(h + 3 + 2 * low, 4)
    hp = lax.rem(h + 5 - 2 * low, 4)
    hf = lax.rem(h + 2, 4)
    sibling = (grp + 1 - 2 * c, sp)
    y_up = ((h * 4 + up) * 2 + c, sp)
    y_down = ((h * 4 + down) * 2 + c, sp)
    pair = (grp, sp + 1 - 2 * low)
    cross = (hx * 8 + y * 2 + c, sp + 1 - 2 * low)
    al = slice(None)
    hs = (h, hx, hp, hf)
    table = {}

    def add(name, where, who):
        table[name] = (len(table), where, who)

    for stream, cols in (("p", pl.ds(0, PACK // 2)), ("q", pl.ds(PACK // 2, PACK // 2))):
        add("z1" + stream, (h, y, c, al, cols), cross)
        add("z2" + stream, (hx, y, c, al, cols), pair)
        add("z3" + stream, (hp, y, c, al, cols), cross)
        for k in range(4):
            add(f"up{stream}{k}", (hs[k], y, c, al, cols), y_up)
            add(f"dn{stream}{k}", (hs[k], y, c, al, cols), y_down)
            if stream == "p":
                add(f"farp{k}", (hs[k], down, c, al, cols), y_up)
            else:
                add(f"farq{k}", (hs[k], up, c, al, cols), y_down)
    for k in range(4):
        add(f"s{k}", (hs[k], al, c), sibling)

    def copy(name):
        i, where, who = table[name]
        return pltpu.make_async_remote_copy(
            src_ref=full.at[where], dst_ref=full.at[where], send_sem=ssem.at[i], recv_sem=rsem.at[i],
            device_id=who, device_id_type=MESH)

    def step(waits, starts):
        def run():
            for name in waits:
                copy(name).wait_recv()
            for name in starts:
                copy(name).start()
        return run

    def settle(k):
        copy(f"s{k}").wait_recv()
        return hs[k]

    def drain():
        for name in table:
            copy(name).wait_send()

    return [step(*both) for both in STEPS], settle, drain, (h, y, c), [sibling, y_up, y_down, cross]


COPIES = 34


def iota(shape, dim):
    return lax.broadcasted_iota(jnp.int32, shape, dim)


def picks(condition):
    return condition.astype(F32).astype(BF)


def unpack(full, settle, wq, wo):
    col, row = iota((144, 192), 1), iota((144, 192), 0)
    of, at = col // 48, col % 48
    top = picks((at < 36) & (36 * of + at == row))
    col, row = iota((72, 192), 1), iota((72, 192), 0)
    of, at = col // 48, col % 48 - 36
    main = picks((at >= 0) & (18 * of + at == row) & (at < 12))
    left = picks((at >= 0) & (at < 6) & (18 * of + 12 + at == row))
    right = picks((at >= 6) & (18 * of + 6 + at == row))
    keep = iota((144, 128), 1) < 64

    wo[INNER:, :] = jnp.zeros((PAD - INNER, WIDTH), BF)
    for k in range(4):
        h = settle(k)
        outs = []
        for i in range(2):
            block = full[h, 2 * i : 2 * i + 2].reshape(192, PACK)
            got = jnp.dot(top, block, preferred_element_type=F32)
            rows = pl.ds(pl.multiple_of((2 * h + i) * 144, 16), 144)
            mixed = got[:, 512:640]
            turned = jnp.concatenate([mixed[:, 64:], mixed[:, :64]], axis=1)
            wq[rows, 0:512] = got[:, 0:512].astype(BF)
            wq[rows, 512:640] = jnp.where(keep, mixed, 0.0).astype(BF)
            wq[rows, 640:1152] = got[:, 640:1152].astype(BF)
            wq[rows, 1152:1280] = jnp.where(keep, turned, 0.0).astype(BF)
            wq[rows, 1280:1920] = got[:, 1152:1792].astype(BF)
            whole = jnp.dot(main, block[:, :WIDTH], preferred_element_type=F32)
            side = block[:, WIDTH:]
            one = jnp.dot(left, side, preferred_element_type=F32)
            two = jnp.dot(right, side, preferred_element_type=F32)
            blank = jnp.zeros((72, 512), F32)
            outs.append(whole + jnp.concatenate([one, blank], axis=1) + jnp.concatenate([blank, two], axis=1))
        wo[pl.ds(pl.multiple_of(144 * h, 16), 144), :] = jnp.concatenate(outs, axis=0).astype(BF)


def modulated(x, offsets, shift_row, scale_row):
    mean = jnp.sum(x, axis=-1, keepdims=True) * (1.0 / WIDTH)
    x = x - mean
    spread = jnp.sum(x * x, axis=-1, keepdims=True) * (1.0 / WIDTH)
    x = x * lax.rsqrt(spread + 1e-06)
    return (x * (1.0 + offsets[scale_row]) + offsets[shift_row]).astype(BF)


def head_masks(j):
    lane = iota((1, 256), 1)
    start = 16 * j
    one = picks((lane >= start) & (lane < start + HDIM))
    two = picks((lane >= start + HDIM) & (lane < start + 2 * HDIM))
    return one, two


def attention(load, keys, valid):
    blocks = [None] * 5
    fill = [] if keys == PIX else [jnp.zeros((PIX - keys, 256), BF)]
    for j in range(4):
        one, two = head_masks(j)
        q, k, v = (load(part * PAD + 128 * j) for part in range(3))
        kk = jnp.concatenate([k * one, *fill, k * two, *fill], axis=0)
        vv = jnp.concatenate([v * one, *fill, v * two, *fill], axis=0)
        heads = jnp.concatenate(
            [jnp.broadcast_to(one, (PIX, 256)), jnp.broadcast_to(two, (PIX, 256))], axis=0)
        s = lax.dot_general(q, kk, (((1,), (1,)), ((), ())), preferred_element_type=F32)
        expo = []
        for part in (s[:, :128], s[:, 128:]):
            if valid is not None:
                part = jnp.where(valid, part, -1e30)
            top = jnp.max(part, axis=-1, keepdims=True)
            expo.append(jnp.exp2((part - top) * SCALE).astype(BF))
        expo = jnp.concatenate(expo, axis=1)
        o = jnp.dot(expo, vv, preferred_element_type=F32)
        total = jnp.dot(expo, heads, preferred_element_type=F32)
        o = o * (1.0 / jnp.where(total == 0.0, 1.0, total))
        for i, piece in ((j, o[:, :128]), (j + 1, o[:, 128:])):
            blocks[i] = piece if blocks[i] is None else blocks[i] + piece
    return jnp.concatenate(blocks, axis=1).astype(BF)


def shuffle(back):
    there, here = iota((128, 128), 1 if back else 0), iota((128, 128), 0 if back else 1)
    return picks(here == (there % 8) * OWN + there // 8)


def block_kernel(
    total_ref, shift_ref, gate_ref, hidden_ref, cot_in_ref, w1_ref, w2_ref, w3_ref, w4_ref,
    out_ref, grad_ref,
    full_s, full_t, wq, wo_s, wo_t, hid, nrm, mid, cot, qkv, att_s, x_in, a_in, xp, qkv_t, ap, attp, att,
    scp, acc, g_part, r0, red, r1, flipped, buf, r2,
    gs_s, gr_s, gs_t, gr_t, load_sem, early_s, early_r, there_s, there_r, there_l, back_s, back_r,
    s0, t0, s1, t1, s2, t2, out_sem,
):
    grp, sp = lax.axis_index("grp"), lax.axis_index("sp")
    c, low, chip = grp % 2, sp % 2, grp // 2
    sibling = (grp + 1 - 2 * c, sp)
    slot = lax.rem(sp, SENDERS)
    busy = sp < SENDERS
    offsets = [shift_ref[i : i + 1, :] for i in range(4)]
    total = total_ref[0]
    rows = SENDERS * 16
    batches = SLOTS // BATCH

    def from_me(d):
        return lax.rem(sp + d, 8)

    def pixels(rank):
        return pl.ds(pl.multiple_of(rank * OWN, OWN), OWN)

    def if_sends(d):
        return pl.when(lax.rem(sp + 8 - d, 8) < SENDERS)

    def if_gets(d):
        return pl.when(from_me(d) < SENDERS)

    def remote(src, dst, send_sem, recv_sem, who):
        return pltpu.make_async_remote_copy(
            src_ref=src, dst_ref=dst, send_sem=send_sem, recv_sem=recv_sem,
            device_id=who, device_id_type=MESH)

    def early(i, d):
        to, frames = from_me(d), pl.ds(BATCH * i, BATCH)
        return remote(
            hidden_ref.at[frames, pixels(to), :], x_in.at[slot, frames], early_s.at[i, d], early_r.at[i, d], (grp, to))

    def there(i, d):
        to, frames = from_me(d), pl.ds(BATCH * i, BATCH)
        return remote(
            att_s.at[frames, pixels(to), :], a_in.at[slot, frames], there_s.at[i, d], there_r.at[i, d], (grp, to))

    def there_own(i):
        frames = pl.ds(BATCH * i, BATCH)
        return pltpu.make_async_copy(att_s.at[frames, pixels(sp), :], a_in.at[slot, frames], there_l.at[i])

    def back(i, d):
        to, pairs = from_me(d), pl.ds(2 * i, 2)
        return remote(
            ap.at[lax.rem(to, SENDERS), pairs], attp.at[sp, pairs], back_s.at[i, d], back_r.at[i, d], (grp, to))

    steps_s, settle_s, drain_s, here, neighbours = gather_plan(full_s, gs_s, gr_s)
    steps_t, settle_t, drain_t, _, _ = gather_plan(full_t, gs_t, gr_t)
    loads = [
        pltpu.make_async_copy(hidden_ref, hid, load_sem.at[0]),
        pltpu.make_async_copy(cot_in_ref, cot, load_sem.at[1]),
        pltpu.make_async_copy(hidden_ref.at[:, pixels(sp), :], x_in.at[slot], load_sem.at[2]),
    ]
    loads[0].start()
    loads[1].start()

    @pl.when(busy)
    def _():
        loads[2].start()

    partners = neighbours + [(grp, from_me(d)) for d in range(1, 8)]
    barrier = pltpu.get_barrier_semaphore()
    for who in partners:
        pl.semaphore_signal(barrier, inc=1, device_id=who, device_id_type=MESH)
    full_s[here] = pack(w1_ref, w2_ref)
    pl.semaphore_wait(barrier, len(partners))
    steps_s[0]()
    steps_s[1]()

    @pl.when(busy)
    def _():
        for d in (3, 5, 1, 7):
            early(0, d).start()
        for i in range(batches):
            for d in (4, 2, 6):
                early(i, d).start()

    full_t[here] = pack(w3_ref, w4_ref)
    loads[0].wait()

    @pl.loop(0, SLOTS)
    def _(f):
        @pl.when(busy)
        def _():
            nrm[f] = modulated(hid[f].astype(F32), offsets, 0, 1)

        for i in range(SLOTS):
            @pl.when(f == i)
            def _(i=i):
                steps_s[2 + i]()

        @pl.when((f == 5) & busy)
        def _():
            @pl.loop(1, batches)
            def _(i):
                for d in (3, 5, 1, 7):
                    early(i, d).start()

    for run in steps_s[10:12]:
        run()
    steps_t[0]()
    for run in steps_s[12:18]:
        run()
    steps_t[1]()
    for run in steps_s[18:]:
        run()
    unpack(full_s, settle_s, wq, wo_s)

    rest = steps_t[2:]

    @pl.loop(0, batches)
    def _(i):
        @pl.when(busy)
        def _():
            tokens = nrm[pl.ds(BATCH * i, BATCH)].reshape(BATCH * PIX, WIDTH)
            got = jnp.dot(tokens, wq[...], preferred_element_type=F32)
            qkv[...] = got.astype(BF).reshape(BATCH, PIX, 3 * PAD)
            for u in range(BATCH):
                att_s[BATCH * i + u] = attention(lambda first: qkv[u, :, first : first + 256], PIX, None)
            for d in (4, 3, 5, 2, 6, 1, 7):
                there(i, d).start()
            there_own(i).start()

        for n in range(batches):
            @pl.when(i == n)
            def _(n=n):
                for run in rest[(0, 5, 8, 10)[n] : (5, 8, 10, 12)[n]]:
                    run()

    rest = rest[12:]
    loads[1].wait()

    @pl.when(busy)
    def _():
        loads[2].wait()

    @pl.loop(0, batches)
    def _(i):
        for n in range(batches):
            @pl.when(i == n)
            def _(n=n):
                for run in rest[2 * n : 2 * n + 2]:
                    run()

        for d in range(1, 8):
            @if_sends(d)
            def _(d=d):
                early(i, d).wait_recv()
                there(i, d).wait_recv()

        @pl.when(busy)
        def _():
            there_own(i).wait()

        frames = pl.ds(BATCH * i, BATCH)
        lines = SENDERS * BATCH * OWN
        branch = jnp.dot(a_in[:, frames].reshape(lines, PAD), wo_s[...], preferred_element_type=F32)
        middle = x_in[:, frames].reshape(lines, WIDTH).astype(F32) + gate_ref[0:1, :] * branch
        normed = modulated(middle.astype(BF).astype(F32), offsets, 2, 3)
        x_in[:, frames] = normed.reshape(SENDERS, BATCH, OWN, WIDTH)

    order = shuffle(False)

    @pl.loop(0, SENDERS)
    def _(s):
        got = jnp.dot(order, x_in[s].reshape(128, WIDTH), preferred_element_type=F32).astype(BF)
        xp[:, s] = got.reshape(GROUPS, 16, WIDTH)

    unpack(full_t, settle_t, wq, wo_t)

    key, row = iota((rows, PIX), 1), iota((rows, PIX), 0)
    frame = (key // 16) * 8 + key % 8
    valid = (key < rows) & (frame < total) & ((key // 8) % 2 == (row // 8) % 2)

    @pl.loop(0, GROUPS // 2)
    def _(i):
        got = jnp.dot(xp[pl.ds(2 * i, 2)].reshape(2 * rows, WIDTH), wq[...], preferred_element_type=F32)
        qkv_t[...] = got.astype(BF).reshape(2, rows, 3 * PAD)
        for u in range(2):
            mixed = attention(lambda first: qkv_t[u, :, first : first + 256], rows, valid)
            ap[:, 2 * i + u] = mixed.reshape(SENDERS, 16, PAD)
        for d in (4, 3, 5, 2, 6, 1, 7):
            @if_gets(d)
            def _(d=d):
                back(i, d).start()

        @pl.when(busy)
        def _():
            attp[sp, pl.ds(2 * i, 2)] = ap[slot, pl.ds(2 * i, 2)]

    def swap(n):
        cols = pl.ds(384 * n, 384)
        return remote(g_part.at[:, 1 - c, :, cols], r0.at[:, :, cols], s0.at[n], t0.at[n], sibling)

    def step1(n, to_x):
        cols = pl.ds(384 * n, 384)
        return remote(
            red.at[to_x, :, cols], r1.at[slot, :, cols], s1.at[n, to_x], t1.at[n, slot], (grp, 2 * to_x + c))

    def step2(d):
        to = lax.rem(grp + d, 32)
        return remote(buf.at[to], r2.at[chip], s2.at[d], t2.at[d], (to, sp))

    @pl.when(busy)
    def _():
        @pl.loop(0, SLOTS)
        def _(f):
            kept = sp * SLOTS + f < total
            branch = jnp.dot(att_s[f], wo_s[...], preferred_element_type=F32)
            mid[f] = (hid[f].astype(F32) + gate_ref[0:1, :] * branch).astype(BF)
            nrm[f] = jnp.where(kept, gate_ref[1:2, :] * cot[f].astype(F32), 0.0).astype(BF)

        @pl.loop(0, 8)
        def _(t):
            got = jnp.dot(order, nrm[:, pixels(t), :].reshape(128, WIDTH), preferred_element_type=F32)
            scp[t] = got.astype(BF).reshape(GROUPS, 16, WIDTH)

        def product(i, cols):
            pairs = pl.ds(2 * i, 2)
            return lax.dot_general(
                attp[:, pairs].reshape(2 * PIX, PAD), scp[:, pairs, :, cols].reshape(2 * PIX, 384),
                (((0,), (0,)), ((), ())), preferred_element_type=F32)

        acc[...] = jnp.zeros_like(acc)

        @pl.loop(0, GROUPS // 2 - 1)
        def _(i):
            for d in range(1, 8):
                back(i, d).wait_recv()
            for n in range(3):
                cols = slice(384 * n, 384 * n + 384)
                acc[:, cols] += product(i, cols)

        for d in range(1, 8):
            back(GROUPS // 2 - 1, d).wait_recv()

        def gradient(n):
            cols = slice(384 * n, 384 * n + 384)
            got = (acc[:, cols] + product(GROUPS // 2 - 1, cols)) * (1.0 / PIX)
            for t in range(8):
                part = jnp.concatenate([got[72 * t : 72 * t + 72], jnp.zeros((8, 384), F32)], axis=0)
                g_part[t // 2, t % 2, :, cols] = part.astype(BF)
            swap(n).start()

        def pass_on(n):
            cols = slice(384 * n, 384 * n + 384)
            swap(n).wait()
            for i in range(4):
                red[i, :, cols] = (g_part[i, c, :, cols].astype(F32) + r0[i, :, cols].astype(F32)).astype(BF)
            for i in range(4):
                @pl.when(2 * i + c != sp)
                def _(i=i):
                    step1(n, i).start()

                @pl.when(2 * i + c == sp)
                def _(i=i):
                    r1[slot, :, cols] = red[i, :, cols]

        gradient(0)
        gradient(1)
        pass_on(0)
        gradient(2)
        pass_on(1)
        pass_on(2)
        unorder = shuffle(True)

        @pl.loop(0, 8)
        def _(t):
            got = jnp.dot(unorder, attp[t].reshape(128, PAD), preferred_element_type=F32).astype(BF)
            att[:, pixels(t), :] = got.reshape(SLOTS, OWN, PAD)

        @pl.loop(0, SLOTS)
        def _(f):
            kept = sp * SLOTS + f < total
            branch = jnp.dot(att[f], wo_t[...], preferred_element_type=F32)
            out = mid[f].astype(F32) + gate_ref[1:2, :] * branch
            hid[f] = jnp.where(kept, out, 0.0).astype(BF)

    @pl.when(sp >= SENDERS)
    def _():
        hid[...] = jnp.zeros_like(hid)

    result = pltpu.make_async_copy(hid, out_ref, out_sem)
    result.start()

    @pl.when(low == c)
    def _():
        for n in range(3):
            for s in range(SENDERS):
                @pl.when(sp != s)
                def _(n=n, s=s):
                    cols = pl.ds(384 * n, 384)
                    remote(
                        red.at[0, :, cols], r1.at[s, :, cols], s1.at[n, 0], t1.at[n, s], sibling).wait_recv()

        whole = r1[0].astype(F32)
        for s in range(1, SENDERS):
            whole = whole + r1[s].astype(F32)
        whole = jnp.concatenate([whole, jnp.zeros((48, WIDTH), F32)], axis=0)
        for n in range(9):
            flipped[128 * n : 128 * n + 128] = whole[:, 128 * n : 128 * n + 128].T
        for g in range(32):
            part = jnp.concatenate([flipped[36 * g : 36 * g + 36], jnp.zeros((12, 128), F32)], axis=0)
            buf[g] = part.astype(BF)

        @pl.loop(1, 32)
        def _(d):
            step2(d).start()

        r2[chip] = buf[grp]

        @pl.loop(1, 32)
        def _(d):
            step2(d).wait_send()

    @pl.loop(1, 32)
    def _(d):
        @pl.when(lax.rem(grp + 32 - d, 2) == low)
        def _():
            step2(d).wait_recv()

    whole = r2[0].astype(F32)
    for i in range(1, 16):
        whole = whole + r2[i].astype(F32)
    grad_ref[...] = whole[:36, :HDIM]

    drain_s()
    drain_t()

    @pl.when(busy)
    def _():
        for n in range(3):
            for i in range(4):
                @pl.when(2 * i + c != sp)
                def _(n=n, i=i):
                    step1(n, i).wait_send()

        for d in range(1, 8):
            for i in range(batches):
                early(i, d).wait_send()
                there(i, d).wait_send()

    for i in range(GROUPS // 2):
        for d in range(1, 8):
            @if_gets(d)
            def _(d=d, i=i):
                back(i, d).wait_send()

    result.wait()


def on_device(
    hidden,
    frame_counts,
    shifts,
    gates,
    w_qkv_spatial,
    w_out_spatial,
    w_qkv_temporal,
    w_out_temporal,
    cotangent,
):
    frames = (SLOTS, PIX, WIDTH)
    dma = pltpu.SemaphoreType.DMA
    block_out, grad = pl.pallas_call(
        block_kernel,
        out_shape=(jax.ShapeDtypeStruct(frames, BF), jax.ShapeDtypeStruct((36, HDIM), F32)),
        in_specs=[SM, VM, VM, ANY, ANY, VM, VM, VM, VM],
        out_specs=(ANY, VM),
        scratch_shapes=[
            pltpu.VMEM((4, 4, 2, 48, PACK), BF),
            pltpu.VMEM((4, 4, 2, 48, PACK), BF),
            pltpu.VMEM((WIDTH, 3 * PAD), BF),
            pltpu.VMEM((PAD, WIDTH), BF),
            pltpu.VMEM((PAD, WIDTH), BF),
            *[pltpu.VMEM(frames, BF)] * 4,
            pltpu.VMEM((BATCH, PIX, 3 * PAD), BF),
            pltpu.VMEM((SLOTS, PIX, PAD), BF),
            pltpu.VMEM((SENDERS, SLOTS, OWN, WIDTH), BF),
            pltpu.VMEM((SENDERS, SLOTS, OWN, PAD), BF),
            pltpu.VMEM((GROUPS, SENDERS, 16, WIDTH), BF),
            pltpu.VMEM((2, SENDERS * 16, 3 * PAD), BF),
            pltpu.VMEM((SENDERS, GROUPS, 16, PAD), BF),
            pltpu.VMEM((8, GROUPS, 16, PAD), BF),
            pltpu.VMEM((SLOTS, PIX, PAD), BF),
            pltpu.VMEM((8, GROUPS, 16, WIDTH), BF),
            pltpu.VMEM((PAD, WIDTH), F32),
            pltpu.VMEM((4, 2, 80, WIDTH), BF),
            pltpu.VMEM((4, 80, WIDTH), BF),
            pltpu.VMEM((4, 80, WIDTH), BF),
            pltpu.VMEM((SENDERS, 80, WIDTH), BF),
            pltpu.VMEM((WIDTH, 128), F32),
            pltpu.VMEM((32, 48, 128), BF),
            pltpu.VMEM((16, 48, 128), BF),
            dma((COPIES,)), dma((COPIES,)), dma((COPIES,)), dma((COPIES,)),
            dma((3,)), dma((4, 8)), dma((4, 8)),
            dma((4, 8)), dma((4, 8)), dma((4,)),
            dma((4, 8)), dma((4, 8)),
            dma((3,)), dma((3,)), dma((3, 4)), dma((3, SENDERS)), dma((32,)), dma((32,)), dma,
        ],
        compiler_params=pltpu.CompilerParams(
            vmem_limit_bytes=BIG, collective_id=1, has_side_effects=True),
        name="block",
    )(
        frame_counts, shifts[0], gates[0], hidden[0], cotangent[0],
        w_qkv_spatial, w_out_spatial, w_qkv_temporal, w_out_temporal,
    )
    return block_out[None], grad


def solution(mesh):
    return jax.shard_map(
        on_device,
        mesh=mesh,
        in_specs=(
            P("grp", "sp", None, None),
            P("grp"),
            P("grp", None, None),
            P("grp", None, None),
            P("grp", None),
            P("grp", None),
            P("grp", None),
            P("grp", None),
            P("grp", "sp", None, None),
        ),
        out_specs=(P("grp", "sp", None, None), P("grp", "sp")),
        check_vma=False,
    )
```

```python
import math

import jax
import jax.numpy as jnp
from jax import lax
from jax.experimental import pallas as pl
from jax.experimental.pallas import tpu as pltpu
from jax.sharding import PartitionSpec as P

MESH = pl.DeviceIdType.MESH
BF = jnp.bfloat16
F32 = jnp.float32
HDIM = 72
WIDTH = 1152
INNER = 576
PAD = 640
PIX = 128
SLOTS = 8
OWN = 16
SENDERS = 6
PACK = 1792
SCALE = math.log2(math.e) / math.sqrt(HDIM)
BATCH = 2
GROUPS = 8
ANY = pl.BlockSpec(memory_space=pl.ANY)
VM = pl.BlockSpec(memory_space=pltpu.VMEM)
SM = pl.BlockSpec(memory_space=pltpu.SMEM)
BIG = 56 * 1024 * 1024


def pack(qkv_ref, out_ref):
    qkv, out = qkv_ref[...].astype(F32), out_ref[...].astype(F32)
    k, v = qkv[:, INNER : 2 * INNER], qkv[:, 2 * INNER :]
    top = jnp.concatenate([qkv[:, :INNER], k[:, 512:], k[:, :512], v, jnp.zeros((36, 64), F32)], axis=1)
    blank = jnp.zeros((6, 64), F32)
    side = jnp.concatenate([
        jnp.concatenate([out[12:, :INNER], blank], axis=1),
        jnp.concatenate([blank, out[12:, INNER:]], axis=1),
    ], axis=0)
    low = jnp.concatenate([out[:12], side], axis=1)
    return jnp.concatenate([top, low], axis=0).astype(BF)


STEPS = (
    ((), ("z1p", "z1q")),
    ((), ("upp0", "dnp0", "upq0", "dnq0")),
    (("z1p",), ("z2p", "upp1", "dnp1")),
    (("z1q",), ("z2q", "upq1", "dnq1")),
    (("upp0", "dnp0"), ("farp0",)),
    (("upq0", "dnq0"), ("farq0",)),
    (("z2p",), ("z3p", "upp2", "dnp2")),
    (("z2q",), ("z3q", "upq2", "dnq2")),
    (("upp1", "dnp1"), ("farp1",)),
    (("upq1", "dnq1"), ("farq1",)),
    (("z3p",), ("upp3", "dnp3")),
    (("z3q",), ("upq3", "dnq3")),
    (("farp0", "farq0"), ("s0",)),
    (("upp2", "dnp2"), ("farp2",)),
    (("upq2", "dnq2"), ("farq2",)),
    (("farp1", "farq1"), ("s1",)),
    (("upp3", "dnp3"), ("farp3",)),
    (("upq3", "dnq3"), ("farq3",)),
    (("farp2", "farq2"), ("s2",)),
    (("farp3", "farq3"), ("s3",)),
)
LATER = (
    ((), ("z1p", "z1q")),
    (("z1p",), ("z2p",)),
    (("z1q",), ("z2q",)),
    ((), ("upp0", "dnp0", "upq0", "dnq0", "upp1", "dnp1", "upq1", "dnq1")),
    (("z2p",), ("z3p", "upp2", "dnp2")),
    (("z2q",), ("z3q", "upq2", "dnq2")),
    (("upp0", "dnp0"), ("farp0",)),
    (("upq0", "dnq0"), ("farq0",)),
    (("upp1", "dnp1"), ("farp1",)),
    (("upq1", "dnq1"), ("farq1",)),
    (("farp0", "farq0"), ("s0",)),
    (("z3p",), ("upp3", "dnp3")),
    (("z3q",), ("upq3", "dnq3")),
    (("upp2", "dnp2"), ("farp2",)),
    (("upq2", "dnq2"), ("farq2",)),
    (("farp1", "farq1"), ("s1",)),
    (("farp2", "farq2"), ("s2",)),
    (("upp3", "dnp3"), ("farp3",)),
    (("upq3", "dnq3"), ("farq3",)),
    (("farp3", "farq3"), ("s3",)),
)


def gather_plan(full, ssem, rsem, order):
    grp, sp = lax.axis_index("grp"), lax.axis_index("sp")
    h, y, c = grp // 8, (grp // 2) % 4, grp % 2
    low = sp % 2
    up, down = lax.rem(y + 1, 4), lax.rem(y + 3, 4)
    hx = lax.rem(h + 3 + 2 * low, 4)
    hp = lax.rem(h + 5 - 2 * low, 4)
    hf = lax.rem(h + 2, 4)
    sibling = (grp + 1 - 2 * c, sp)
    y_up = ((h * 4 + up) * 2 + c, sp)
    y_down = ((h * 4 + down) * 2 + c, sp)
    pair = (grp, sp + 1 - 2 * low)
    cross = (hx * 8 + y * 2 + c, sp + 1 - 2 * low)
    al = slice(None)
    hs = (h, hx, hp, hf)
    table = {}

    def add(name, where, who):
        table[name] = (len(table), where, who)

    for stream, cols in (("p", pl.ds(0, PACK // 2)), ("q", pl.ds(PACK // 2, PACK // 2))):
        add("z1" + stream, (h, y, c, al, cols), cross)
        add("z2" + stream, (hx, y, c, al, cols), pair)
        add("z3" + stream, (hp, y, c, al, cols), cross)
        for k in range(4):
            add(f"up{stream}{k}", (hs[k], y, c, al, cols), y_up)
            add(f"dn{stream}{k}", (hs[k], y, c, al, cols), y_down)
            if stream == "p":
                add(f"farp{k}", (hs[k], down, c, al, cols), y_up)
            else:
                add(f"farq{k}", (hs[k], up, c, al, cols), y_down)
    for k in range(4):
        add(f"s{k}", (hs[k], al, c), sibling)

    def copy(name):
        i, where, who = table[name]
        return pltpu.make_async_remote_copy(
            src_ref=full.at[where], dst_ref=full.at[where], send_sem=ssem.at[i], recv_sem=rsem.at[i],
            device_id=who, device_id_type=MESH)

    def step(waits, starts):
        def run():
            for name in waits:
                copy(name).wait_recv()
            for name in starts:
                copy(name).start()
        return run

    def settle(k):
        copy(f"s{k}").wait_recv()
        return hs[k]

    def drain():
        for name in table:
            copy(name).wait_send()

    return [step(*both) for both in order], settle, drain, (h, y, c), [sibling, y_up, y_down, cross]


COPIES = 34


def iota(shape, dim):
    return lax.broadcasted_iota(jnp.int32, shape, dim)


def picks(condition):
    return condition.astype(F32).astype(BF)


def unpack(full, settle, wq, wo):
    col, row = iota((144, 192), 1), iota((144, 192), 0)
    of, at = col // 48, col % 48
    top = picks((at < 36) & (36 * of + at == row))
    col, row = iota((72, 192), 1), iota((72, 192), 0)
    of, at = col // 48, col % 48 - 36
    main = picks((at >= 0) & (18 * of + at == row) & (at < 12))
    left = picks((at >= 0) & (at < 6) & (18 * of + 12 + at == row))
    right = picks((at >= 6) & (18 * of + 6 + at == row))
    keep = iota((144, 128), 1) < 64

    wo[INNER:, :] = jnp.zeros((PAD - INNER, WIDTH), BF)
    for k in range(4):
        h = settle(k)
        outs = []
        for i in range(2):
            block = full[h, 2 * i : 2 * i + 2].reshape(192, PACK)
            got = jnp.dot(top, block, preferred_element_type=F32)
            rows = pl.ds(pl.multiple_of((2 * h + i) * 144, 16), 144)
            mixed = got[:, 512:640]
            turned = jnp.concatenate([mixed[:, 64:], mixed[:, :64]], axis=1)
            wq[rows, 0:512] = got[:, 0:512].astype(BF)
            wq[rows, 512:640] = jnp.where(keep, mixed, 0.0).astype(BF)
            wq[rows, 640:1152] = got[:, 640:1152].astype(BF)
            wq[rows, 1152:1280] = jnp.where(keep, turned, 0.0).astype(BF)
            wq[rows, 1280:1920] = got[:, 1152:1792].astype(BF)
            whole = jnp.dot(main, block[:, :WIDTH], preferred_element_type=F32)
            side = block[:, WIDTH:]
            one = jnp.dot(left, side, preferred_element_type=F32)
            two = jnp.dot(right, side, preferred_element_type=F32)
            blank = jnp.zeros((72, 512), F32)
            outs.append(whole + jnp.concatenate([one, blank], axis=1) + jnp.concatenate([blank, two], axis=1))
        wo[pl.ds(pl.multiple_of(144 * h, 16), 144), :] = jnp.concatenate(outs, axis=0).astype(BF)


def modulated(x, offsets, shift_row, scale_row):
    mean = jnp.sum(x, axis=-1, keepdims=True) * (1.0 / WIDTH)
    x = x - mean
    spread = jnp.sum(x * x, axis=-1, keepdims=True) * (1.0 / WIDTH)
    x = x * lax.rsqrt(spread + 1e-06)
    return (x * (1.0 + offsets[scale_row]) + offsets[shift_row]).astype(BF)


def head_masks(j):
    lane = iota((1, 256), 1)
    start = 16 * j
    one = picks((lane >= start) & (lane < start + HDIM))
    two = picks((lane >= start + HDIM) & (lane < start + 2 * HDIM))
    return one, two


def attention(load, keys, valid):
    blocks = [None] * 5
    fill = [] if keys == PIX else [jnp.zeros((PIX - keys, 256), BF)]
    for j in range(4):
        one, two = head_masks(j)
        q, k, v = (load(part * PAD + 128 * j) for part in range(3))
        kk = jnp.concatenate([k * one, *fill, k * two, *fill], axis=0)
        vv = jnp.concatenate([v * one, *fill, v * two, *fill], axis=0)
        heads = jnp.concatenate(
            [jnp.broadcast_to(one, (PIX, 256)), jnp.broadcast_to(two, (PIX, 256))], axis=0)
        s = lax.dot_general(q, kk, (((1,), (1,)), ((), ())), preferred_element_type=F32)
        expo = []
        for part in (s[:, :128], s[:, 128:]):
            if valid is not None:
                part = jnp.where(valid, part, -1e30)
            top = jnp.max(part, axis=-1, keepdims=True)
            expo.append(jnp.exp2((part - top) * SCALE).astype(BF))
        expo = jnp.concatenate(expo, axis=1)
        o = jnp.dot(expo, vv, preferred_element_type=F32)
        total = jnp.dot(expo, heads, preferred_element_type=F32)
        o = o * (1.0 / jnp.where(total == 0.0, 1.0, total))
        for i, piece in ((j, o[:, :128]), (j + 1, o[:, 128:])):
            blocks[i] = piece if blocks[i] is None else blocks[i] + piece
    return jnp.concatenate(blocks, axis=1).astype(BF)


def shuffle(back):
    there, here = iota((128, 128), 1 if back else 0), iota((128, 128), 0 if back else 1)
    return picks(here == (there % 8) * OWN + there // 8)


def block_kernel(
    total_ref, shift_ref, gate_ref, hidden_ref, cot_in_ref, w1_ref, w2_ref, w3_ref, w4_ref,
    out_ref, grad_ref,
    full_s, full_t, wq, wo_s, wo_t, hid, nrm, mid, cot, qkv, att_s, x_in, a_in, xp, qkv_t, ap, attp, att,
    scp, acc, g_part, r0, red, r1, flipped, buf, r2,
    gs_s, gr_s, gs_t, gr_t, load_sem, early_s, early_r, there_s, there_r, there_l, back_s, back_r,
    s0, t0, s1, t1, s2, t2, out_sem,
):
    grp, sp = lax.axis_index("grp"), lax.axis_index("sp")
    c, low, chip = grp % 2, sp % 2, grp // 2
    sibling = (grp + 1 - 2 * c, sp)
    slot = lax.rem(sp, SENDERS)
    busy = sp < SENDERS
    offsets = [shift_ref[i : i + 1, :] for i in range(4)]
    total = total_ref[0]
    rows = SENDERS * 16
    batches = SLOTS // BATCH

    def from_me(d):
        return lax.rem(sp + d, 8)

    def pixels(rank):
        return pl.ds(pl.multiple_of(rank * OWN, OWN), OWN)

    def if_sends(d):
        return pl.when(lax.rem(sp + 8 - d, 8) < SENDERS)

    def if_gets(d):
        return pl.when(from_me(d) < SENDERS)

    def remote(src, dst, send_sem, recv_sem, who):
        return pltpu.make_async_remote_copy(
            src_ref=src, dst_ref=dst, send_sem=send_sem, recv_sem=recv_sem,
            device_id=who, device_id_type=MESH)

    def early(i, d):
        to, frames = from_me(d), pl.ds(BATCH * i, BATCH)
        return remote(
            hidden_ref.at[frames, pixels(to), :], x_in.at[slot, frames], early_s.at[i, d], early_r.at[i, d], (grp, to))

    def there(i, d):
        to, frames = from_me(d), pl.ds(BATCH * i, BATCH)
        return remote(
            att_s.at[frames, pixels(to), :], a_in.at[slot, frames], there_s.at[i, d], there_r.at[i, d], (grp, to))

    def there_own(i):
        frames = pl.ds(BATCH * i, BATCH)
        return pltpu.make_async_copy(att_s.at[frames, pixels(sp), :], a_in.at[slot, frames], there_l.at[i])

    def back(g, d):
        to = from_me(d)
        return remote(
            ap.at[lax.rem(to, SENDERS), g], attp.at[sp, g], back_s.at[g, d], back_r.at[g, d], (grp, to))

    steps_s, settle_s, drain_s, here, neighbours = gather_plan(full_s, gs_s, gr_s, STEPS)
    steps_t, settle_t, drain_t, _, _ = gather_plan(full_t, gs_t, gr_t, LATER)
    loads = [
        pltpu.make_async_copy(hidden_ref, hid, load_sem.at[0]),
        pltpu.make_async_copy(cot_in_ref, cot, load_sem.at[1]),
        pltpu.make_async_copy(hidden_ref.at[:, pixels(sp), :], x_in.at[slot], load_sem.at[2]),
    ]
    loads[0].start()
    loads[1].start()

    @pl.when(busy)
    def _():
        loads[2].start()

    partners = neighbours + [(grp, from_me(d)) for d in range(1, 8)]
    barrier = pltpu.get_barrier_semaphore()
    for who in partners:
        pl.semaphore_signal(barrier, inc=1, device_id=who, device_id_type=MESH)
    full_s[here] = pack(w1_ref, w2_ref)
    pl.semaphore_wait(barrier, len(partners))
    steps_s[0]()
    steps_s[1]()

    @pl.when(busy)
    def _():
        for d in (3, 5, 1, 7):
            early(0, d).start()
        for i in range(batches):
            for d in (4, 2, 6):
                early(i, d).start()

    full_t[here] = pack(w3_ref, w4_ref)
    loads[0].wait()

    @pl.loop(0, SLOTS)
    def _(f):
        @pl.when(busy)
        def _():
            nrm[f] = modulated(hid[f].astype(F32), offsets, 0, 1)

        for i in range(SLOTS):
            @pl.when(f == i)
            def _(i=i):
                steps_s[2 + i]()

        @pl.when((f == 5) & busy)
        def _():
            @pl.loop(1, batches)
            def _(i):
                for d in (3, 5, 1, 7):
                    early(i, d).start()

    for run in steps_s[10:12] + steps_t[0:1] + steps_s[12:16] + steps_t[1:3] + steps_s[16:18] + steps_t[3:4]:
        run()
    for run in steps_s[18:]:
        run()
    unpack(full_s, settle_s, wq, wo_s)
    for run in steps_t[4:8]:
        run()

    @pl.loop(0, batches)
    def _(i):
        @pl.when(busy)
        def _():
            tokens = nrm[pl.ds(BATCH * i, BATCH)].reshape(BATCH * PIX, WIDTH)
            got = jnp.dot(tokens, wq[...], preferred_element_type=F32)
            qkv[...] = got.astype(BF).reshape(BATCH, PIX, 3 * PAD)
            for u in range(BATCH):
                att_s[BATCH * i + u] = attention(lambda first: qkv[u, :, first : first + 256], PIX, None)
            for d in (4, 3, 5, 2, 6, 1, 7):
                there(i, d).start()
            there_own(i).start()

        for n in range(batches):
            @pl.when(i == n)
            def _(n=n):
                for run in steps_t[(8, 11, 13, 16)[n] : (11, 13, 16, 17)[n]]:
                    run()

    loads[1].wait()

    @pl.when(busy)
    def _():
        loads[2].wait()

    @pl.loop(0, batches)
    def _(i):
        for n in range(batches):
            @pl.when(i == n)
            def _(n=n):
                for run in steps_t[(17, 19, 20, 20)[n] : (19, 20, 20, 20)[n]]:
                    run()

        @pl.when(busy)
        def _():
            for u in range(BATCH):
                f = BATCH * i + u
                kept = sp * SLOTS + f < total
                branch = jnp.dot(att_s[f], wo_s[...], preferred_element_type=F32)
                mid[f] = (hid[f].astype(F32) + gate_ref[0:1, :] * branch).astype(BF)
                nrm[f] = jnp.where(kept, gate_ref[1:2, :] * cot[f].astype(F32), 0.0).astype(BF)

        for d in range(1, 8):
            @if_sends(d)
            def _(d=d):
                early(i, d).wait_recv()
                there(i, d).wait_recv()

        @pl.when(busy)
        def _():
            there_own(i).wait()

        frames = pl.ds(BATCH * i, BATCH)
        lines = SENDERS * BATCH * OWN
        branch = jnp.dot(a_in[:, frames].reshape(lines, PAD), wo_s[...], preferred_element_type=F32)
        middle = x_in[:, frames].reshape(lines, WIDTH).astype(F32) + gate_ref[0:1, :] * branch
        normed = modulated(middle.astype(BF).astype(F32), offsets, 2, 3)
        x_in[:, frames] = normed.reshape(SENDERS, BATCH, OWN, WIDTH)

    order = shuffle(False)

    @pl.loop(0, SENDERS)
    def _(s):
        got = jnp.dot(order, x_in[s].reshape(128, WIDTH), preferred_element_type=F32).astype(BF)
        xp[:, s] = got.reshape(GROUPS, 16, WIDTH)

    @pl.when(busy)
    def _():
        @pl.loop(0, 8)
        def _(t):
            got = jnp.dot(order, nrm[:, pixels(t), :].reshape(128, WIDTH), preferred_element_type=F32)
            scp[t] = got.astype(BF).reshape(GROUPS, 16, WIDTH)

        acc[...] = jnp.zeros_like(acc)

    unpack(full_t, settle_t, wq, wo_t)

    key, row = iota((rows, PIX), 1), iota((rows, PIX), 0)
    frame = (key // 16) * 8 + key % 8
    valid = (key < rows) & (frame < total) & ((key // 8) % 2 == (row // 8) % 2)

    @pl.loop(0, GROUPS // 2)
    def _(i):
        got = jnp.dot(xp[pl.ds(2 * i, 2)].reshape(2 * rows, WIDTH), wq[...], preferred_element_type=F32)
        qkv_t[...] = got.astype(BF).reshape(2, rows, 3 * PAD)
        for u in range(2):
            mixed = attention(lambda first: qkv_t[u, :, first : first + 256], rows, valid)
            ap[:, 2 * i + u] = mixed.reshape(SENDERS, 16, PAD)
            for d in (4, 3, 5, 2, 6, 1, 7):
                @if_gets(d)
                def _(d=d, u=u):
                    back(2 * i + u, d).start()

        @pl.when(busy)
        def _():
            attp[sp, pl.ds(2 * i, 2)] = ap[slot, pl.ds(2 * i, 2)]

    def swap(n):
        cols = pl.ds(384 * n, 384)
        return remote(g_part.at[:, 1 - c, :, cols], r0.at[:, :, cols], s0.at[n], t0.at[n], sibling)

    def step1(n, to_x):
        cols = pl.ds(384 * n, 384)
        return remote(
            red.at[to_x, :, cols], r1.at[slot, :, cols], s1.at[n, to_x], t1.at[n, slot], (grp, 2 * to_x + c))

    def step2(d):
        to = lax.rem(grp + d, 32)
        return remote(buf.at[to], r2.at[chip], s2.at[d], t2.at[d], (to, sp))

    @pl.when(busy)
    def _():
        def product(i, cols):
            pairs = pl.ds(2 * i, 2)
            return lax.dot_general(
                attp[:, pairs].reshape(2 * PIX, PAD), scp[:, pairs, :, cols].reshape(2 * PIX, 384),
                (((0,), (0,)), ((), ())), preferred_element_type=F32)

        @pl.loop(0, GROUPS // 2 - 1)
        def _(i):
            for d in range(1, 8):
                back(2 * i, d).wait_recv()
                back(2 * i + 1, d).wait_recv()
            for n in range(3):
                cols = slice(384 * n, 384 * n + 384)
                acc[:, cols] += product(i, cols)

        for d in range(1, 8):
            back(GROUPS - 2, d).wait_recv()
            back(GROUPS - 1, d).wait_recv()

        def gradient(n):
            cols = slice(384 * n, 384 * n + 384)
            got = (acc[:, cols] + product(GROUPS // 2 - 1, cols)) * (1.0 / PIX)
            for t in range(8):
                part = jnp.concatenate([got[72 * t : 72 * t + 72], jnp.zeros((8, 384), F32)], axis=0)
                g_part[t // 2, t % 2, :, cols] = part.astype(BF)
            swap(n).start()

        def pass_on(n):
            cols = slice(384 * n, 384 * n + 384)
            swap(n).wait()
            for i in range(4):
                red[i, :, cols] = (g_part[i, c, :, cols].astype(F32) + r0[i, :, cols].astype(F32)).astype(BF)
            for i in range(4):
                @pl.when(2 * i + c != sp)
                def _(i=i):
                    step1(n, i).start()

                @pl.when(2 * i + c == sp)
                def _(i=i):
                    r1[slot, :, cols] = red[i, :, cols]

        gradient(0)
        gradient(1)
        pass_on(0)
        gradient(2)
        pass_on(1)
        pass_on(2)
        unorder = shuffle(True)

        @pl.loop(0, 8)
        def _(t):
            got = jnp.dot(unorder, attp[t].reshape(128, PAD), preferred_element_type=F32).astype(BF)
            att[:, pixels(t), :] = got.reshape(SLOTS, OWN, PAD)

        @pl.loop(0, SLOTS)
        def _(f):
            kept = sp * SLOTS + f < total
            branch = jnp.dot(att[f], wo_t[...], preferred_element_type=F32)
            out = mid[f].astype(F32) + gate_ref[1:2, :] * branch
            hid[f] = jnp.where(kept, out, 0.0).astype(BF)

    @pl.when(sp >= SENDERS)
    def _():
        hid[...] = jnp.zeros_like(hid)

    result = pltpu.make_async_copy(hid, out_ref, out_sem)
    result.start()

    @pl.when(low == c)
    def _():
        for n in range(3):
            for s in range(SENDERS):
                @pl.when(sp != s)
                def _(n=n, s=s):
                    cols = pl.ds(384 * n, 384)
                    remote(
                        red.at[0, :, cols], r1.at[s, :, cols], s1.at[n, 0], t1.at[n, s], sibling).wait_recv()

        whole = r1[0].astype(F32)
        for s in range(1, SENDERS):
            whole = whole + r1[s].astype(F32)
        whole = jnp.concatenate([whole, jnp.zeros((48, WIDTH), F32)], axis=0)
        for n in range(9):
            flipped[128 * n : 128 * n + 128] = whole[:, 128 * n : 128 * n + 128].T
        for g in range(32):
            part = jnp.concatenate([flipped[36 * g : 36 * g + 36], jnp.zeros((12, 128), F32)], axis=0)
            buf[g] = part.astype(BF)

        @pl.loop(1, 32)
        def _(d):
            step2(d).start()

        r2[chip] = buf[grp]

        @pl.loop(1, 32)
        def _(d):
            step2(d).wait_send()

    @pl.loop(1, 32)
    def _(d):
        @pl.when(lax.rem(grp + 32 - d, 2) == low)
        def _():
            step2(d).wait_recv()

    whole = r2[0].astype(F32)
    for i in range(1, 16):
        whole = whole + r2[i].astype(F32)
    grad_ref[...] = whole[:36, :HDIM]

    drain_s()
    drain_t()

    @pl.when(busy)
    def _():
        for n in range(3):
            for i in range(4):
                @pl.when(2 * i + c != sp)
                def _(n=n, i=i):
                    step1(n, i).wait_send()

        for d in range(1, 8):
            for i in range(batches):
                early(i, d).wait_send()
                there(i, d).wait_send()

    for g in range(GROUPS):
        for d in range(1, 8):
            @if_gets(d)
            def _(d=d, g=g):
                back(g, d).wait_send()

    result.wait()


def on_device(
    hidden,
    frame_counts,
    shifts,
    gates,
    w_qkv_spatial,
    w_out_spatial,
    w_qkv_temporal,
    w_out_temporal,
    cotangent,
):
    frames = (SLOTS, PIX, WIDTH)
    dma = pltpu.SemaphoreType.DMA
    block_out, grad = pl.pallas_call(
        block_kernel,
        out_shape=(jax.ShapeDtypeStruct(frames, BF), jax.ShapeDtypeStruct((36, HDIM), F32)),
        in_specs=[SM, VM, VM, ANY, ANY, VM, VM, VM, VM],
        out_specs=(ANY, VM),
        scratch_shapes=[
            pltpu.VMEM((4, 4, 2, 48, PACK), BF),
            pltpu.VMEM((4, 4, 2, 48, PACK), BF),
            pltpu.VMEM((WIDTH, 3 * PAD), BF),
            pltpu.VMEM((PAD, WIDTH), BF),
            pltpu.VMEM((PAD, WIDTH), BF),
            *[pltpu.VMEM(frames, BF)] * 4,
            pltpu.VMEM((BATCH, PIX, 3 * PAD), BF),
            pltpu.VMEM((SLOTS, PIX, PAD), BF),
            pltpu.VMEM((SENDERS, SLOTS, OWN, WIDTH), BF),
            pltpu.VMEM((SENDERS, SLOTS, OWN, PAD), BF),
            pltpu.VMEM((GROUPS, SENDERS, 16, WIDTH), BF),
            pltpu.VMEM((2, SENDERS * 16, 3 * PAD), BF),
            pltpu.VMEM((SENDERS, GROUPS, 16, PAD), BF),
            pltpu.VMEM((8, GROUPS, 16, PAD), BF),
            pltpu.VMEM((SLOTS, PIX, PAD), BF),
            pltpu.VMEM((8, GROUPS, 16, WIDTH), BF),
            pltpu.VMEM((PAD, WIDTH), F32),
            pltpu.VMEM((4, 2, 80, WIDTH), BF),
            pltpu.VMEM((4, 80, WIDTH), BF),
            pltpu.VMEM((4, 80, WIDTH), BF),
            pltpu.VMEM((SENDERS, 80, WIDTH), BF),
            pltpu.VMEM((WIDTH, 128), F32),
            pltpu.VMEM((32, 48, 128), BF),
            pltpu.VMEM((16, 48, 128), BF),
            dma((COPIES,)), dma((COPIES,)), dma((COPIES,)), dma((COPIES,)),
            dma((3,)), dma((4, 8)), dma((4, 8)),
            dma((4, 8)), dma((4, 8)), dma((4,)),
            dma((8, 8)), dma((8, 8)),
            dma((3,)), dma((3,)), dma((3, 4)), dma((3, SENDERS)), dma((32,)), dma((32,)), dma,
        ],
        compiler_params=pltpu.CompilerParams(
            vmem_limit_bytes=BIG, collective_id=1, has_side_effects=True),
        name="block",
    )(
        frame_counts, shifts[0], gates[0], hidden[0], cotangent[0],
        w_qkv_spatial, w_out_spatial, w_qkv_temporal, w_out_temporal,
    )
    return block_out[None], grad


def solution(mesh):
    return jax.shard_map(
        on_device,
        mesh=mesh,
        in_specs=(
            P("grp", "sp", None, None),
            P("grp"),
            P("grp", None, None),
            P("grp", None, None),
            P("grp", None),
            P("grp", None),
            P("grp", None),
            P("grp", None),
            P("grp", "sp", None, None),
        ),
        out_specs=(P("grp", "sp", None, None), P("grp", "sp")),
        check_vma=False,
    )
```

```python
import math

import jax
import jax.numpy as jnp
from jax import lax
from jax.experimental import pallas as pl
from jax.experimental.pallas import tpu as pltpu
from jax.sharding import PartitionSpec as P

MESH = pl.DeviceIdType.MESH
BF = jnp.bfloat16
F32 = jnp.float32
HDIM = 72
WIDTH = 1152
INNER = 576
PAD = 640
PIX = 128
SLOTS = 8
OWN = 16
SENDERS = 6
PACK = 1792
SCALE = math.log2(math.e) / math.sqrt(HDIM)
BATCH = 2
GROUPS = 8
ANY = pl.BlockSpec(memory_space=pl.ANY)
VM = pl.BlockSpec(memory_space=pltpu.VMEM)
SM = pl.BlockSpec(memory_space=pltpu.SMEM)
BIG = 56 * 1024 * 1024


def pack(qkv_ref, out_ref):
    qkv, out = qkv_ref[...].astype(F32), out_ref[...].astype(F32)
    k, v = qkv[:, INNER : 2 * INNER], qkv[:, 2 * INNER :]
    top = jnp.concatenate([qkv[:, :INNER], k[:, 512:], k[:, :512], v, jnp.zeros((36, 64), F32)], axis=1)
    blank = jnp.zeros((6, 64), F32)
    side = jnp.concatenate([
        jnp.concatenate([out[12:, :INNER], blank], axis=1),
        jnp.concatenate([blank, out[12:, INNER:]], axis=1),
    ], axis=0)
    low = jnp.concatenate([out[:12], side], axis=1)
    return jnp.concatenate([top, low], axis=0).astype(BF)


STEPS = (
    ((), ("z1p", "z1q")),
    ((), ("upp0", "dnp0", "upq0", "dnq0")),
    (("z1p",), ("z2p", "upp1", "dnp1")),
    (("z1q",), ("z2q", "upq1", "dnq1")),
    (("upp0", "dnp0"), ("farp0",)),
    (("upq0", "dnq0"), ("farq0",)),
    (("z2p",), ("z3p", "upp2", "dnp2")),
    (("z2q",), ("z3q", "upq2", "dnq2")),
    (("upp1", "dnp1"), ("farp1",)),
    (("upq1", "dnq1"), ("farq1",)),
    (("z3p",), ("upp3", "dnp3")),
    (("z3q",), ("upq3", "dnq3")),
    (("farp0", "farq0"), ("s0",)),
    (("upp2", "dnp2"), ("farp2",)),
    (("upq2", "dnq2"), ("farq2",)),
    (("farp1", "farq1"), ("s1",)),
    (("upp3", "dnp3"), ("farp3",)),
    (("upq3", "dnq3"), ("farq3",)),
    (("farp2", "farq2"), ("s2",)),
    (("farp3", "farq3"), ("s3",)),
)
LATER = (
    ((), ("z1p", "z1q")),
    (("z1p",), ("z2p",)),
    (("z1q",), ("z2q",)),
    (("z2p",), ("z3p",)),
    (("z2q",), ("z3q",)),
    ((), ("upp0", "dnp0", "upq0", "dnq0", "upp1", "dnp1", "upq1", "dnq1", "upp2", "dnp2", "upq2", "dnq2")),
    (("z3p", "z3q"), ("upp3", "dnp3", "upq3", "dnq3")),
    (("upp0", "dnp0"), ("farp0",)),
    (("upq0", "dnq0"), ("farq0",)),
    (("upp1", "dnp1"), ("farp1",)),
    (("upq1", "dnq1"), ("farq1",)),
    (("farp0", "farq0"), ("s0",)),
    (("upp2", "dnp2"), ("farp2",)),
    (("upq2", "dnq2"), ("farq2",)),
    (("farp1", "farq1"), ("s1",)),
    (("upp3", "dnp3"), ("farp3",)),
    (("upq3", "dnq3"), ("farq3",)),
    (("farp2", "farq2"), ("s2",)),
    (("farp3", "farq3"), ("s3",)),
)


def gather_plan(full, ssem, rsem, order):
    grp, sp = lax.axis_index("grp"), lax.axis_index("sp")
    h, y, c = grp // 8, (grp // 2) % 4, grp % 2
    low = sp % 2
    up, down = lax.rem(y + 1, 4), lax.rem(y + 3, 4)
    hx = lax.rem(h + 3 + 2 * low, 4)
    hp = lax.rem(h + 5 - 2 * low, 4)
    hf = lax.rem(h + 2, 4)
    sibling = (grp + 1 - 2 * c, sp)
    y_up = ((h * 4 + up) * 2 + c, sp)
    y_down = ((h * 4 + down) * 2 + c, sp)
    pair = (grp, sp + 1 - 2 * low)
    cross = (hx * 8 + y * 2 + c, sp + 1 - 2 * low)
    al = slice(None)
    hs = (h, hx, hp, hf)
    table = {}

    def add(name, where, who):
        table[name] = (len(table), where, who)

    for stream, cols in (("p", pl.ds(0, PACK // 2)), ("q", pl.ds(PACK // 2, PACK // 2))):
        add("z1" + stream, (h, y, c, al, cols), cross)
        add("z2" + stream, (hx, y, c, al, cols), pair)
        add("z3" + stream, (hp, y, c, al, cols), cross)
        for k in range(4):
            add(f"up{stream}{k}", (hs[k], y, c, al, cols), y_up)
            add(f"dn{stream}{k}", (hs[k], y, c, al, cols), y_down)
            if stream == "p":
                add(f"farp{k}", (hs[k], down, c, al, cols), y_up)
            else:
                add(f"farq{k}", (hs[k], up, c, al, cols), y_down)
    for k in range(4):
        add(f"s{k}", (hs[k], al, c), sibling)

    def copy(name):
        i, where, who = table[name]
        return pltpu.make_async_remote_copy(
            src_ref=full.at[where], dst_ref=full.at[where], send_sem=ssem.at[i], recv_sem=rsem.at[i],
            device_id=who, device_id_type=MESH)

    def step(waits, starts):
        def run():
            for name in waits:
                copy(name).wait_recv()
            for name in starts:
                copy(name).start()
        return run

    def settle(k):
        copy(f"s{k}").wait_recv()
        return hs[k]

    def drain():
        for name in table:
            copy(name).wait_send()

    return [step(*both) for both in order], settle, drain, (h, y, c), [sibling, y_up, y_down, cross]


COPIES = 34


def iota(shape, dim):
    return lax.broadcasted_iota(jnp.int32, shape, dim)


def picks(condition):
    return condition.astype(F32).astype(BF)


def unpack(full, settle, wq, wo):
    col, row = iota((144, 192), 1), iota((144, 192), 0)
    of, at = col // 48, col % 48
    top = picks((at < 36) & (36 * of + at == row))
    col, row = iota((72, 192), 1), iota((72, 192), 0)
    of, at = col // 48, col % 48 - 36
    main = picks((at >= 0) & (18 * of + at == row) & (at < 12))
    left = picks((at >= 0) & (at < 6) & (18 * of + 12 + at == row))
    right = picks((at >= 6) & (18 * of + 6 + at == row))
    keep = iota((144, 128), 1) < 64

    wo[INNER:, :] = jnp.zeros((PAD - INNER, WIDTH), BF)
    for k in range(4):
        h = settle(k)
        outs = []
        for i in range(2):
            block = full[h, 2 * i : 2 * i + 2].reshape(192, PACK)
            got = jnp.dot(top, block, preferred_element_type=F32)
            rows = pl.ds(pl.multiple_of((2 * h + i) * 144, 16), 144)
            mixed = got[:, 512:640]
            turned = jnp.concatenate([mixed[:, 64:], mixed[:, :64]], axis=1)
            wq[rows, 0:512] = got[:, 0:512].astype(BF)
            wq[rows, 512:640] = jnp.where(keep, mixed, 0.0).astype(BF)
            wq[rows, 640:1152] = got[:, 640:1152].astype(BF)
            wq[rows, 1152:1280] = jnp.where(keep, turned, 0.0).astype(BF)
            wq[rows, 1280:1920] = got[:, 1152:1792].astype(BF)
            whole = jnp.dot(main, block[:, :WIDTH], preferred_element_type=F32)
            side = block[:, WIDTH:]
            one = jnp.dot(left, side, preferred_element_type=F32)
            two = jnp.dot(right, side, preferred_element_type=F32)
            blank = jnp.zeros((72, 512), F32)
            outs.append(whole + jnp.concatenate([one, blank], axis=1) + jnp.concatenate([blank, two], axis=1))
        wo[pl.ds(pl.multiple_of(144 * h, 16), 144), :] = jnp.concatenate(outs, axis=0).astype(BF)


def modulated(x, offsets, shift_row, scale_row):
    mean = jnp.sum(x, axis=-1, keepdims=True) * (1.0 / WIDTH)
    x = x - mean
    spread = jnp.sum(x * x, axis=-1, keepdims=True) * (1.0 / WIDTH)
    x = x * lax.rsqrt(spread + 1e-06)
    return (x * (1.0 + offsets[scale_row]) + offsets[shift_row]).astype(BF)


def head_masks(j):
    lane = iota((1, 256), 1)
    start = 16 * j
    one = picks((lane >= start) & (lane < start + HDIM))
    two = picks((lane >= start + HDIM) & (lane < start + 2 * HDIM))
    return one, two


def attention(load, keys, valid):
    blocks = [None] * 5
    fill = [] if keys == PIX else [jnp.zeros((PIX - keys, 256), BF)]
    for j in range(4):
        one, two = head_masks(j)
        q, k, v = (load(part * PAD + 128 * j) for part in range(3))
        kk = jnp.concatenate([k * one, *fill, k * two, *fill], axis=0)
        vv = jnp.concatenate([v * one, *fill, v * two, *fill], axis=0)
        heads = jnp.concatenate(
            [jnp.broadcast_to(one, (PIX, 256)), jnp.broadcast_to(two, (PIX, 256))], axis=0)
        s = lax.dot_general(q, kk, (((1,), (1,)), ((), ())), preferred_element_type=F32)
        expo = []
        for part in (s[:, :128], s[:, 128:]):
            if valid is not None:
                part = jnp.where(valid, part, -1e30)
            top = jnp.max(part, axis=-1, keepdims=True)
            expo.append(jnp.exp2((part - top) * SCALE).astype(BF))
        expo = jnp.concatenate(expo, axis=1)
        o = jnp.dot(expo, vv, preferred_element_type=F32)
        total = jnp.dot(expo, heads, preferred_element_type=F32)
        o = o * (1.0 / jnp.where(total == 0.0, 1.0, total))
        for i, piece in ((j, o[:, :128]), (j + 1, o[:, 128:])):
            blocks[i] = piece if blocks[i] is None else blocks[i] + piece
    return jnp.concatenate(blocks, axis=1).astype(BF)


def shuffle(back):
    there, here = iota((128, 128), 1 if back else 0), iota((128, 128), 0 if back else 1)
    return picks(here == (there % 8) * OWN + there // 8)


def block_kernel(
    total_ref, shift_ref, gate_ref, hidden_ref, cot_in_ref, w1_ref, w2_ref, w3_ref, w4_ref,
    out_ref, grad_ref,
    full_s, full_t, wq, wo_s, wo_t, hid, nrm, mid, cot, qkv, att_s, x_in, a_in, xp, qkv_t, ap, attp, att,
    scp, acc, g_part, r0, red, r1, flipped, buf, r2,
    gs_s, gr_s, gs_t, gr_t, load_sem, early_s, early_r, there_s, there_r, there_l, back_s, back_r,
    s0, t0, s1, t1, s2, t2, out_sem,
):
    grp, sp = lax.axis_index("grp"), lax.axis_index("sp")
    c, low, chip = grp % 2, sp % 2, grp // 2
    sibling = (grp + 1 - 2 * c, sp)
    slot = lax.rem(sp, SENDERS)
    busy = sp < SENDERS
    offsets = [shift_ref[i : i + 1, :] for i in range(4)]
    total = total_ref[0]
    rows = SENDERS * 16
    batches = SLOTS // BATCH

    def from_me(d):
        return lax.rem(sp + d, 8)

    def pixels(rank):
        return pl.ds(pl.multiple_of(rank * OWN, OWN), OWN)

    def if_sends(d):
        return pl.when(lax.rem(sp + 8 - d, 8) < SENDERS)

    def if_gets(d):
        return pl.when(from_me(d) < SENDERS)

    def remote(src, dst, send_sem, recv_sem, who):
        return pltpu.make_async_remote_copy(
            src_ref=src, dst_ref=dst, send_sem=send_sem, recv_sem=recv_sem,
            device_id=who, device_id_type=MESH)

    def early(i, d):
        to, frames = from_me(d), pl.ds(BATCH * i, BATCH)
        return remote(
            hidden_ref.at[frames, pixels(to), :], x_in.at[slot, frames], early_s.at[i, d], early_r.at[i, d], (grp, to))

    def there(i, d):
        to, frames = from_me(d), pl.ds(BATCH * i, BATCH)
        return remote(
            att_s.at[frames, pixels(to), :], a_in.at[slot, frames], there_s.at[i, d], there_r.at[i, d], (grp, to))

    def there_own(i):
        frames = pl.ds(BATCH * i, BATCH)
        return pltpu.make_async_copy(att_s.at[frames, pixels(sp), :], a_in.at[slot, frames], there_l.at[i])

    def back(g, d):
        to = from_me(d)
        return remote(
            ap.at[lax.rem(to, SENDERS), g], attp.at[sp, g], back_s.at[g, d], back_r.at[g, d], (grp, to))

    steps_s, settle_s, drain_s, here, neighbours = gather_plan(full_s, gs_s, gr_s, STEPS)
    steps_t, settle_t, drain_t, _, _ = gather_plan(full_t, gs_t, gr_t, LATER)
    loads = [
        pltpu.make_async_copy(hidden_ref, hid, load_sem.at[0]),
        pltpu.make_async_copy(cot_in_ref, cot, load_sem.at[1]),
        pltpu.make_async_copy(hidden_ref.at[:, pixels(sp), :], x_in.at[slot], load_sem.at[2]),
    ]
    loads[0].start()
    loads[1].start()

    @pl.when(busy)
    def _():
        loads[2].start()

    partners = neighbours + [(grp, from_me(d)) for d in range(1, 8)]
    barrier = pltpu.get_barrier_semaphore()
    for who in partners:
        pl.semaphore_signal(barrier, inc=1, device_id=who, device_id_type=MESH)
    full_s[here] = pack(w1_ref, w2_ref)
    pl.semaphore_wait(barrier, len(partners))
    steps_s[0]()
    steps_s[1]()
    full_t[here] = pack(w3_ref, w4_ref)
    steps_t[0]()

    @pl.when(busy)
    def _():
        for d in (3, 5, 1, 7):
            early(0, d).start()
        for i in range(batches):
            for d in (4, 2, 6):
                early(i, d).start()

    loads[0].wait()

    @pl.loop(0, SLOTS)
    def _(f):
        @pl.when(busy)
        def _():
            nrm[f] = modulated(hid[f].astype(F32), offsets, 0, 1)

        for i in range(SLOTS):
            @pl.when(f == i)
            def _(i=i):
                steps_s[2 + i]()
                if i in (4, 5):
                    steps_t[i - 3]()

        @pl.when((f == 5) & busy)
        def _():
            @pl.loop(1, batches)
            def _(i):
                for d in (3, 5, 1, 7):
                    early(i, d).start()

    for run in steps_s[10:14] + steps_t[3:5] + steps_s[14:18] + steps_t[5:6] + steps_s[18:] + steps_t[6:7]:
        run()
    unpack(full_s, settle_s, wq, wo_s)
    for run in steps_t[7:9]:
        run()

    @pl.loop(0, batches)
    def _(i):
        @pl.when(busy)
        def _():
            tokens = nrm[pl.ds(BATCH * i, BATCH)].reshape(BATCH * PIX, WIDTH)
            got = jnp.dot(tokens, wq[...], preferred_element_type=F32)
            qkv[...] = got.astype(BF).reshape(BATCH, PIX, 3 * PAD)
            for u in range(BATCH):
                att_s[BATCH * i + u] = attention(lambda first: qkv[u, :, first : first + 256], PIX, None)
            for d in (4, 3, 5, 2, 6, 1, 7):
                there(i, d).start()
            there_own(i).start()

        for n in range(batches):
            @pl.when(i == n)
            def _(n=n):
                for run in steps_t[(9, 12, 12, 15)[n] : (12, 12, 15, 15)[n]]:
                    run()

    loads[1].wait()

    @pl.when(busy)
    def _():
        loads[2].wait()

    @pl.loop(0, batches)
    def _(i):
        for n in range(batches):
            @pl.when(i == n)
            def _(n=n):
                for run in steps_t[(15, 18, 19, 19)[n] : (18, 19, 19, 19)[n]]:
                    run()

        @pl.when(busy)
        def _():
            for u in range(BATCH):
                f = BATCH * i + u
                kept = sp * SLOTS + f < total
                branch = jnp.dot(att_s[f], wo_s[...], preferred_element_type=F32)
                mid[f] = (hid[f].astype(F32) + gate_ref[0:1, :] * branch).astype(BF)
                nrm[f] = jnp.where(kept, gate_ref[1:2, :] * cot[f].astype(F32), 0.0).astype(BF)

        for d in range(1, 8):
            @if_sends(d)
            def _(d=d):
                early(i, d).wait_recv()
                there(i, d).wait_recv()

        @pl.when(busy)
        def _():
            there_own(i).wait()

        frames = pl.ds(BATCH * i, BATCH)
        lines = SENDERS * BATCH * OWN
        branch = jnp.dot(a_in[:, frames].reshape(lines, PAD), wo_s[...], preferred_element_type=F32)
        middle = x_in[:, frames].reshape(lines, WIDTH).astype(F32) + gate_ref[0:1, :] * branch
        normed = modulated(middle.astype(BF).astype(F32), offsets, 2, 3)
        x_in[:, frames] = normed.reshape(SENDERS, BATCH, OWN, WIDTH)

    order = shuffle(False)

    @pl.loop(0, SENDERS)
    def _(s):
        got = jnp.dot(order, x_in[s].reshape(128, WIDTH), preferred_element_type=F32).astype(BF)
        xp[:, s] = got.reshape(GROUPS, 16, WIDTH)

    unpack(full_t, settle_t, wq, wo_t)

    key, row = iota((rows, PIX), 1), iota((rows, PIX), 0)
    frame = (key // 16) * 8 + key % 8
    valid = (key < rows) & (frame < total) & ((key // 8) % 2 == (row // 8) % 2)

    @pl.loop(0, GROUPS // 2)
    def _(i):
        got = jnp.dot(xp[pl.ds(2 * i, 2)].reshape(2 * rows, WIDTH), wq[...], preferred_element_type=F32)
        qkv_t[...] = got.astype(BF).reshape(2, rows, 3 * PAD)
        for u in range(2):
            mixed = attention(lambda first: qkv_t[u, :, first : first + 256], rows, valid)
            ap[:, 2 * i + u] = mixed.reshape(SENDERS, 16, PAD)
            for d in (4, 3, 5, 2, 6, 1, 7):
                @if_gets(d)
                def _(d=d, u=u):
                    back(2 * i + u, d).start()

        @pl.when(busy)
        def _():
            attp[sp, pl.ds(2 * i, 2)] = ap[slot, pl.ds(2 * i, 2)]

    def swap(n):
        cols = pl.ds(384 * n, 384)
        return remote(g_part.at[:, 1 - c, :, cols], r0.at[:, :, cols], s0.at[n], t0.at[n], sibling)

    def step1(n, to_x):
        cols = pl.ds(384 * n, 384)
        return remote(
            red.at[to_x, :, cols], r1.at[slot, :, cols], s1.at[n, to_x], t1.at[n, slot], (grp, 2 * to_x + c))

    def step2(d):
        to = lax.rem(grp + d, 32)
        return remote(buf.at[to], r2.at[chip], s2.at[d], t2.at[d], (to, sp))

    @pl.when(busy)
    def _():
        @pl.loop(0, 8)
        def _(t):
            got = jnp.dot(order, nrm[:, pixels(t), :].reshape(128, WIDTH), preferred_element_type=F32)
            scp[t] = got.astype(BF).reshape(GROUPS, 16, WIDTH)

        acc[...] = jnp.zeros_like(acc)

        def product(i, cols):
            pairs = pl.ds(2 * i, 2)
            return lax.dot_general(
                attp[:, pairs].reshape(2 * PIX, PAD), scp[:, pairs, :, cols].reshape(2 * PIX, 384),
                (((0,), (0,)), ((), ())), preferred_element_type=F32)

        @pl.loop(0, GROUPS // 2 - 1)
        def _(i):
            for d in range(1, 8):
                back(2 * i, d).wait_recv()
                back(2 * i + 1, d).wait_recv()
            for n in range(3):
                cols = slice(384 * n, 384 * n + 384)
                acc[:, cols] += product(i, cols)

        for d in range(1, 8):
            back(GROUPS - 2, d).wait_recv()
            back(GROUPS - 1, d).wait_recv()

        def gradient(n):
            cols = slice(384 * n, 384 * n + 384)
            got = (acc[:, cols] + product(GROUPS // 2 - 1, cols)) * (1.0 / PIX)
            for t in range(8):
                part = jnp.concatenate([got[72 * t : 72 * t + 72], jnp.zeros((8, 384), F32)], axis=0)
                g_part[t // 2, t % 2, :, cols] = part.astype(BF)
            swap(n).start()

        def pass_on(n):
            cols = slice(384 * n, 384 * n + 384)
            swap(n).wait()
            for i in range(4):
                red[i, :, cols] = (g_part[i, c, :, cols].astype(F32) + r0[i, :, cols].astype(F32)).astype(BF)
            for i in range(4):
                @pl.when(2 * i + c != sp)
                def _(i=i):
                    step1(n, i).start()

                @pl.when(2 * i + c == sp)
                def _(i=i):
                    r1[slot, :, cols] = red[i, :, cols]

        gradient(0)
        gradient(1)
        pass_on(0)
        gradient(2)
        pass_on(1)
        pass_on(2)
        unorder = shuffle(True)

        @pl.loop(0, 8)
        def _(t):
            got = jnp.dot(unorder, attp[t].reshape(128, PAD), preferred_element_type=F32).astype(BF)
            att[:, pixels(t), :] = got.reshape(SLOTS, OWN, PAD)

        @pl.loop(0, SLOTS)
        def _(f):
            kept = sp * SLOTS + f < total
            branch = jnp.dot(att[f], wo_t[...], preferred_element_type=F32)
            out = mid[f].astype(F32) + gate_ref[1:2, :] * branch
            hid[f] = jnp.where(kept, out, 0.0).astype(BF)

    @pl.when(sp >= SENDERS)
    def _():
        hid[...] = jnp.zeros_like(hid)

    result = pltpu.make_async_copy(hid, out_ref, out_sem)
    result.start()

    @pl.when(low == c)
    def _():
        for n in range(3):
            for s in range(SENDERS):
                @pl.when(sp != s)
                def _(n=n, s=s):
                    cols = pl.ds(384 * n, 384)
                    remote(
                        red.at[0, :, cols], r1.at[s, :, cols], s1.at[n, 0], t1.at[n, s], sibling).wait_recv()

        whole = r1[0].astype(F32)
        for s in range(1, SENDERS):
            whole = whole + r1[s].astype(F32)
        whole = jnp.concatenate([whole, jnp.zeros((48, WIDTH), F32)], axis=0)
        for n in range(9):
            flipped[128 * n : 128 * n + 128] = whole[:, 128 * n : 128 * n + 128].T
        for g in range(32):
            part = jnp.concatenate([flipped[36 * g : 36 * g + 36], jnp.zeros((12, 128), F32)], axis=0)
            buf[g] = part.astype(BF)

        @pl.loop(1, 32)
        def _(d):
            step2(d).start()

        r2[chip] = buf[grp]

        @pl.loop(1, 32)
        def _(d):
            step2(d).wait_send()

    @pl.loop(1, 32)
    def _(d):
        @pl.when(lax.rem(grp + 32 - d, 2) == low)
        def _():
            step2(d).wait_recv()

    whole = r2[0].astype(F32)
    for i in range(1, 16):
        whole = whole + r2[i].astype(F32)
    grad_ref[...] = whole[:36, :HDIM]

    drain_s()
    drain_t()

    @pl.when(busy)
    def _():
        for n in range(3):
            for i in range(4):
                @pl.when(2 * i + c != sp)
                def _(n=n, i=i):
                    step1(n, i).wait_send()

        for d in range(1, 8):
            for i in range(batches):
                early(i, d).wait_send()
                there(i, d).wait_send()

    for g in range(GROUPS):
        for d in range(1, 8):
            @if_gets(d)
            def _(d=d, g=g):
                back(g, d).wait_send()

    result.wait()


def on_device(
    hidden,
    frame_counts,
    shifts,
    gates,
    w_qkv_spatial,
    w_out_spatial,
    w_qkv_temporal,
    w_out_temporal,
    cotangent,
):
    frames = (SLOTS, PIX, WIDTH)
    dma = pltpu.SemaphoreType.DMA
    block_out, grad = pl.pallas_call(
        block_kernel,
        out_shape=(jax.ShapeDtypeStruct(frames, BF), jax.ShapeDtypeStruct((36, HDIM), F32)),
        in_specs=[SM, VM, VM, ANY, ANY, VM, VM, VM, VM],
        out_specs=(ANY, VM),
        scratch_shapes=[
            pltpu.VMEM((4, 4, 2, 48, PACK), BF),
            pltpu.VMEM((4, 4, 2, 48, PACK), BF),
            pltpu.VMEM((WIDTH, 3 * PAD), BF),
            pltpu.VMEM((PAD, WIDTH), BF),
            pltpu.VMEM((PAD, WIDTH), BF),
            *[pltpu.VMEM(frames, BF)] * 4,
            pltpu.VMEM((BATCH, PIX, 3 * PAD), BF),
            pltpu.VMEM((SLOTS, PIX, PAD), BF),
            pltpu.VMEM((SENDERS, SLOTS, OWN, WIDTH), BF),
            pltpu.VMEM((SENDERS, SLOTS, OWN, PAD), BF),
            pltpu.VMEM((GROUPS, SENDERS, 16, WIDTH), BF),
            pltpu.VMEM((2, SENDERS * 16, 3 * PAD), BF),
            pltpu.VMEM((SENDERS, GROUPS, 16, PAD), BF),
            pltpu.VMEM((8, GROUPS, 16, PAD), BF),
            pltpu.VMEM((SLOTS, PIX, PAD), BF),
            pltpu.VMEM((8, GROUPS, 16, WIDTH), BF),
            pltpu.VMEM((PAD, WIDTH), F32),
            pltpu.VMEM((4, 2, 80, WIDTH), BF),
            pltpu.VMEM((4, 80, WIDTH), BF),
            pltpu.VMEM((4, 80, WIDTH), BF),
            pltpu.VMEM((SENDERS, 80, WIDTH), BF),
            pltpu.VMEM((WIDTH, 128), F32),
            pltpu.VMEM((32, 48, 128), BF),
            pltpu.VMEM((16, 48, 128), BF),
            dma((COPIES,)), dma((COPIES,)), dma((COPIES,)), dma((COPIES,)),
            dma((3,)), dma((4, 8)), dma((4, 8)),
            dma((4, 8)), dma((4, 8)), dma((4,)),
            dma((8, 8)), dma((8, 8)),
            dma((3,)), dma((3,)), dma((3, 4)), dma((3, SENDERS)), dma((32,)), dma((32,)), dma,
        ],
        compiler_params=pltpu.CompilerParams(
            vmem_limit_bytes=BIG, collective_id=1, has_side_effects=True),
        name="block",
    )(
        frame_counts, shifts[0], gates[0], hidden[0], cotangent[0],
        w_qkv_spatial, w_out_spatial, w_qkv_temporal, w_out_temporal,
    )
    return block_out[None], grad


def solution(mesh):
    return jax.shard_map(
        on_device,
        mesh=mesh,
        in_specs=(
            P("grp", "sp", None, None),
            P("grp"),
            P("grp", None, None),
            P("grp", None, None),
            P("grp", None),
            P("grp", None),
            P("grp", None),
            P("grp", None),
            P("grp", "sp", None, None),
        ),
        out_specs=(P("grp", "sp", None, None), P("grp", "sp")),
        check_vma=False,
    )
```

```python
import math

import jax
import jax.numpy as jnp
from jax import lax
from jax.experimental import pallas as pl
from jax.experimental.pallas import tpu as pltpu
from jax.sharding import PartitionSpec as P

MESH = pl.DeviceIdType.MESH
BF = jnp.bfloat16
F32 = jnp.float32
HDIM = 72
WIDTH = 1152
INNER = 576
PAD = 640
PIX = 128
SLOTS = 8
OWN = 16
SENDERS = 6
PACK = 1792
SCALE = math.log2(math.e) / math.sqrt(HDIM)
BATCH = 2
GROUPS = 8
ANY = pl.BlockSpec(memory_space=pl.ANY)
VM = pl.BlockSpec(memory_space=pltpu.VMEM)
SM = pl.BlockSpec(memory_space=pltpu.SMEM)
BIG = 56 * 1024 * 1024


def pack(qkv_ref, out_ref):
    qkv, out = qkv_ref[...].astype(F32), out_ref[...].astype(F32)
    k, v = qkv[:, INNER : 2 * INNER], qkv[:, 2 * INNER :]
    top = jnp.concatenate([qkv[:, :INNER], k[:, 512:], k[:, :512], v, jnp.zeros((36, 64), F32)], axis=1)
    blank = jnp.zeros((6, 64), F32)
    side = jnp.concatenate([
        jnp.concatenate([out[12:, :INNER], blank], axis=1),
        jnp.concatenate([blank, out[12:, INNER:]], axis=1),
    ], axis=0)
    low = jnp.concatenate([out[:12], side], axis=1)
    return jnp.concatenate([top, low], axis=0).astype(BF)


STEPS = (
    ((), ("z1p", "z1q")),
    ((), ("upp0", "dnp0", "upq0", "dnq0")),
    (("z1p",), ("z2p", "upp1", "dnp1")),
    (("z1q",), ("z2q", "upq1", "dnq1")),
    (("upp0", "dnp0"), ("farp0",)),
    (("upq0", "dnq0"), ("farq0",)),
    (("z2p",), ("z3p", "upp2", "dnp2")),
    (("z2q",), ("z3q", "upq2", "dnq2")),
    (("upp1", "dnp1"), ("farp1",)),
    (("upq1", "dnq1"), ("farq1",)),
    (("z3p",), ("upp3", "dnp3")),
    (("z3q",), ("upq3", "dnq3")),
    (("farp0", "farq0"), ("s0",)),
    (("upp2", "dnp2"), ("farp2",)),
    (("upq2", "dnq2"), ("farq2",)),
    (("farp1", "farq1"), ("s1",)),
    (("upp3", "dnp3"), ("farp3",)),
    (("upq3", "dnq3"), ("farq3",)),
    (("farp2", "farq2"), ("s2",)),
    (("farp3", "farq3"), ("s3",)),
)
LATER = (
    ((), ("z1p", "z1q")),
    (("z1p",), ("z2p",)),
    (("z1q",), ("z2q",)),
    (("z2p",), ("z3p",)),
    (("z2q",), ("z3q",)),
    ((), ("upp0", "dnp0", "upq0", "dnq0", "upp1", "dnp1", "upq1", "dnq1", "upp2", "dnp2", "upq2", "dnq2")),
    (("z3p", "z3q"), ("upp3", "dnp3", "upq3", "dnq3")),
    (("upp0", "dnp0"), ("farp0",)),
    (("upq0", "dnq0"), ("farq0",)),
    (("upp1", "dnp1"), ("farp1",)),
    (("upq1", "dnq1"), ("farq1",)),
    (("upp2", "dnp2"), ("farp2",)),
    (("upq2", "dnq2"), ("farq2",)),
    (("upp3", "dnp3"), ("farp3",)),
    (("upq3", "dnq3"), ("farq3",)),
    (("farp0", "farq0"), ("s0",)),
    (("farp1", "farq1"), ("s1",)),
    (("farp2", "farq2"), ("s2",)),
    (("farp3", "farq3"), ("s3",)),
)


def gather_plan(full, ssem, rsem, order):
    grp, sp = lax.axis_index("grp"), lax.axis_index("sp")
    h, y, c = grp // 8, (grp // 2) % 4, grp % 2
    low = sp % 2
    up, down = lax.rem(y + 1, 4), lax.rem(y + 3, 4)
    hx = lax.rem(h + 3 + 2 * low, 4)
    hp = lax.rem(h + 5 - 2 * low, 4)
    hf = lax.rem(h + 2, 4)
    sibling = (grp + 1 - 2 * c, sp)
    y_up = ((h * 4 + up) * 2 + c, sp)
    y_down = ((h * 4 + down) * 2 + c, sp)
    pair = (grp, sp + 1 - 2 * low)
    cross = (hx * 8 + y * 2 + c, sp + 1 - 2 * low)
    al = slice(None)
    hs = (h, hx, hp, hf)
    table = {}

    def add(name, where, who):
        table[name] = (len(table), where, who)

    for stream, cols in (("p", pl.ds(0, PACK // 2)), ("q", pl.ds(PACK // 2, PACK // 2))):
        add("z1" + stream, (h, y, c, al, cols), cross)
        add("z2" + stream, (hx, y, c, al, cols), pair)
        add("z3" + stream, (hp, y, c, al, cols), cross)
        for k in range(4):
            add(f"up{stream}{k}", (hs[k], y, c, al, cols), y_up)
            add(f"dn{stream}{k}", (hs[k], y, c, al, cols), y_down)
            if stream == "p":
                add(f"farp{k}", (hs[k], down, c, al, cols), y_up)
            else:
                add(f"farq{k}", (hs[k], up, c, al, cols), y_down)
    for k in range(4):
        add(f"s{k}", (hs[k], al, c), sibling)

    def copy(name):
        i, where, who = table[name]
        return pltpu.make_async_remote_copy(
            src_ref=full.at[where], dst_ref=full.at[where], send_sem=ssem.at[i], recv_sem=rsem.at[i],
            device_id=who, device_id_type=MESH)

    def step(waits, starts):
        def run():
            for name in waits:
                copy(name).wait_recv()
            for name in starts:
                copy(name).start()
        return run

    def settle(k):
        copy(f"s{k}").wait_recv()
        return hs[k]

    def drain():
        for name in table:
            copy(name).wait_send()

    return [step(*both) for both in order], settle, drain, (h, y, c), [sibling, y_up, y_down, cross]


COPIES = 34


def iota(shape, dim):
    return lax.broadcasted_iota(jnp.int32, shape, dim)


def picks(condition):
    return condition.astype(F32).astype(BF)


def unpack(full, settle, wq, wo):
    col, row = iota((144, 192), 1), iota((144, 192), 0)
    of, at = col // 48, col % 48
    top = picks((at < 36) & (36 * of + at == row))
    col, row = iota((72, 192), 1), iota((72, 192), 0)
    of, at = col // 48, col % 48 - 36
    main = picks((at >= 0) & (18 * of + at == row) & (at < 12))
    left = picks((at >= 0) & (at < 6) & (18 * of + 12 + at == row))
    right = picks((at >= 6) & (18 * of + 6 + at == row))
    keep = iota((144, 128), 1) < 64

    wo[INNER:, :] = jnp.zeros((PAD - INNER, WIDTH), BF)
    for k in range(4):
        h = settle(k)
        outs = []
        for i in range(2):
            block = full[h, 2 * i : 2 * i + 2].reshape(192, PACK)
            got = jnp.dot(top, block, preferred_element_type=F32)
            rows = pl.ds(pl.multiple_of((2 * h + i) * 144, 16), 144)
            mixed = got[:, 512:640]
            turned = jnp.concatenate([mixed[:, 64:], mixed[:, :64]], axis=1)
            wq[rows, 0:512] = got[:, 0:512].astype(BF)
            wq[rows, 512:640] = jnp.where(keep, mixed, 0.0).astype(BF)
            wq[rows, 640:1152] = got[:, 640:1152].astype(BF)
            wq[rows, 1152:1280] = jnp.where(keep, turned, 0.0).astype(BF)
            wq[rows, 1280:1920] = got[:, 1152:1792].astype(BF)
            whole = jnp.dot(main, block[:, :WIDTH], preferred_element_type=F32)
            side = block[:, WIDTH:]
            one = jnp.dot(left, side, preferred_element_type=F32)
            two = jnp.dot(right, side, preferred_element_type=F32)
            blank = jnp.zeros((72, 512), F32)
            outs.append(whole + jnp.concatenate([one, blank], axis=1) + jnp.concatenate([blank, two], axis=1))
        wo[pl.ds(pl.multiple_of(144 * h, 16), 144), :] = jnp.concatenate(outs, axis=0).astype(BF)


def modulated(x, offsets, shift_row, scale_row):
    mean = jnp.sum(x, axis=-1, keepdims=True) * (1.0 / WIDTH)
    x = x - mean
    spread = jnp.sum(x * x, axis=-1, keepdims=True) * (1.0 / WIDTH)
    x = x * lax.rsqrt(spread + 1e-06)
    return (x * (1.0 + offsets[scale_row]) + offsets[shift_row]).astype(BF)


def head_masks(j):
    lane = iota((1, 256), 1)
    start = 16 * j
    one = picks((lane >= start) & (lane < start + HDIM))
    two = picks((lane >= start + HDIM) & (lane < start + 2 * HDIM))
    return one, two


def attention(load, keys, valid):
    blocks = [None] * 5
    fill = [] if keys == PIX else [jnp.zeros((PIX - keys, 256), BF)]
    for j in range(4):
        one, two = head_masks(j)
        q, k, v = (load(part * PAD + 128 * j) for part in range(3))
        kk = jnp.concatenate([k * one, *fill, k * two, *fill], axis=0)
        vv = jnp.concatenate([v * one, *fill, v * two, *fill], axis=0)
        heads = jnp.concatenate(
            [jnp.broadcast_to(one, (PIX, 256)), jnp.broadcast_to(two, (PIX, 256))], axis=0)
        s = lax.dot_general(q, kk, (((1,), (1,)), ((), ())), preferred_element_type=F32)
        expo = []
        for part in (s[:, :128], s[:, 128:]):
            if valid is not None:
                part = jnp.where(valid, part, -1e30)
            top = jnp.max(part, axis=-1, keepdims=True)
            expo.append(jnp.exp2((part - top) * SCALE).astype(BF))
        expo = jnp.concatenate(expo, axis=1)
        o = jnp.dot(expo, vv, preferred_element_type=F32)
        total = jnp.dot(expo, heads, preferred_element_type=F32)
        o = o * (1.0 / jnp.where(total == 0.0, 1.0, total))
        for i, piece in ((j, o[:, :128]), (j + 1, o[:, 128:])):
            blocks[i] = piece if blocks[i] is None else blocks[i] + piece
    return jnp.concatenate(blocks, axis=1).astype(BF)


def shuffle(back):
    there, here = iota((128, 128), 1 if back else 0), iota((128, 128), 0 if back else 1)
    return picks(here == (there % 8) * OWN + there // 8)


def block_kernel(
    total_ref, shift_ref, gate_ref, hidden_ref, cot_in_ref, w1_ref, w2_ref, w3_ref, w4_ref,
    out_ref, grad_ref,
    full_s, full_t, wq, wo_s, wo_t, hid, nrm, mid, cot, qkv, att_s, x_in, a_in, xp, qkv_t, ap, attp, att,
    scp, acc, g_part, r0, red, r1, flipped, buf, r2,
    gs_s, gr_s, gs_t, gr_t, load_sem, early_s, early_r, there_s, there_r, there_l, back_s, back_r,
    s0, t0, s1, t1, s2, t2, out_sem,
):
    grp, sp = lax.axis_index("grp"), lax.axis_index("sp")
    c, low, chip = grp % 2, sp % 2, grp // 2
    sibling = (grp + 1 - 2 * c, sp)
    slot = lax.rem(sp, SENDERS)
    busy = sp < SENDERS
    offsets = [shift_ref[i : i + 1, :] for i in range(4)]
    total = total_ref[0]
    rows = SENDERS * 16
    batches = SLOTS // BATCH

    def from_me(d):
        return lax.rem(sp + d, 8)

    def pixels(rank):
        return pl.ds(pl.multiple_of(rank * OWN, OWN), OWN)

    def if_sends(d):
        return pl.when(lax.rem(sp + 8 - d, 8) < SENDERS)

    def if_gets(d):
        return pl.when(from_me(d) < SENDERS)

    def remote(src, dst, send_sem, recv_sem, who):
        return pltpu.make_async_remote_copy(
            src_ref=src, dst_ref=dst, send_sem=send_sem, recv_sem=recv_sem,
            device_id=who, device_id_type=MESH)

    def early(i, d):
        to, frames = from_me(d), pl.ds(BATCH * i, BATCH)
        return remote(
            hidden_ref.at[frames, pixels(to), :], x_in.at[slot, frames], early_s.at[i, d], early_r.at[i, d], (grp, to))

    def there(i, d):
        to, frames = from_me(d), pl.ds(BATCH * i, BATCH)
        return remote(
            att_s.at[frames, pixels(to), :], a_in.at[slot, frames], there_s.at[i, d], there_r.at[i, d], (grp, to))

    def there_own(i):
        frames = pl.ds(BATCH * i, BATCH)
        return pltpu.make_async_copy(att_s.at[frames, pixels(sp), :], a_in.at[slot, frames], there_l.at[i])

    def back(g, d):
        to = from_me(d)
        return remote(
            ap.at[lax.rem(to, SENDERS), g], attp.at[sp, g], back_s.at[g, d], back_r.at[g, d], (grp, to))

    steps_s, settle_s, drain_s, here, neighbours = gather_plan(full_s, gs_s, gr_s, STEPS)
    steps_t, settle_t, drain_t, _, _ = gather_plan(full_t, gs_t, gr_t, LATER)
    loads = [
        pltpu.make_async_copy(hidden_ref, hid, load_sem.at[0]),
        pltpu.make_async_copy(cot_in_ref, cot, load_sem.at[1]),
        pltpu.make_async_copy(hidden_ref.at[:, pixels(sp), :], x_in.at[slot], load_sem.at[2]),
    ]
    loads[0].start()
    loads[1].start()

    @pl.when(busy)
    def _():
        loads[2].start()

    partners = neighbours + [(grp, from_me(d)) for d in range(1, 8)]
    barrier = pltpu.get_barrier_semaphore()
    for who in partners:
        pl.semaphore_signal(barrier, inc=1, device_id=who, device_id_type=MESH)
    full_s[here] = pack(w1_ref, w2_ref)
    pl.semaphore_wait(barrier, len(partners))
    steps_s[0]()
    steps_s[1]()
    full_t[here] = pack(w3_ref, w4_ref)
    steps_t[0]()

    @pl.when(busy)
    def _():
        for d in (3, 5, 1, 7):
            early(0, d).start()
        for i in range(batches):
            for d in (4, 2, 6):
                early(i, d).start()

    loads[0].wait()

    @pl.loop(0, SLOTS)
    def _(f):
        @pl.when(busy)
        def _():
            nrm[f] = modulated(hid[f].astype(F32), offsets, 0, 1)

        for i in range(SLOTS):
            @pl.when(f == i)
            def _(i=i):
                steps_s[2 + i]()
                if i in (4, 5):
                    steps_t[i - 3]()

        @pl.when((f == 5) & busy)
        def _():
            @pl.loop(1, batches)
            def _(i):
                for d in (3, 5, 1, 7):
                    early(i, d).start()

    for run in steps_s[10:14] + steps_t[3:5] + steps_s[14:18] + steps_t[5:6] + steps_s[18:] + steps_t[6:7]:
        run()
    unpack(full_s, settle_s, wq, wo_s)
    for run in steps_t[7:9]:
        run()

    @pl.loop(0, batches)
    def _(i):
        @pl.when(busy)
        def _():
            tokens = nrm[pl.ds(BATCH * i, BATCH)].reshape(BATCH * PIX, WIDTH)
            got = jnp.dot(tokens, wq[...], preferred_element_type=F32)
            qkv[...] = got.astype(BF).reshape(BATCH, PIX, 3 * PAD)
            for u in range(BATCH):
                att_s[BATCH * i + u] = attention(lambda first: qkv[u, :, first : first + 256], PIX, None)
            for d in (4, 3, 5, 2, 6, 1, 7):
                there(i, d).start()
            there_own(i).start()

        for n in range(batches):
            @pl.when(i == n)
            def _(n=n):
                for run in steps_t[(9, 11, 13, 13)[n] : (11, 13, 13, 13)[n]]:
                    run()

    loads[1].wait()

    @pl.when(busy)
    def _():
        loads[2].wait()

    @pl.loop(0, batches)
    def _(i):
        for n in range(batches):
            @pl.when(i == n)
            def _(n=n):
                for run in steps_t[(13, 15, 17, 18)[n] : (15, 17, 18, 19)[n]]:
                    run()

        @pl.when(busy)
        def _():
            for u in range(BATCH):
                f = BATCH * i + u
                kept = sp * SLOTS + f < total
                branch = jnp.dot(att_s[f], wo_s[...], preferred_element_type=F32)
                mid[f] = (hid[f].astype(F32) + gate_ref[0:1, :] * branch).astype(BF)
                nrm[f] = jnp.where(kept, gate_ref[1:2, :] * cot[f].astype(F32), 0.0).astype(BF)

        for d in range(1, 8):
            @if_sends(d)
            def _(d=d):
                early(i, d).wait_recv()
                there(i, d).wait_recv()

        @pl.when(busy)
        def _():
            there_own(i).wait()

        frames = pl.ds(BATCH * i, BATCH)
        lines = SENDERS * BATCH * OWN
        branch = jnp.dot(a_in[:, frames].reshape(lines, PAD), wo_s[...], preferred_element_type=F32)
        middle = x_in[:, frames].reshape(lines, WIDTH).astype(F32) + gate_ref[0:1, :] * branch
        normed = modulated(middle.astype(BF).astype(F32), offsets, 2, 3)
        x_in[:, frames] = normed.reshape(SENDERS, BATCH, OWN, WIDTH)

    order = shuffle(False)

    @pl.loop(0, SENDERS)
    def _(s):
        got = jnp.dot(order, x_in[s].reshape(128, WIDTH), preferred_element_type=F32).astype(BF)
        xp[:, s] = got.reshape(GROUPS, 16, WIDTH)

    unpack(full_t, settle_t, wq, wo_t)

    key, row = iota((rows, PIX), 1), iota((rows, PIX), 0)
    frame = (key // 16) * 8 + key % 8
    valid = (key < rows) & (frame < total) & ((key // 8) % 2 == (row // 8) % 2)

    @pl.loop(0, GROUPS // 2)
    def _(i):
        got = jnp.dot(xp[pl.ds(2 * i, 2)].reshape(2 * rows, WIDTH), wq[...], preferred_element_type=F32)
        qkv_t[...] = got.astype(BF).reshape(2, rows, 3 * PAD)
        for u in range(2):
            mixed = attention(lambda first: qkv_t[u, :, first : first + 256], rows, valid)
            ap[:, 2 * i + u] = mixed.reshape(SENDERS, 16, PAD)
            for d in (4, 3, 5, 2, 6, 1, 7):
                @if_gets(d)
                def _(d=d, u=u):
                    back(2 * i + u, d).start()

        @pl.when(busy)
        def _():
            attp[sp, pl.ds(2 * i, 2)] = ap[slot, pl.ds(2 * i, 2)]

    def swap(n):
        cols = pl.ds(384 * n, 384)
        return remote(g_part.at[:, 1 - c, :, cols], r0.at[:, :, cols], s0.at[n], t0.at[n], sibling)

    def step1(n, to_x):
        cols = pl.ds(384 * n, 384)
        return remote(
            red.at[to_x, :, cols], r1.at[slot, :, cols], s1.at[n, to_x], t1.at[n, slot], (grp, 2 * to_x + c))

    def step2(d):
        to = lax.rem(grp + d, 32)
        return remote(buf.at[to], r2.at[chip], s2.at[d], t2.at[d], (to, sp))

    @pl.when(busy)
    def _():
        @pl.loop(0, 8)
        def _(t):
            got = jnp.dot(order, nrm[:, pixels(t), :].reshape(128, WIDTH), preferred_element_type=F32)
            scp[t] = got.astype(BF).reshape(GROUPS, 16, WIDTH)

        acc[...] = jnp.zeros_like(acc)

        def product(i, cols):
            pairs = pl.ds(2 * i, 2)
            return lax.dot_general(
                attp[:, pairs].reshape(2 * PIX, PAD), scp[:, pairs, :, cols].reshape(2 * PIX, 384),
                (((0,), (0,)), ((), ())), preferred_element_type=F32)

        @pl.loop(0, GROUPS // 2 - 1)
        def _(i):
            for d in range(1, 8):
                back(2 * i, d).wait_recv()
                back(2 * i + 1, d).wait_recv()
            for n in range(3):
                cols = slice(384 * n, 384 * n + 384)
                acc[:, cols] += product(i, cols)

        for d in range(1, 8):
            back(GROUPS - 2, d).wait_recv()
            back(GROUPS - 1, d).wait_recv()

        def gradient(n):
            cols = slice(384 * n, 384 * n + 384)
            got = (acc[:, cols] + product(GROUPS // 2 - 1, cols)) * (1.0 / PIX)
            for t in range(8):
                part = jnp.concatenate([got[72 * t : 72 * t + 72], jnp.zeros((8, 384), F32)], axis=0)
                g_part[t // 2, t % 2, :, cols] = part.astype(BF)
            swap(n).start()

        def pass_on(n):
            cols = slice(384 * n, 384 * n + 384)
            swap(n).wait()
            for i in range(4):
                red[i, :, cols] = (g_part[i, c, :, cols].astype(F32) + r0[i, :, cols].astype(F32)).astype(BF)
            for i in range(4):
                @pl.when(2 * i + c != sp)
                def _(i=i):
                    step1(n, i).start()

                @pl.when(2 * i + c == sp)
                def _(i=i):
                    r1[slot, :, cols] = red[i, :, cols]

        gradient(0)
        gradient(1)
        pass_on(0)
        gradient(2)
        pass_on(1)
        pass_on(2)
        unorder = shuffle(True)

        @pl.loop(0, 8)
        def _(t):
            got = jnp.dot(unorder, attp[t].reshape(128, PAD), preferred_element_type=F32).astype(BF)
            att[:, pixels(t), :] = got.reshape(SLOTS, OWN, PAD)

        @pl.loop(0, SLOTS)
        def _(f):
            kept = sp * SLOTS + f < total
            branch = jnp.dot(att[f], wo_t[...], preferred_element_type=F32)
            out = mid[f].astype(F32) + gate_ref[1:2, :] * branch
            hid[f] = jnp.where(kept, out, 0.0).astype(BF)

    @pl.when(sp >= SENDERS)
    def _():
        hid[...] = jnp.zeros_like(hid)

    result = pltpu.make_async_copy(hid, out_ref, out_sem)
    result.start()

    @pl.when(low == c)
    def _():
        for n in range(3):
            for s in range(SENDERS):
                @pl.when(sp != s)
                def _(n=n, s=s):
                    cols = pl.ds(384 * n, 384)
                    remote(
                        red.at[0, :, cols], r1.at[s, :, cols], s1.at[n, 0], t1.at[n, s], sibling).wait_recv()

        whole = r1[0].astype(F32)
        for s in range(1, SENDERS):
            whole = whole + r1[s].astype(F32)
        whole = jnp.concatenate([whole, jnp.zeros((48, WIDTH), F32)], axis=0)
        for n in range(9):
            flipped[128 * n : 128 * n + 128] = whole[:, 128 * n : 128 * n + 128].T
        for g in range(32):
            part = jnp.concatenate([flipped[36 * g : 36 * g + 36], jnp.zeros((12, 128), F32)], axis=0)
            buf[g] = part.astype(BF)

        @pl.loop(1, 32)
        def _(d):
            step2(d).start()

        r2[chip] = buf[grp]

        @pl.loop(1, 32)
        def _(d):
            step2(d).wait_send()

    @pl.loop(1, 32)
    def _(d):
        @pl.when(lax.rem(grp + 32 - d, 2) == low)
        def _():
            step2(d).wait_recv()

    whole = r2[0].astype(F32)
    for i in range(1, 16):
        whole = whole + r2[i].astype(F32)
    grad_ref[...] = whole[:36, :HDIM]

    drain_s()
    drain_t()

    @pl.when(busy)
    def _():
        for n in range(3):
            for i in range(4):
                @pl.when(2 * i + c != sp)
                def _(n=n, i=i):
                    step1(n, i).wait_send()

        for d in range(1, 8):
            for i in range(batches):
                early(i, d).wait_send()
                there(i, d).wait_send()

    for g in range(GROUPS):
        for d in range(1, 8):
            @if_gets(d)
            def _(d=d, g=g):
                back(g, d).wait_send()

    result.wait()


def on_device(
    hidden,
    frame_counts,
    shifts,
    gates,
    w_qkv_spatial,
    w_out_spatial,
    w_qkv_temporal,
    w_out_temporal,
    cotangent,
):
    frames = (SLOTS, PIX, WIDTH)
    dma = pltpu.SemaphoreType.DMA
    block_out, grad = pl.pallas_call(
        block_kernel,
        out_shape=(jax.ShapeDtypeStruct(frames, BF), jax.ShapeDtypeStruct((36, HDIM), F32)),
        in_specs=[SM, VM, VM, ANY, ANY, VM, VM, VM, VM],
        out_specs=(ANY, VM),
        scratch_shapes=[
            pltpu.VMEM((4, 4, 2, 48, PACK), BF),
            pltpu.VMEM((4, 4, 2, 48, PACK), BF),
            pltpu.VMEM((WIDTH, 3 * PAD), BF),
            pltpu.VMEM((PAD, WIDTH), BF),
            pltpu.VMEM((PAD, WIDTH), BF),
            *[pltpu.VMEM(frames, BF)] * 4,
            pltpu.VMEM((BATCH, PIX, 3 * PAD), BF),
            pltpu.VMEM((SLOTS, PIX, PAD), BF),
            pltpu.VMEM((SENDERS, SLOTS, OWN, WIDTH), BF),
            pltpu.VMEM((SENDERS, SLOTS, OWN, PAD), BF),
            pltpu.VMEM((GROUPS, SENDERS, 16, WIDTH), BF),
            pltpu.VMEM((2, SENDERS * 16, 3 * PAD), BF),
            pltpu.VMEM((SENDERS, GROUPS, 16, PAD), BF),
            pltpu.VMEM((8, GROUPS, 16, PAD), BF),
            pltpu.VMEM((SLOTS, PIX, PAD), BF),
            pltpu.VMEM((8, GROUPS, 16, WIDTH), BF),
            pltpu.VMEM((PAD, WIDTH), F32),
            pltpu.VMEM((4, 2, 80, WIDTH), BF),
            pltpu.VMEM((4, 80, WIDTH), BF),
            pltpu.VMEM((4, 80, WIDTH), BF),
            pltpu.VMEM((SENDERS, 80, WIDTH), BF),
            pltpu.VMEM((WIDTH, 128), F32),
            pltpu.VMEM((32, 48, 128), BF),
            pltpu.VMEM((16, 48, 128), BF),
            dma((COPIES,)), dma((COPIES,)), dma((COPIES,)), dma((COPIES,)),
            dma((3,)), dma((4, 8)), dma((4, 8)),
            dma((4, 8)), dma((4, 8)), dma((4,)),
            dma((8, 8)), dma((8, 8)),
            dma((3,)), dma((3,)), dma((3, 4)), dma((3, SENDERS)), dma((32,)), dma((32,)), dma,
        ],
        compiler_params=pltpu.CompilerParams(
            vmem_limit_bytes=BIG, collective_id=1, has_side_effects=True),
        name="block",
    )(
        frame_counts, shifts[0], gates[0], hidden[0], cotangent[0],
        w_qkv_spatial, w_out_spatial, w_qkv_temporal, w_out_temporal,
    )
    return block_out[None], grad


def solution(mesh):
    return jax.shard_map(
        on_device,
        mesh=mesh,
        in_specs=(
            P("grp", "sp", None, None),
            P("grp"),
            P("grp", None, None),
            P("grp", None, None),
            P("grp", None),
            P("grp", None),
            P("grp", None),
            P("grp", None),
            P("grp", "sp", None, None),
        ),
        out_specs=(P("grp", "sp", None, None), P("grp", "sp")),
        check_vma=False,
    )
```
